512 devices in a mesh: tile: 64 (over y_lo, z, core), kern: 8 (over x, y_hi).
Axes of the slice: x: 4, y: 8 (y_hi: 2, y_lo: 4; y = y_hi * 4 + y_lo), z: 8, core: 2. Of those that a mesh axis runs over, the one named last changes fastest.
Arguments:
- mask_tile: float32 [64, 256, 256], P('tile'), may hold values from 0 to 1
- kernels: float32 [2, 24, 128, 128], P(None, 'kern'), may hold values from -0.03125 to 0.03125
- socs_weight: float32 [24], P('kern'), may hold values from 0.1 to 1
- adjacency: int32 [64, 2], P('tile'), may hold values from 0 to 1, as said below
- target: int32 [64, 256, 256], P('tile'), may hold values 0 or 1
Outputs:
- resist: float32 [64, 256, 256], P('tile')
- mask_grad: float32 [64, 256, 256], P('tile')
The draws below stay inside these ranges and needn't reach their ends.
Inputs may be any that keep to these rules, and one draw needn't show every extreme that they name: `adjacency`: every tile in an even column of the grid, or in column 3, is joined to its right neighbour, and every tile in an even row to its lower neighbour; other links are drawn.
All inputs are finite; a program needn't handle non-finite values. No bound on the sum of `target` on one device may be relied on, other than what follows from the above.
Results may differ from the reference program's by a relative error of at most 0.00027.
Values sent between devices are 32-bit elements; how exact they have to be, the bound alone decides.
A program may use at most 64 MiB of HBM per device.

```python
import math
import jax
import jax.numpy as jnp
from jax import lax

CORE = 256
KSIZE = 128
GRID_W = 8
HALO = 64
EXTENT = 384
KERNELS = 24
TILES = 64


def draw_adjacency(key, part):
    key = jax.random.fold_in(key, 5)
    drawn = jax.random.randint(key, (TILES, 2), 0, 4)
    linked = (drawn > 0).astype(jnp.int32)
    place = jnp.arange(TILES, dtype=jnp.int32)
    column = (place + GRID_W // 2) % GRID_W
    grid_row = (place + GRID_W // 2) // GRID_W
    forced_right = ((column % 2 == 0) | (column == GRID_W // 2 - 1)).astype(jnp.int32)
    even_row = (grid_row % 2 == 0).astype(jnp.int32)
    right_col = jnp.maximum(linked[:, 0], forced_right)
    down_col = jnp.maximum(linked[:, 1], even_row)
    return jnp.stack([right_col, down_col], axis=1).astype(jnp.int32)


def place_ends(result, rng, smallest, largest):
    dims = result.shape
    index_at = [jax.random.randint(jax.random.fold_in(rng, axis), (), 0, dims[axis]) for axis in range(len(dims))]
    result = result.at[tuple(index_at)].set(smallest)
    longest = dims.index(max(dims))
    index_at[longest] = (index_at[longest] + 1) % dims[longest]
    return result.at[tuple(index_at)].set(largest)


def levels(stream_key, extent, cuts, low, largest):
    loudness, own = 1.0, jax.random.fold_in(stream_key, 6)
    for position, shards_of in cuts:
        heights = jnp.exp(jax.random.uniform(jax.random.fold_in(own, position), (shards_of,), jnp.float32, low / len(cuts), largest / len(cuts)))
        loudness = loudness * jnp.repeat(heights, extent[position] // shards_of).reshape([-1 if axis == position else 1 for axis in range(len(extent))])
    return loudness


def scatter_about(key, shape, scale, bound, cuts=(), held_as=jnp.bfloat16):
    factor_of = levels(key, shape, cuts, -0.22, 0.18) if cuts else 1.0
    entries = jax.random.normal(key, shape, jnp.float32) * scale * factor_of
    return jnp.minimum(jnp.maximum(entries, -bound), bound).astype(held_as)


def setup_inputs(seed: int = 0) -> dict:
    splits = jax.random.split(jax.random.key(seed), 6)
    return {
        "mask_tile": jnp.clip(1.0 * jax.random.uniform(splits[0], (TILES, CORE, CORE), jnp.float32) ** levels(splits[0], (TILES, CORE, CORE), ((0, 64),), -0.2, 0.2), 0.0, 1.0),
        "kernels": scatter_about(splits[1], (2, KERNELS, KSIZE, KSIZE), (2 * KSIZE * KSIZE) ** -0.5, 0.03125, ((1, 8),), jnp.float32),
        "socs_weight": jnp.clip(jnp.exp(math.log(1.0) - 2.3025851 * jax.random.uniform(splits[2], (KERNELS,), jnp.float32) ** levels(splits[2], (KERNELS,), ((0, 8),), -0.2, 0.2)), 0.1, 1.0),
        "adjacency": draw_adjacency(jax.random.fold_in(splits[5], 71), 0),
        "target": place_ends((jax.random.randint(splits[4], (TILES, CORE, CORE), 0, 2) < 1).astype(jnp.int32), jax.random.fold_in(splits[4], 1), 0, 1),
    }


STEEP = 20.0
THRESH = 0.33

def links_of(adjacency):
    place = jnp.arange(TILES)
    column = (place + GRID_W // 2) % GRID_W
    right_ok = (column < GRID_W - 1) & (place + 1 < TILES)
    down_ok = place + GRID_W < TILES
    right_link = adjacency[:, 0].astype(jnp.float32) * right_ok.astype(jnp.float32)
    down_link = adjacency[:, 1].astype(jnp.float32) * down_ok.astype(jnp.float32)
    return (right_link[:, None, None], down_link[:, None, None])

def extend(mask_tile, right_link, down_link):
    left_link = jnp.roll(right_link, 1, axis=0)
    up_link = jnp.roll(down_link, GRID_W, axis=0)
    from_left = jnp.roll(mask_tile[:, :, CORE - HALO:], 1, axis=0) * left_link
    from_right = jnp.roll(mask_tile[:, :, :HALO], -1, axis=0) * right_link
    widened = jnp.concatenate([from_left, mask_tile, from_right], axis=2)
    from_above = jnp.roll(widened[:, CORE - HALO:], GRID_W, axis=0) * up_link
    from_below = jnp.roll(widened[:, :HALO], -GRID_W, axis=0) * down_link
    return jnp.concatenate([from_above, widened, from_below], axis=1)

def fold(ext_grad, right_link, down_link):
    left_link = jnp.roll(right_link, 1, axis=0)
    up_link = jnp.roll(down_link, GRID_W, axis=0)
    widened = ext_grad[:, HALO:HALO + CORE]
    widened = widened.at[:, :HALO].add(jnp.roll(ext_grad[:, EXTENT - HALO:], GRID_W, axis=0) * up_link)
    widened = widened.at[:, CORE - HALO:].add(jnp.roll(ext_grad[:, :HALO], -GRID_W, axis=0) * down_link)
    core_grad = widened[:, :, HALO:HALO + CORE]
    core_grad = core_grad.at[:, :, :HALO].add(jnp.roll(widened[:, :, EXTENT - HALO:], 1, axis=0) * left_link)
    core_grad = core_grad.at[:, :, CORE - HALO:].add(jnp.roll(widened[:, :, :HALO], -1, axis=0) * right_link)
    return core_grad

def resist_step(intensity, target_bits):
    resist = jax.nn.sigmoid(STEEP * (intensity - THRESH))
    slope_map = 2.0 * STEEP * (resist - target_bits.astype(jnp.float32)) * resist * (1.0 - resist)
    return (resist, slope_map)

def reference(mask_tile, kernels, socs_weight, adjacency, target):
    right_link, down_link = links_of(adjacency)
    extended = extend(mask_tile, right_link, down_link)
    spectrum = jnp.fft.fft2(extended)
    padded = jnp.zeros((2, KERNELS, EXTENT, EXTENT), kernels.dtype)
    padded = padded.at[:, :, :KSIZE, :KSIZE].set(kernels)
    response = jnp.fft.ifft2(padded[0] + 1j * padded[1]) * (EXTENT * EXTENT)
    tap_sums = lax.optimization_barrier(jnp.sum(kernels, axis=(2, 3)))
    clear_sum = jnp.sum(socs_weight * (tap_sums[0] * tap_sums[0] + tap_sums[1] * tap_sums[1]))

    def field_of(resp_one):
        return jnp.fft.ifft2(spectrum * resp_one[None])[:, :CORE, :CORE]

    def add_power(power_sum, kernel_pair):
        resp_one, weight_one = kernel_pair
        optical_field = field_of(resp_one)
        squares = optical_field.real * optical_field.real + optical_field.imag * optical_field.imag
        return (power_sum + weight_one * squares, None)
    power_sum, unused = lax.scan(add_power, jnp.zeros((TILES, CORE, CORE), jnp.float32), (response, socs_weight))
    resist, slope_map = resist_step(power_sum / clear_sum, target)

    def add_grad(acc_spec, kernel_pair):
        resp_one, weight_one = kernel_pair
        optical_field = field_of(resp_one)
        source = 2.0 * weight_one / clear_sum * slope_map * optical_field
        source_pad = jnp.zeros_like(spectrum).at[:, :CORE, :CORE].set(source)
        return (acc_spec + jnp.fft.fft2(source_pad) * jnp.conj(resp_one)[None], None)
    acc_spec, unused = lax.scan(add_grad, jnp.zeros_like(spectrum), (response, socs_weight))
    ext_grad = jnp.real(jnp.fft.ifft2(acc_spec))
    return (resist, fold(ext_grad, right_link, down_link))
```

```python
import functools
import math

import jax
import jax.numpy as jnp
import ml_dtypes
import numpy as np
from jax import lax
from jax.experimental import pallas as pl
from jax.experimental.pallas import tpu as pltpu
from jax.sharding import PartitionSpec as P

GRID_W = 8
STEEP = 20.0
THRESH = 0.33
BLK = 128
EXTENT = 3 * BLK
CORE = 2 * BLK
HALO = BLK // 2
HALF_SQRT3 = math.sqrt(3.0) / 2.0
MESH = pl.DeviceIdType.MESH
F32 = jnp.float32
BF16 = jnp.bfloat16


def dft_tables():
    place = np.arange(BLK)
    groups = (3 * place, 3 * place + 1, -(3 * place + 1))
    mats = []
    for freq in groups:
        angle = 2.0 * np.pi * (np.outer(place, freq) % EXTENT) / EXTENT
        c, s = np.cos(angle), -np.sin(angle)
        mats.append(np.block([[c, s], [-s, c]]))
    fwd = np.stack(mats).astype(np.float32)
    both = np.stack([fwd, fwd.transpose(0, 2, 1)])
    high = both.astype(ml_dtypes.bfloat16)
    low = (both - high.astype(np.float32)).astype(ml_dtypes.bfloat16)
    return np.stack([high, low])


def split(x):
    high = x.astype(BF16)
    return high, (x - high.astype(F32)).astype(BF16)


def dot(a, b):
    return jnp.dot(a, b, preferred_element_type=F32)


def mul_right(x, high, low):
    xh, xl = split(x)
    return dot(xh, high) + (dot(xh, low) + dot(xl, high))


def mul_left(high, low, x):
    xh, xl = split(x)
    return dot(high, xh) + (dot(low, xh) + dot(high, xl))


def fwd_mat(tab, g):
    return tab[0, 0, g], tab[1, 0, g]


def t_mat(tab, g):
    return tab[0, 1, g], tab[1, 1, g]


def lanes(re, im):
    return jnp.concatenate([re, im], axis=1)


def rows(re, im):
    return jnp.concatenate([re, im], axis=0)


def responses(kernels, tab, mid, resp):
    scale = 1.0 / (EXTENT * EXTENT)
    re = jnp.concatenate([kernels[0, k] for k in range(3)], axis=1) * scale
    im = jnp.concatenate([kernels[1, k] for k in range(3)], axis=1) * -scale
    taps = rows(re, im)
    for g in range(3):
        out = mul_left(*t_mat(tab, g), taps)
        mid[0, pl.ds(g * BLK, BLK), :] = out[:BLK]
        mid[1, pl.ds(g * BLK, BLK), :] = out[BLK:]
    for k in range(3):
        cols = pl.ds(k * BLK, BLK)
        x = lanes(mid[0, :, cols], mid[1, :, cols])
        for g in range(3):
            out = mul_right(x, *fwd_mat(tab, g))
            resp[k, 0, :, pl.ds(g * BLK, BLK)] = out[:, :BLK]
            resp[k, 1, :, pl.ds(g * BLK, BLK)] = out[:, BLK:]


def spectrum(ext, tab, mid, spec):
    x0, x1, x2 = (ext[:, pl.ds(j * BLK, BLK)] for j in range(3))
    z0 = x0 + x1 + x2
    z1 = lanes(x0 - 0.5 * (x1 + x2), HALF_SQRT3 * (x2 - x1))
    h0, l0 = fwd_mat(tab, 0)
    out0 = mul_right(z0, h0[:BLK], l0[:BLK])
    out1 = mul_right(z1, *fwd_mat(tab, 1))
    mid[0, :, pl.ds(0, BLK)] = out0[:, :BLK]
    mid[1, :, pl.ds(0, BLK)] = out0[:, BLK:]
    mid[0, :, pl.ds(BLK, BLK)] = out1[:, :BLK]
    mid[1, :, pl.ds(BLK, BLK)] = out1[:, BLK:]
    two = pl.ds(0, CORE)
    a_re, b_re, c_re = (mid[0, pl.ds(j * BLK, BLK), two] for j in range(3))
    a_im, b_im, c_im = (mid[1, pl.ds(j * BLK, BLK), two] for j in range(3))
    s_re, s_im = b_re + c_re, b_im + c_im
    e_re, e_im = a_re - 0.5 * s_re, a_im - 0.5 * s_im
    f_re, f_im = HALF_SQRT3 * (b_re - c_re), HALF_SQRT3 * (b_im - c_im)
    z_re, z_im = a_re + s_re, a_im + s_im
    z_re = lanes(z_re, z_re[:, BLK:])
    z_im = lanes(z_im, -z_im[:, BLK:])
    out = mul_left(*t_mat(tab, 0), rows(z_re, z_im))
    spec[0, pl.ds(0, BLK), :] = out[:BLK]
    spec[1, pl.ds(0, BLK), :] = out[BLK:]
    out1 = mul_left(*t_mat(tab, 1), rows(e_re + f_im, e_im - f_re))
    out2 = mul_left(*t_mat(tab, 2), rows(e_re - f_im, e_im + f_re))
    spec[0, pl.ds(BLK, BLK), :] = lanes(out1[:BLK], out2[:BLK, BLK:])
    spec[1, pl.ds(BLK, BLK), :] = lanes(out1[BLK:], -out2[BLK:, BLK:])
    spec[0, pl.ds(2 * BLK, BLK), :] = lanes(out2[:BLK], out1[:BLK, BLK:])
    spec[1, pl.ds(2 * BLK, BLK), :] = lanes(out2[BLK:], -out1[BLK:, BLK:])


def field_of(k, resp, spec, tab, mid, field):
    t = []
    for g in range(3):
        cols = pl.ds(g * BLK, BLK)
        q_re, q_im = resp[k, 0, :, cols], resp[k, 1, :, cols]
        e_re, e_im = spec[0, :, cols], spec[1, :, cols]
        x = lanes(e_re * q_re + e_im * q_im, e_im * q_re - e_re * q_im)
        t.append(mul_right(x, *t_mat(tab, g)))
    s, d = t[1] + t[2], HALF_SQRT3 * (t[1] - t[2])
    first, e = t[0] + s, t[0] - 0.5 * s
    mid[0, :, pl.ds(0, BLK)] = first[:, :BLK]
    mid[1, :, pl.ds(0, BLK)] = first[:, BLK:]
    mid[0, :, pl.ds(BLK, BLK)] = e[:, :BLK] - d[:, BLK:]
    mid[1, :, pl.ds(BLK, BLK)] = e[:, BLK:] + d[:, :BLK]
    t = []
    for g in range(3):
        block = pl.ds(g * BLK, BLK)
        x = rows(mid[0, block, pl.ds(0, CORE)], mid[1, block, pl.ds(0, CORE)])
        t.append(mul_left(*fwd_mat(tab, g), x))
    s, d = t[1] + t[2], HALF_SQRT3 * (t[1] - t[2])
    first, e = t[0] + s, t[0] - 0.5 * s
    field[k, 0, pl.ds(0, BLK), :] = first[:BLK]
    field[k, 1, pl.ds(0, BLK), :] = first[BLK:]
    field[k, 0, pl.ds(BLK, BLK), :] = e[:BLK] - d[BLK:]
    field[k, 1, pl.ds(BLK, BLK), :] = e[BLK:] + d[:BLK]


def grad_of(k, factor, slope, field, resp, tab, mid, acc):
    scaled = factor * slope[...]
    s_re, s_im = scaled * field[k, 0], scaled * field[k, 1]
    a_re, a_im, b_re, b_im = s_re[:BLK], s_im[:BLK], s_re[BLK:], s_im[BLK:]
    e_re, e_im = a_re - 0.5 * b_re, a_im - 0.5 * b_im
    f_re, f_im = HALF_SQRT3 * b_re, HALF_SQRT3 * b_im
    z = (
        rows(a_re + b_re, a_im + b_im),
        rows(e_re + f_im, e_im - f_re),
        rows(e_re - f_im, e_im + f_re),
    )
    for g in range(3):
        out = mul_left(*t_mat(tab, g), z[g])
        mid[0, pl.ds(g * BLK, BLK), pl.ds(0, CORE)] = out[:BLK]
        mid[1, pl.ds(g * BLK, BLK), pl.ds(0, CORE)] = out[BLK:]
    first, second = pl.ds(0, BLK), pl.ds(BLK, BLK)
    a_re, a_im, b_re, b_im = mid[0, :, first], mid[1, :, first], mid[0, :, second], mid[1, :, second]
    e_re, e_im = a_re - 0.5 * b_re, a_im - 0.5 * b_im
    f_re, f_im = HALF_SQRT3 * b_re, HALF_SQRT3 * b_im
    z = (
        lanes(a_re + b_re, a_im + b_im),
        lanes(e_re + f_im, e_im - f_re),
        lanes(e_re - f_im, e_im + f_re),
    )
    for g in range(3):
        cols = pl.ds(g * BLK, BLK)
        out = mul_right(z[g], *fwd_mat(tab, g))
        o_re, o_im = out[:, :BLK], out[:, BLK:]
        q_re, q_im = resp[k, 0, :, cols], resp[k, 1, :, cols]
        acc[0, :, cols] += o_re * q_re - o_im * q_im
        acc[1, :, cols] += o_re * q_im + o_im * q_re


def ext_gradient(acc, tab, mid):
    p0, p1, p2 = (pl.ds(g * BLK, BLK) for g in range(3))
    t0 = mul_left(*fwd_mat(tab, 0), rows(acc[0, p0, :], acc[1, p0, :]))
    t0_re, t0_im = t0[:BLK], t0[BLK:]
    t0_re = lanes(t0_re[:, :BLK], t0_re[:, BLK:CORE] + t0_re[:, CORE:])
    t0_im = lanes(t0_im[:, :BLK], t0_im[:, BLK:CORE] - t0_im[:, CORE:])
    x_re = lanes(acc[0, p1, p0], acc[0, p1, p1] + acc[0, p2, p2])
    x_im = lanes(acc[1, p1, p0], acc[1, p1, p1] - acc[1, p2, p2])
    t1 = mul_left(*fwd_mat(tab, 1), rows(x_re, x_im))
    x_re = lanes(acc[0, p2, p0], acc[0, p2, p1] + acc[0, p1, p2])
    x_im = lanes(acc[1, p2, p0], acc[1, p2, p1] - acc[1, p1, p2])
    t2 = mul_left(*fwd_mat(tab, 2), rows(x_re, x_im))
    s, d = t1 + t2, HALF_SQRT3 * (t1 - t2)
    e_re, e_im = t0_re - 0.5 * s[:BLK], t0_im - 0.5 * s[BLK:]
    two = pl.ds(0, CORE)
    mid[0, p0, two], mid[1, p0, two] = t0_re + s[:BLK], t0_im + s[BLK:]
    mid[0, p1, two], mid[1, p1, two] = e_re - d[BLK:], e_im + d[:BLK]
    mid[0, p2, two], mid[1, p2, two] = e_re + d[BLK:], e_im - d[:BLK]
    h0, l0 = t_mat(tab, 0)
    r0 = mul_right(lanes(mid[0, :, p0], mid[1, :, p0]), h0[:, :BLK], l0[:, :BLK])
    r1 = mul_right(lanes(mid[0, :, p1], mid[1, :, p1]), *t_mat(tab, 1))
    e, d = r0 - 0.5 * r1[:, :BLK], HALF_SQRT3 * r1[:, BLK:]
    return r0 + r1[:, :BLK], e - d, e + d


def body_kernel(
    mask, kernels, target, tab, weight, link, resist_out, grad_out,
    mid, resp, spec, field, acc, ext, side_out, side_in, vert_out, vert_in,
    clear_in, clear_sum, clear_far, power, power_in, power_mine, power_far, power_all, slope,
    grad_parts, grad_in, grad_sum, grad_far, owned, fold_out, fold_in, edge_out, edge_in, gathered,
    side_send, side_recv, vert_send, vert_recv, share_send, share_recv,
    clear_send, clear_recv, cfar_send, cfar_recv,
    psc_send, psc_recv, pfar_send, pfar_recv, pall_send, pall_recv,
    gsc_send, gsc_recv, gfar_send, gfar_recv, fold_send, fold_recv,
    edge_send, edge_recv, near_send, near_recv, all_send, all_recv,
):
    tile = lax.axis_index("tile")
    kern = lax.axis_index("kern")
    tiles = lax.axis_size("tile")
    x = kern // 2
    half = kern % 2
    column = (tile + GRID_W // 2) % GRID_W
    right_ok = jnp.where((column < GRID_W - 1) & (tile + 1 < tiles), 1.0, 0.0)
    down_ok = jnp.where(tile + GRID_W < tiles, 1.0, 0.0)
    right_link = link[0, 0].astype(F32) * right_ok
    down_link = link[0, 1].astype(F32) * down_ok

    def at(tile_by, kern_index):
        return {"tile": (tile + tile_by + tiles) % tiles, "kern": kern_index}

    right, left, below, above = at(1, kern), at(-1, kern), at(GRID_W, kern), at(-GRID_W, kern)
    far = at(0, 2 * x + 1 - half)
    x_at = [(x + d) % 4 for d in range(4)]
    peers = [at(0, 2 * x_at[d] + half) for d in range(4)]
    corner_tile = jnp.where((x == 0) | (x == 2), -GRID_W, GRID_W)
    cross = at(corner_tile, 2 * (x + 1 - 2 * (x % 2)) + half)

    barrier = pltpu.get_barrier_semaphore()
    partners = [right, left, below, above, far, cross] + peers[1:]
    for one in partners:
        pl.semaphore_signal(barrier, inc=1, device_id=one, device_id_type=MESH)

    def remote(src, dst, send, recv, device):
        return pltpu.make_async_remote_copy(
            src_ref=src, dst_ref=dst, send_sem=send, recv_sem=recv, device_id=device, device_id_type=MESH
        )

    lane = lax.broadcasted_iota(jnp.int32, (BLK, BLK), 1) < HALO
    lane_all = lax.broadcasted_iota(jnp.int32, (CORE, BLK), 1) < HALO

    a0, a1 = mask[0, :, pl.ds(0, BLK)], mask[0, :, pl.ds(BLK, BLK)]
    r0, r1 = pltpu.roll(a0, HALO, 1), pltpu.roll(a1, HALO, 1)
    outer = jnp.where(lane_all, r1, r0)
    inner = jnp.where(lane_all, r0, r1)
    flipped = pltpu.roll(outer, HALO, 1)
    side_out[0] = jnp.where(lane, outer[:BLK], flipped[BLK:]) * right_link
    side_out[1] = jnp.where(lane, flipped[:BLK], outer[BLK:])
    taps = [[jnp.sum(kernels[c, k], keepdims=True) for k in range(3)] for c in range(2)]
    clear_part = sum(weight[k] * (taps[0][k] * taps[0][k] + taps[1][k] * taps[1][k]) for k in range(3))
    clear_in[x] = jnp.broadcast_to(clear_part, (8, BLK))

    pl.semaphore_wait(barrier, len(partners))
    to_right = remote(side_out.at[0], side_in.at[0], side_send.at[0], side_recv.at[0], right)
    to_left = remote(side_out.at[1], side_in.at[1], side_send.at[1], side_recv.at[1], left)
    to_right.start()
    to_left.start()
    clear_copies = [
        remote(clear_in.at[x], clear_in.at[x], clear_send.at[d - 1], clear_recv.at[d - 1], peers[d])
        for d in range(1, 4)
    ]
    for copy in clear_copies:
        copy.start()

    middle = pl.ds(HALO, CORE)
    ext[middle, pl.ds(BLK, BLK)] = inner
    to_right.wait_recv()
    to_left.wait_recv()
    from_left, from_right = side_in[0], side_in[1] * right_link
    upper, lower = pl.ds(HALO, BLK), pl.ds(HALO + BLK, BLK)
    ext[upper, pl.ds(0, BLK)] = jnp.where(lane, from_left, outer[:BLK])
    ext[lower, pl.ds(0, BLK)] = jnp.where(lane, pltpu.roll(from_left, HALO, 1), outer[BLK:])
    ext[upper, pl.ds(CORE, BLK)] = jnp.where(lane, outer[:BLK], pltpu.roll(from_right, HALO, 1))
    ext[lower, pl.ds(CORE, BLK)] = jnp.where(lane, outer[BLK:], from_right)

    part = HALO // 4
    vert_out[0] = ext[pl.ds(pl.multiple_of(CORE + part * x, part), part), :] * down_link
    vert_out[1] = ext[pl.ds(pl.multiple_of(HALO + part * x, part), part), :]
    to_below = remote(vert_out.at[0], vert_in.at[x, 0], vert_send.at[0], vert_recv.at[0], below)
    to_above = remote(vert_out.at[1], vert_in.at[x, 1], vert_send.at[1], vert_recv.at[1], above)
    to_below.start()
    to_above.start()

    responses(kernels, tab, mid, resp)

    to_below.wait_recv()
    to_above.wait_recv()
    shares = [
        remote(vert_in.at[x], vert_in.at[x], share_send.at[d - 1], share_recv.at[d - 1], peers[d])
        for d in range(1, 4)
    ]
    for copy in shares:
        copy.start()
    for copy in clear_copies:
        copy.wait_recv()
    clear_sum[...] = clear_in[0] + clear_in[1] + clear_in[2] + clear_in[3]
    clear_copy = remote(clear_sum, clear_far, cfar_send, cfar_recv, far)
    clear_copy.start()
    for copy in shares:
        copy.wait_recv()
    for q in range(4):
        ext[pl.ds(part * q, part), :] = vert_in[q, 0]
        ext[pl.ds(HALO + CORE + part * q, part), :] = vert_in[q, 1] * down_link

    spectrum(ext, tab, mid, spec)

    def field_step(k, carry):
        field_of(k, resp, spec, tab, mid, field)
        return carry

    lax.fori_loop(0, 3, field_step, 0)
    for q in range(4):
        block = pl.ds(q * HALO, HALO)
        power[q] = sum(
            weight[k] * (field[k, 0, block, :] * field[k, 0, block, :] + field[k, 1, block, :] * field[k, 1, block, :])
            for k in range(3)
        )

    scatter = [
        remote(power.at[x_at[d]], power_in.at[d - 1], psc_send.at[d - 1], psc_recv.at[d - 1], peers[d])
        for d in range(1, 4)
    ]
    for copy in scatter:
        copy.start()
    acc[...] = jnp.zeros_like(acc)
    clear_copy.wait_recv()
    for copy in scatter:
        copy.wait_recv()
    power_mine[...] = power[x] + power_in[0] + power_in[1] + power_in[2]
    swap = remote(power_mine, power_far, pfar_send, pfar_recv, far)
    swap.start()
    swap.wait_recv()
    power_all[x] = power_mine[...] + power_far[...]
    gather = [
        remote(power_all.at[x], power_all.at[x], pall_send.at[d - 1], pall_recv.at[d - 1], peers[d])
        for d in range(1, 4)
    ]
    for copy in gather:
        copy.start()
    for copy in gather:
        copy.wait_recv()
    clear = (clear_sum[...] + clear_far[...])[0:1, 0:1]
    for q in range(4):
        block = pl.ds(q * HALO, HALO)
        intensity = power_all[q] / clear
        resist = 1.0 / (1.0 + jnp.exp(-STEEP * (intensity - THRESH)))
        resist_out[0, block, :] = resist
        wanted = target[0, block, :].astype(F32)
        slope[block, :] = (4.0 * STEEP) * (resist - wanted) * resist * (1.0 - resist) / clear

    def grad_step(k, carry):
        grad_of(k, weight[k], slope, field, resp, tab, mid, acc)
        return carry

    lax.fori_loop(0, 3, grad_step, 0)
    blocks = ext_gradient(acc, tab, mid)
    bits = [(HALO + 64 * q + 32 * h, q, h, 0, 32) for q in range(4) for h in range(2)]
    bits += [(EXTENT - HALO + 32 * h + 16 * q, q, h, 32, 16) for q in range(2) for h in range(2)]
    bits += [(32 * h + 16 * (3 - q), q, h, 32, 16) for q in (2, 3) for h in range(2)]
    for c in range(3):
        for start, q, h, to, count in bits:
            grad_parts[q, h, pl.ds(to, count), pl.ds(c * BLK, BLK)] = blocks[c][start : start + count]

    scatter = [
        remote(grad_parts.at[x_at[d]], grad_in.at[d - 1], gsc_send.at[d - 1], gsc_recv.at[d - 1], peers[d])
        for d in range(1, 4)
    ]
    for copy in scatter:
        copy.start()
    for copy in scatter:
        copy.wait_recv()
    grad_sum[...] = grad_parts[x] + grad_in[0] + grad_in[1] + grad_in[2]
    swap2 = remote(grad_sum.at[1 - half], grad_far, gfar_send, gfar_recv, far)
    swap2.start()
    swap2.wait_recv()
    total = grad_sum[half] + grad_far[...]

    low_x = x < 2
    fold_out[...] = total[32:] * jnp.where(low_x, down_link, 1.0)
    owned[...] = total[:32]
    slot = jnp.where((x == 1) | (x == 2), 1, 0)
    fold_copy = remote(
        fold_out, fold_in.at[slot], fold_send, fold_recv.at[slot],
        at(jnp.where(low_x, GRID_W, -GRID_W), jnp.where(low_x, 0, 6) + half),
    )
    fold_copy.start()

    @pl.when((x == 0) | (x == 3))
    def _():
        factor = jnp.where(x == 0, 1.0, down_link)
        for s in range(2):
            remote(fold_out, fold_in.at[s], fold_send, fold_recv.at[s], far).wait_recv()
        for s in range(2):
            owned[pl.ds(16 * s, 16), :] += fold_in[s] * factor

    edge_out[0] = owned[:, pl.ds(CORE, BLK)] * right_link
    edge_out[1] = owned[:, pl.ds(0, BLK)]
    edges = [
        remote(edge_out.at[0], edge_in.at[0], edge_send.at[0], edge_recv.at[0], right),
        remote(edge_out.at[1], edge_in.at[1], edge_send.at[1], edge_recv.at[1], left),
    ]
    for copy in edges:
        copy.start()
    for copy in edges:
        copy.wait_recv()
    near_lane = lax.broadcasted_iota(jnp.int32, (32, BLK), 1) < HALO
    b0 = owned[:, pl.ds(0, BLK)] + edge_in[0]
    b1 = owned[:, pl.ds(BLK, BLK)]
    b2 = owned[:, pl.ds(CORE, BLK)] + edge_in[1] * right_link
    c0, c1, c2 = (pltpu.roll(b, HALO, 1) for b in (b0, b1, b2))
    gathered[x, half] = lanes(jnp.where(near_lane, c0, c1), jnp.where(near_lane, c1, c2))

    mine = gathered.at[x, half]
    near = remote(mine, mine, near_send, near_recv, far)
    near.start()
    near.wait_recv()
    finals = [
        remote(gathered.at[x], gathered.at[x], all_send.at[d - 1], all_recv.at[d - 1], peers[d])
        for d in range(1, 4)
    ]
    for copy in finals:
        copy.start()
    for copy in finals:
        copy.wait_recv()
    for q in range(4):
        for h in range(2):
            grad_out[0, pl.ds(64 * q + 32 * h, 32), :] = gathered[q, h]

    sent = [to_right, to_left, to_below, to_above, clear_copy, swap, swap2, fold_copy, near]
    for copy in sent + clear_copies + shares + gather + edges + finals:
        copy.wait_send()
    for d in range(1, 4):
        remote(power.at[x], power_in.at[d - 1], psc_send.at[d - 1], psc_recv.at[d - 1], peers[d]).wait_send()
    for copy in scatter:
        copy.wait_send()


def body(mask, kernels, weight, link, target):
    vmem = pl.BlockSpec(memory_space=pltpu.VMEM)
    smem = pl.BlockSpec(memory_space=pltpu.SMEM)
    dma = pltpu.SemaphoreType.DMA
    f32 = lambda *shape: pltpu.VMEM(shape, F32)
    scratch = [
        f32(2, EXTENT, EXTENT), f32(3, 2, EXTENT, EXTENT), f32(2, EXTENT, EXTENT), f32(3, 2, CORE, CORE),
        f32(2, EXTENT, EXTENT), f32(EXTENT, EXTENT),
        f32(2, BLK, BLK), f32(2, BLK, BLK), f32(2, 16, EXTENT), f32(4, 2, 16, EXTENT),
        f32(4, 8, BLK), f32(8, BLK), f32(8, BLK),
        f32(4, HALO, CORE), f32(3, HALO, CORE), f32(HALO, CORE), f32(HALO, CORE), f32(4, HALO, CORE), f32(CORE, CORE),
        f32(4, 2, 48, EXTENT), f32(3, 2, 48, EXTENT), f32(2, 48, EXTENT), f32(48, EXTENT),
        f32(32, EXTENT), f32(16, EXTENT), f32(2, 16, EXTENT), f32(2, 32, BLK), f32(2, 32, BLK), f32(4, 2, 32, CORE),
    ]
    scratch += [dma((2,))] * 4 + [dma((3,))] * 4 + [dma] * 2 + [dma((3,))] * 2 + [dma] * 2 + [dma((3,))] * 2
    scratch += [dma((3,))] * 2 + [dma] * 2 + [dma, dma((2,))] + [dma((2,))] * 2 + [dma] * 2 + [dma((3,))] * 2
    out = jax.ShapeDtypeStruct((1, CORE, CORE), F32)
    return pl.pallas_call(
        body_kernel,
        out_shape=(out, out),
        in_specs=[vmem, vmem, vmem, vmem, smem, smem],
        out_specs=(vmem, vmem),
        scratch_shapes=scratch,
        compiler_params=pltpu.CompilerParams(
            collective_id=0, has_side_effects=True, vmem_limit_bytes=48 * 2**20
        ),
    )(mask, kernels, target, jnp.asarray(dft_tables()), weight, link)


def solution(mesh):
    in_specs = (
        P("tile", None, None),
        P(None, "kern", None, None),
        P("kern"),
        P("tile", None),
        P("tile", None, None),
    )
    out_specs = (P("tile", None, None), P("tile", None, None))
    return jax.shard_map(body, mesh=mesh, in_specs=in_specs, out_specs=out_specs, check_vma=False)
```

```python
import functools
import math

import jax
import jax.numpy as jnp
import ml_dtypes
import numpy as np
from jax import lax
from jax.experimental import pallas as pl
from jax.experimental.pallas import tpu as pltpu
from jax.sharding import PartitionSpec as P

GRID_W = 8
STEEP = 20.0
THRESH = 0.33
BLK = 128
EXTENT = 3 * BLK
CORE = 2 * BLK
HALO = BLK // 2
HALF_SQRT3 = math.sqrt(3.0) / 2.0
MESH = pl.DeviceIdType.MESH
F32 = jnp.float32
BF16 = jnp.bfloat16


def dft_tables():
    place = np.arange(BLK)
    groups = (3 * place, 3 * place + 1, -(3 * place + 1))
    mats = []
    for freq in groups:
        angle = 2.0 * np.pi * (np.outer(place, freq) % EXTENT) / EXTENT
        c, s = np.cos(angle), -np.sin(angle)
        mats.append(np.block([[c, s], [-s, c]]))
    fwd = np.stack(mats).astype(np.float32)
    both = np.stack([fwd, fwd.transpose(0, 2, 1)])
    high = both.astype(ml_dtypes.bfloat16)
    low = (both - high.astype(np.float32)).astype(ml_dtypes.bfloat16)
    return np.stack([high, low])


def split(x):
    high = x.astype(BF16)
    return high, (x - high.astype(F32)).astype(BF16)


def dot(a, b):
    return jnp.dot(a, b, preferred_element_type=F32)


def mul_right(x, high, low):
    xh, xl = split(x)
    return dot(xh, high) + (dot(xh, low) + dot(xl, high))


def mul_left(high, low, x):
    xh, xl = split(x)
    return dot(high, xh) + (dot(low, xh) + dot(high, xl))


def fwd_mat(tab, g):
    return tab[0, 0, g], tab[1, 0, g]


def t_mat(tab, g):
    return tab[0, 1, g], tab[1, 1, g]


def lanes(re, im):
    return jnp.concatenate([re, im], axis=1)


def rows(re, im):
    return jnp.concatenate([re, im], axis=0)


def response_rows(kernels, tab, mid):
    scale = 1.0 / (EXTENT * EXTENT)
    re = jnp.concatenate([kernels[0, k] for k in range(3)], axis=1) * scale
    im = jnp.concatenate([kernels[1, k] for k in range(3)], axis=1) * -scale
    taps = rows(re, im)
    for g in range(3):
        out = mul_left(*t_mat(tab, g), taps)
        mid[0, pl.ds(g * BLK, BLK), :] = out[:BLK]
        mid[1, pl.ds(g * BLK, BLK), :] = out[BLK:]


def response_cols(k, tab, mid, resp):
    cols = pl.ds(k * BLK, BLK)
    x = lanes(mid[0, :, cols], mid[1, :, cols])
    for g in range(3):
        out = mul_right(x, *fwd_mat(tab, g))
        resp[0, :, pl.ds(k * EXTENT + g * BLK, BLK)] = out[:, :BLK]
        resp[1, :, pl.ds(k * EXTENT + g * BLK, BLK)] = out[:, BLK:]


def spectrum_cols(ext, places, tab, mid):
    x0, x1, x2 = (
        jnp.concatenate([ext[pl.ds(s, n), pl.ds(j * BLK, BLK)] for s, n in places], axis=0) for j in range(3)
    )
    z0 = x0 + x1 + x2
    z1 = lanes(x0 - 0.5 * (x1 + x2), HALF_SQRT3 * (x2 - x1))
    h0, l0 = fwd_mat(tab, 0)
    outs = (mul_right(z0, h0[:BLK], l0[:BLK]), mul_right(z1, *fwd_mat(tab, 1)))
    for g, out in enumerate(outs):
        at = 0
        for s, n in places:
            mid[0, pl.ds(s, n), pl.ds(g * BLK, BLK)] = out[at : at + n, :BLK]
            mid[1, pl.ds(s, n), pl.ds(g * BLK, BLK)] = out[at : at + n, BLK:]
            at += n


def spectrum_rows(tab, mid, spec):
    two = pl.ds(0, CORE)
    a_re, b_re, c_re = (mid[0, pl.ds(j * BLK, BLK), two] for j in range(3))
    a_im, b_im, c_im = (mid[1, pl.ds(j * BLK, BLK), two] for j in range(3))
    s_re, s_im = b_re + c_re, b_im + c_im
    e_re, e_im = a_re - 0.5 * s_re, a_im - 0.5 * s_im
    f_re, f_im = HALF_SQRT3 * (b_re - c_re), HALF_SQRT3 * (b_im - c_im)
    z_re, z_im = a_re + s_re, a_im + s_im
    z_re = lanes(z_re, z_re[:, BLK:])
    z_im = lanes(z_im, -z_im[:, BLK:])
    out = mul_left(*t_mat(tab, 0), rows(z_re, z_im))
    spec[0, pl.ds(0, BLK), :] = out[:BLK]
    spec[1, pl.ds(0, BLK), :] = out[BLK:]
    out1 = mul_left(*t_mat(tab, 1), rows(e_re + f_im, e_im - f_re))
    out2 = mul_left(*t_mat(tab, 2), rows(e_re - f_im, e_im + f_re))
    spec[0, pl.ds(BLK, BLK), :] = lanes(out1[:BLK], out2[:BLK, BLK:])
    spec[1, pl.ds(BLK, BLK), :] = lanes(out1[BLK:], -out2[BLK:, BLK:])
    spec[0, pl.ds(2 * BLK, BLK), :] = lanes(out2[:BLK], out1[:BLK, BLK:])
    spec[1, pl.ds(2 * BLK, BLK), :] = lanes(out2[BLK:], -out1[BLK:, BLK:])


PAIRS = [[(b // 3, b % 3) for b in range(s, min(s + 2, 9))] for s in range(0, 9, 2)]


def field_rows(pair, resp, spec, tab, mid):
    width = len(pair) * BLK
    start = (pair[0][0] * 3 + pair[0][1]) * BLK
    cols = pl.ds(start, width)
    t = []
    for g in range(3):
        block = pl.ds(g * BLK, BLK)
        q_re, q_im = resp[0, block, cols], resp[1, block, cols]
        e_re = jnp.concatenate([spec[0, block, pl.ds(f * BLK, BLK)] for _, f in pair], axis=1)
        e_im = jnp.concatenate([spec[1, block, pl.ds(f * BLK, BLK)] for _, f in pair], axis=1)
        x = rows(e_re * q_re + e_im * q_im, e_im * q_re - e_re * q_im)
        t.append(mul_left(*fwd_mat(tab, g), x))
    s, d = t[1] + t[2], HALF_SQRT3 * (t[1] - t[2])
    first, e = t[0] + s, t[0] - 0.5 * s
    upper, lower = pl.ds(0, BLK), pl.ds(BLK, BLK)
    mid[0, upper, cols] = first[:BLK]
    mid[1, upper, cols] = first[BLK:]
    mid[0, lower, cols] = e[:BLK] - d[BLK:]
    mid[1, lower, cols] = e[BLK:] + d[:BLK]


def field_cols(h, tab, mid, field):
    t = []
    for g in range(3):
        x = jnp.concatenate(
            [
                lanes(*(mid[c, pl.ds(h * BLK, BLK), pl.ds(k * EXTENT + g * BLK, BLK)] for c in range(2)))
                for k in range(3)
            ],
            axis=0,
        )
        t.append(mul_right(x, *t_mat(tab, g)))
    s, d = t[1] + t[2], HALF_SQRT3 * (t[1] - t[2])
    first, e = t[0] + s, t[0] - 0.5 * s
    field[h, 0] = lanes(first[:, :BLK], e[:, :BLK] - d[:, BLK:])
    field[h, 1] = lanes(first[:, BLK:], e[:, BLK:] + d[:, :BLK])


def source_cols(h, slope, weight, tab, field, mid):
    scaled = jnp.concatenate([weight[k] * slope for k in range(3)], axis=0)
    s_re, s_im = scaled * field[h, 0], scaled * field[h, 1]
    a_re, a_im, b_re, b_im = s_re[:, :BLK], s_im[:, :BLK], s_re[:, BLK:], s_im[:, BLK:]
    e_re, e_im = a_re - 0.5 * b_re, a_im - 0.5 * b_im
    f_re, f_im = HALF_SQRT3 * b_re, HALF_SQRT3 * b_im
    z = (
        lanes(a_re + b_re, a_im + b_im),
        lanes(e_re + f_im, e_im - f_re),
        lanes(e_re - f_im, e_im + f_re),
    )
    for g in range(3):
        out = mul_right(z[g], *fwd_mat(tab, g))
        for k in range(3):
            cols = pl.ds(k * EXTENT + g * BLK, BLK)
            mid[0, pl.ds(h * BLK, BLK), cols] = out[k * BLK : (k + 1) * BLK, :BLK]
            mid[1, pl.ds(h * BLK, BLK), cols] = out[k * BLK : (k + 1) * BLK, BLK:]


def source_rows(pair, resp, tab, mid, acc):
    width = len(pair) * BLK
    start = (pair[0][0] * 3 + pair[0][1]) * BLK
    cols = pl.ds(start, width)
    upper, lower = pl.ds(0, BLK), pl.ds(BLK, BLK)
    a_re, a_im, b_re, b_im = mid[0, upper, cols], mid[1, upper, cols], mid[0, lower, cols], mid[1, lower, cols]
    e_re, e_im = a_re - 0.5 * b_re, a_im - 0.5 * b_im
    f_re, f_im = HALF_SQRT3 * b_re, HALF_SQRT3 * b_im
    z = (
        rows(a_re + b_re, a_im + b_im),
        rows(e_re + f_im, e_im - f_re),
        rows(e_re - f_im, e_im + f_re),
    )
    for g in range(3):
        out = mul_left(*t_mat(tab, g), z[g])
        block = pl.ds(g * BLK, BLK)
        o_re, o_im = out[:BLK], out[BLK:]
        q_re, q_im = resp[0, block, cols], resp[1, block, cols]
        p_re, p_im = o_re * q_re - o_im * q_im, o_re * q_im + o_im * q_re
        for n, (k, f) in enumerate(pair):
            into = pl.ds(f * BLK, BLK)
            part = slice(n * BLK, (n + 1) * BLK)
            if k == 0:
                acc[0, block, into] = p_re[:, part]
                acc[1, block, into] = p_im[:, part]
            else:
                acc[0, block, into] += p_re[:, part]
                acc[1, block, into] += p_im[:, part]


def gradient_rows(acc, tab, mid):
    p0, p1, p2 = (pl.ds(g * BLK, BLK) for g in range(3))
    t0 = mul_left(*fwd_mat(tab, 0), rows(acc[0, p0, :], acc[1, p0, :]))
    t0_re, t0_im = t0[:BLK], t0[BLK:]
    t0_re = lanes(t0_re[:, :BLK], t0_re[:, BLK:CORE] + t0_re[:, CORE:])
    t0_im = lanes(t0_im[:, :BLK], t0_im[:, BLK:CORE] - t0_im[:, CORE:])
    x_re = lanes(acc[0, p1, p0], acc[0, p1, p1] + acc[0, p2, p2])
    x_im = lanes(acc[1, p1, p0], acc[1, p1, p1] - acc[1, p2, p2])
    t1 = mul_left(*fwd_mat(tab, 1), rows(x_re, x_im))
    x_re = lanes(acc[0, p2, p0], acc[0, p2, p1] + acc[0, p1, p2])
    x_im = lanes(acc[1, p2, p0], acc[1, p2, p1] - acc[1, p1, p2])
    t2 = mul_left(*fwd_mat(tab, 2), rows(x_re, x_im))
    s, d = t1 + t2, HALF_SQRT3 * (t1 - t2)
    e_re, e_im = t0_re - 0.5 * s[:BLK], t0_im - 0.5 * s[BLK:]
    two = pl.ds(0, CORE)
    mid[0, p0, two], mid[1, p0, two] = t0_re + s[:BLK], t0_im + s[BLK:]
    mid[0, p1, two], mid[1, p1, two] = e_re - d[BLK:], e_im + d[:BLK]
    mid[0, p2, two], mid[1, p2, two] = e_re + d[BLK:], e_im - d[:BLK]


def gradient_cols(places, tab, mid):
    h0, l0 = t_mat(tab, 0)
    part = lambda c, g: jnp.concatenate([mid[c, pl.ds(s, n), pl.ds(g * BLK, BLK)] for s, n in places], axis=0)
    r0 = mul_right(lanes(part(0, 0), part(1, 0)), h0[:, :BLK], l0[:, :BLK])
    r1 = mul_right(lanes(part(0, 1), part(1, 1)), *t_mat(tab, 1))
    e, d = r0 - 0.5 * r1[:, :BLK], HALF_SQRT3 * r1[:, BLK:]
    return r0 + r1[:, :BLK], e - d, e + d


QUARTER = CORE // 4
EIGHTH = CORE // 8
PART = HALO // 4


def body_kernel(
    mask_hbm, kernels_hbm, target_hbm, tab_hbm, weight, link, resist_out, grad_out,
    mask, kernels, target, tab, mid, wide, resp, spec, field, acc, ext, resist,
    side_out, side_in, vert_out, vert_in, corner_out, corner_in, margin,
    clear_in, clear_sum, clear_far, power, power_in, power_mine, power_far, power_all,
    halo_parts, halo_in, core_parts, core_in, fold_out, fold_in, bend_out, bend_in, edge_out, edge_in,
    mine, other, gathered,
    load_sem, store_sem, side_send, side_recv, vert_send, vert_recv, corner_send, corner_recv, share_send, share_recv,
    clear_send, clear_recv, cfar_send, cfar_recv,
    psc_send, psc_recv, pfar_send, pfar_recv, pall_send, pall_recv,
    hsc_send, hsc_recv, gsc_send, gsc_recv, fold_send, fold_recv, bend_send, bend_recv,
    edge_send, edge_recv, gfar_send, gfar_recv, all_send, all_recv,
):
    tile = lax.axis_index("tile")
    kern = lax.axis_index("kern")
    tiles = lax.axis_size("tile")
    x = kern // 2
    half = kern % 2
    column = (tile + GRID_W // 2) % GRID_W
    right_ok = jnp.where((column < GRID_W - 1) & (tile + 1 < tiles), 1.0, 0.0)
    down_ok = jnp.where(tile + GRID_W < tiles, 1.0, 0.0)
    right_link = link[0, 0].astype(F32) * right_ok
    down_link = link[0, 1].astype(F32) * down_ok

    def at(tile_by, kern_index):
        return {"tile": (tile + tile_by + tiles) % tiles, "kern": kern_index}

    right, left = at(1, kern), at(-1, kern)
    far = at(0, 2 * x + 1 - half)
    x_at = [(x + d) % 4 for d in range(4)]
    peers = [at(0, 2 * x_at[d] + half) for d in range(4)]
    verticals = [at(s * GRID_W + e, kern) for s in (1, -1) for e in (-1, 0, 1)]
    sign = 2 * (x % 2) - 1
    crossed = 2 * (x + 1 - 2 * (x % 2)) + half
    crosses = [at(sign * GRID_W + e, crossed) for e in (-1, 0, 1)]

    barrier = pltpu.get_barrier_semaphore()
    partners = verticals + [right, left, far] + peers[1:] + crosses
    for one in partners:
        pl.semaphore_signal(barrier, inc=1, device_id=one, device_id_type=MESH)

    loads = [
        pltpu.make_async_copy(src, dst, load_sem.at[n])
        for n, (src, dst) in enumerate(((mask_hbm, mask), (kernels_hbm, kernels), (tab_hbm, tab), (target_hbm, target)))
    ]
    for copy in loads:
        copy.start()
    started = []

    def remote(src, dst, send, recv, device):
        copy = pltpu.make_async_remote_copy(
            src_ref=src, dst_ref=dst, send_sem=send, recv_sem=recv, device_id=device, device_id_type=MESH
        )
        copy.start()
        started.append(copy)
        return copy

    lane = lax.broadcasted_iota(jnp.int32, (BLK, BLK), 1) < HALO
    lane_all = lax.broadcasted_iota(jnp.int32, (CORE, BLK), 1) < HALO
    lane_part = lax.broadcasted_iota(jnp.int32, (PART, BLK), 1) < HALO

    loads[0].wait()
    a0, a1 = mask[0, :, pl.ds(0, BLK)], mask[0, :, pl.ds(BLK, BLK)]
    r0, r1 = pltpu.roll(a0, HALO, 1), pltpu.roll(a1, HALO, 1)
    outer = jnp.where(lane_all, r1, r0)
    inner = jnp.where(lane_all, r0, r1)
    flipped = pltpu.roll(outer, HALO, 1)
    side_out[0] = jnp.where(lane, outer[:BLK], flipped[BLK:]) * right_link
    side_out[1] = jnp.where(lane, flipped[:BLK], outer[BLK:])
    middle = pl.ds(HALO, CORE)
    ext[middle, pl.ds(BLK, BLK)] = inner
    ext[middle, pl.ds(0, BLK)] = outer
    for n, first in enumerate((CORE - HALO, 0)):
        block = pl.ds(pl.multiple_of(HALO + first + PART * x, PART), PART)
        outer_part = ext[block, pl.ds(0, BLK)]
        vert_out[n, pl.ds(0, PART), pl.ds(0, BLK)] = outer_part
        vert_out[n, pl.ds(0, PART), pl.ds(BLK, BLK)] = ext[block, pl.ds(BLK, BLK)]
        vert_out[n, pl.ds(PART, 8), pl.ds(0, BLK)] = jnp.full((8, BLK), down_link, F32)
        vert_out[n, pl.ds(PART, 8), pl.ds(BLK, BLK)] = jnp.full((8, BLK), right_link, F32)
        corner_out[n, 0] = outer_part
        corner_out[n, 1] = outer_part * right_link

    pl.semaphore_wait(barrier, len(partners))
    verts = [
        remote(vert_out.at[0], vert_in.at[0], vert_send.at[0], vert_recv.at[0], verticals[1]),
        remote(vert_out.at[1], vert_in.at[1], vert_send.at[1], vert_recv.at[1], verticals[4]),
        remote(corner_out.at[0, 1], corner_in.at[0], corner_send.at[0], corner_recv.at[0], verticals[2]),
        remote(corner_out.at[0, 0], corner_in.at[1], corner_send.at[1], corner_recv.at[1], verticals[0]),
        remote(corner_out.at[1, 1], corner_in.at[2], corner_send.at[2], corner_recv.at[2], verticals[5]),
        remote(corner_out.at[1, 0], corner_in.at[3], corner_send.at[3], corner_recv.at[3], verticals[3]),
    ]
    sides = [
        remote(side_out.at[0], side_in.at[0], side_send.at[0], side_recv.at[0], right),
        remote(side_out.at[1], side_in.at[1], side_send.at[1], side_recv.at[1], left),
    ]

    loads[1].wait()
    taps = [[jnp.sum(kernels[c, k], keepdims=True) for k in range(3)] for c in range(2)]
    clear_part = sum(weight[k] * (taps[0][k] * taps[0][k] + taps[1][k] * taps[1][k]) for k in range(3))
    clear_in[x] = jnp.broadcast_to(clear_part, (8, BLK))
    clears = [
        remote(clear_in.at[x], clear_in.at[x], clear_send.at[d - 1], clear_recv.at[d - 1], peers[d])
        for d in range(1, 4)
    ]
    loads[2].wait()
    response_rows(kernels, tab, mid)
    response_cols(0, tab, mid, resp)

    for copy in sides:
        copy.wait_recv()
    from_left, from_right = side_in[0], side_in[1] * right_link
    upper, lower = pl.ds(HALO, BLK), pl.ds(HALO + BLK, BLK)
    up_outer, low_outer = ext[upper, pl.ds(0, BLK)], ext[lower, pl.ds(0, BLK)]
    ext[upper, pl.ds(0, BLK)] = jnp.where(lane, from_left, up_outer)
    ext[lower, pl.ds(0, BLK)] = jnp.where(lane, pltpu.roll(from_left, HALO, 1), low_outer)
    ext[upper, pl.ds(CORE, BLK)] = jnp.where(lane, up_outer, pltpu.roll(from_right, HALO, 1))
    ext[lower, pl.ds(CORE, BLK)] = jnp.where(lane, low_outer, from_right)

    for copy in verts:
        copy.wait_recv()
    down_above, right_above = vert_in[0, pl.ds(PART, 1), pl.ds(0, 1)], vert_in[0, pl.ds(PART, 1), pl.ds(BLK, 1)]
    right_below = vert_in[1, pl.ds(PART, 1), pl.ds(BLK, 1)]
    for n, (factor, beside) in enumerate(((down_above, right_above), (down_link, right_below))):
        edge = vert_in[n, pl.ds(0, PART), pl.ds(0, BLK)]
        margin[x, n, :, pl.ds(0, BLK)] = jnp.where(lane_part, corner_in[2 * n], edge) * factor
        margin[x, n, :, pl.ds(BLK, BLK)] = vert_in[n, pl.ds(0, PART), pl.ds(BLK, BLK)] * factor
        margin[x, n, :, pl.ds(CORE, BLK)] = jnp.where(lane_part, edge, corner_in[2 * n + 1] * beside) * factor
    shares = [
        remote(margin.at[x], margin.at[x], share_send.at[d - 1], share_recv.at[d - 1], peers[d])
        for d in range(1, 4)
    ]
    for copy in clears:
        copy.wait_recv()
    clear_sum[...] = clear_in[0] + clear_in[1] + clear_in[2] + clear_in[3]
    clear_copy = remote(clear_sum, clear_far, cfar_send, cfar_recv, far)
    response_cols(1, tab, mid, resp)
    response_cols(2, tab, mid, resp)
    spectrum_cols(ext, [(HALO, CORE)], tab, mid)
    for copy in shares:
        copy.wait_recv()
    for q in range(4):
        ext[pl.ds(PART * q, PART), :] = margin[q, 0]
        ext[pl.ds(HALO + CORE + PART * q, PART), :] = margin[q, 1]
    spectrum_cols(ext, [(0, HALO), (HALO + CORE, HALO)], tab, mid)
    spectrum_rows(tab, mid, spec)
    for pair in PAIRS:
        field_rows(pair, resp, spec, tab, wide)

    scatter = []
    for h in range(2):
        field_cols(h, tab, wide, field)
        for q in range(4):
            p = 0.0
            for k in range(3):
                block = pl.ds(k * BLK + q * EIGHTH, EIGHTH)
                f_re, f_im = field[h, 0, block, :], field[h, 1, block, :]
                p = p + weight[k] * (f_re * f_re + f_im * f_im)
            power[h, q] = p
        scatter.append([
            remote(power.at[h, x_at[d]], power_in.at[h, d - 1], psc_send.at[h, d - 1], psc_recv.at[h, d - 1], peers[d])
            for d in range(1, 4)
        ])
    loads[3].wait()
    clear_copy.wait_recv()
    swaps = []
    for h in range(2):
        for copy in scatter[h]:
            copy.wait_recv()
        power_mine[h] = power[h, x] + power_in[h, 0] + power_in[h, 1] + power_in[h, 2]
        swaps.append(remote(power_mine.at[h], power_far.at[h], pfar_send.at[h], pfar_recv.at[h], far))
    gathers = []
    for h in range(2):
        swaps[h].wait_recv()
        power_all[h, x] = power_mine[h] + power_far[h]
        gathers.append([
            remote(power_all.at[h, x], power_all.at[h, x], pall_send.at[h, d - 1], pall_recv.at[h, d - 1], peers[d])
            for d in range(1, 4)
        ])
    clear = (clear_sum[...] + clear_far[...])[0:1, 0:1]
    for h in range(2):
        for copy in gathers[h]:
            copy.wait_recv()
        total = jnp.concatenate([power_all[h, q] for q in range(4)], axis=0)
        printed = 1.0 / (1.0 + jnp.exp(-STEEP * (total / clear - THRESH)))
        block = pl.ds(h * BLK, BLK)
        resist[0, block, :] = printed
        wanted = target[0, block, :].astype(F32)
        slope = (4.0 * STEEP) * (printed - wanted) * printed * (1.0 - printed) / clear
        source_cols(h, slope, weight, tab, field, wide)
    store = pltpu.make_async_copy(resist, resist_out, store_sem.at[0])
    store.start()
    for pair in PAIRS:
        source_rows(pair, resp, tab, wide, acc)
    gradient_rows(acc, tab, mid)

    blocks = gradient_cols([(0, HALO), (HALO + CORE, HALO)], tab, mid)
    for c in range(3):
        for q, start in enumerate((64, 96, 32, 0)):
            halo_parts[q, :, pl.ds(c * BLK, BLK)] = blocks[c][start : start + 32]
    halo_scatter = [
        remote(halo_parts.at[x_at[d]], halo_in.at[d - 1], hsc_send.at[d - 1], hsc_recv.at[d - 1], peers[d])
        for d in range(1, 4)
    ]
    blocks = gradient_cols([(HALO, CORE)], tab, mid)
    for c in range(3):
        for q in range(4):
            core_parts[q, :, pl.ds(c * BLK, BLK)] = blocks[c][q * QUARTER : (q + 1) * QUARTER]
    core_scatter = [
        remote(core_parts.at[x_at[d]], core_in.at[d - 1], gsc_send.at[d - 1], gsc_recv.at[d - 1], peers[d])
        for d in range(1, 4)
    ]

    low_x = x < 2
    for copy in halo_scatter:
        copy.wait_recv()
    is_low = jnp.where(low_x, 1.0, 0.0)
    down_factor = is_low * down_link + (1.0 - is_low) * down_above
    right_factor = is_low * right_below + (1.0 - is_low) * right_above
    fold_out[...] = (halo_parts[x] + halo_in[0] + halo_in[1] + halo_in[2]) * down_factor
    bend_out[0] = fold_out[:, pl.ds(0, BLK)]
    bend_out[1] = fold_out[:, pl.ds(CORE, BLK)] * right_factor
    slot = jnp.where((x == 1) | (x == 2), 1, 0)
    step = jnp.where(low_x, GRID_W, -GRID_W)
    owner = jnp.where(low_x, 0, 6) + half
    folds = [
        remote(fold_out, fold_in.at[slot], fold_send, fold_recv.at[slot], at(step, owner)),
        remote(bend_out.at[0], bend_in.at[slot, 0], bend_send.at[0], bend_recv.at[slot, 0], at(step - 1, owner)),
        remote(bend_out.at[1], bend_in.at[slot, 1], bend_send.at[1], bend_recv.at[slot, 1], at(step + 1, owner)),
    ]

    for copy in core_scatter:
        copy.wait_recv()
    owned = core_parts[x] + core_in[0] + core_in[1] + core_in[2]
    edge_out[0] = owned[:, CORE:] * right_link
    edge_out[1] = owned[:, :BLK]
    edges = [
        remote(edge_out.at[0], edge_in.at[0], edge_send.at[0], edge_recv.at[0], right),
        remote(edge_out.at[1], edge_in.at[1], edge_send.at[1], edge_recv.at[1], left),
    ]
    core_parts[x] = owned

    @pl.when((x == 0) | (x == 3))
    def _():
        for s in range(2):
            waits = [
                (fold_out, fold_in.at[s], fold_send, fold_recv.at[s]),
                (bend_out.at[0], bend_in.at[s, 0], bend_send.at[0], bend_recv.at[s, 0]),
                (bend_out.at[1], bend_in.at[s, 1], bend_send.at[1], bend_recv.at[s, 1]),
            ]
            for src, dst, send, recv in waits:
                pltpu.make_async_remote_copy(
                    src_ref=src, dst_ref=dst, send_sem=send, recv_sem=recv, device_id=far, device_id_type=MESH
                ).wait_recv()
            block = pl.ds(32 * s, 32)
            core_parts[x, block, pl.ds(0, BLK)] += fold_in[s, :, pl.ds(0, BLK)] + bend_in[s, 1]
            core_parts[x, block, pl.ds(BLK, BLK)] += fold_in[s, :, pl.ds(BLK, BLK)]
            core_parts[x, block, pl.ds(CORE, BLK)] += fold_in[s, :, pl.ds(CORE, BLK)] + bend_in[s, 0] * right_link

    for copy in edges:
        copy.wait_recv()
    near_lane = lax.broadcasted_iota(jnp.int32, (QUARTER, BLK), 1) < HALO
    b0 = core_parts[x, :, pl.ds(0, BLK)] + edge_in[0]
    b1 = core_parts[x, :, pl.ds(BLK, BLK)]
    b2 = core_parts[x, :, pl.ds(CORE, BLK)] + edge_in[1] * right_link
    c0, c1, c2 = (pltpu.roll(b, HALO, 1) for b in (b0, b1, b2))
    whole = lanes(jnp.where(near_lane, c0, c1), jnp.where(near_lane, c1, c2))
    swaps = []
    for h in range(2):
        mine[h] = whole[h * 32 : (h + 1) * 32]
        swaps.append(remote(mine.at[h], other.at[h], gfar_send.at[h], gfar_recv.at[h], far))
    finals = []
    for h in range(2):
        swaps[h].wait_recv()
        gathered[x, h] = mine[h] + other[h]
        finals.append([
            remote(gathered.at[x, h], gathered.at[x, h], all_send.at[h, d - 1], all_recv.at[h, d - 1], peers[d])
            for d in range(1, 4)
        ])
    for h in range(2):
        for copy in finals[h]:
            copy.wait_recv()
    stores = []
    for q in range(4):
        for h in range(2):
            stores.append(
                pltpu.make_async_copy(
                    gathered.at[q, h], grad_out.at[0, pl.ds(64 * q + 32 * h, 32)], store_sem.at[1 + 2 * q + h]
                )
            )
            stores[-1].start()
    for copy in started:
        copy.wait_send()
    store.wait()
    for copy in stores:
        copy.wait()


def body(mask, kernels, weight, link, target):
    smem = pl.BlockSpec(memory_space=pltpu.SMEM)
    anywhere = pl.BlockSpec(memory_space=pl.ANY)
    dma = pltpu.SemaphoreType.DMA
    f32 = lambda *shape: pltpu.VMEM(shape, F32)
    buffers = [
        f32(1, CORE, CORE), f32(2, 3, BLK, BLK), pltpu.VMEM((1, CORE, CORE), jnp.int32),
        pltpu.VMEM((2, 2, 3, CORE, CORE), BF16),
        f32(2, EXTENT, EXTENT), f32(2, CORE, 3 * EXTENT), f32(2, EXTENT, 3 * EXTENT), f32(2, EXTENT, EXTENT),
        f32(2, 2, EXTENT, CORE), f32(2, EXTENT, EXTENT), f32(EXTENT, EXTENT), f32(1, CORE, CORE),
        f32(2, BLK, BLK), f32(2, BLK, BLK), f32(2, PART + 8, CORE), f32(2, PART + 8, CORE),
        f32(2, 2, PART, BLK), f32(4, PART, BLK), f32(4, 2, PART, EXTENT),
        f32(4, 8, BLK), f32(8, BLK), f32(8, BLK),
        f32(2, 4, EIGHTH, CORE), f32(2, 3, EIGHTH, CORE), f32(2, EIGHTH, CORE), f32(2, EIGHTH, CORE),
        f32(2, 4, EIGHTH, CORE),
        f32(4, 32, EXTENT), f32(3, 32, EXTENT), f32(4, QUARTER, EXTENT), f32(3, QUARTER, EXTENT),
        f32(32, EXTENT), f32(2, 32, EXTENT), f32(2, 32, BLK), f32(2, 2, 32, BLK),
        f32(2, QUARTER, BLK), f32(2, QUARTER, BLK),
        f32(2, 32, CORE), f32(2, 32, CORE), f32(4, 2, 32, CORE),
    ]
    sems = [dma((4,)), dma((9,))] + [dma((2,))] * 4 + [dma((4,))] * 2 + [dma((3,))] * 2
    sems += [dma((3,))] * 2 + [dma] * 2
    sems += [dma((2, 3))] * 2 + [dma((2,))] * 2 + [dma((2, 3))] * 2
    sems += [dma((3,))] * 4 + [dma, dma((2,)), dma((2,)), dma((2, 2))]
    sems += [dma((2,))] * 4 + [dma((2, 3))] * 2
    out = jax.ShapeDtypeStruct((1, CORE, CORE), F32)
    return pl.pallas_call(
        body_kernel,
        out_shape=(out, out),
        in_specs=[anywhere] * 4 + [smem] * 2,
        out_specs=(anywhere, anywhere),
        scratch_shapes=buffers + sems,
        compiler_params=pltpu.CompilerParams(
            collective_id=0, has_side_effects=True, vmem_limit_bytes=60 * 2**20
        ),
    )(mask, kernels, target, jnp.asarray(dft_tables()), weight, link)


def solution(mesh):
    in_specs = (
        P("tile", None, None),
        P(None, "kern", None, None),
        P("kern"),
        P("tile", None),
        P("tile", None, None),
    )
    out_specs = (P("tile", None, None), P("tile", None, None))
    return jax.shard_map(body, mesh=mesh, in_specs=in_specs, out_specs=out_specs, check_vma=False)
```

```python
import functools
import math

import jax
import jax.numpy as jnp
import ml_dtypes
import numpy as np
from jax import lax
from jax.experimental import pallas as pl
from jax.experimental.pallas import tpu as pltpu
from jax.sharding import PartitionSpec as P

GRID_W = 8
STEEP = 20.0
THRESH = 0.33
BLK = 128
EXTENT = 3 * BLK
CORE = 2 * BLK
HALO = BLK // 2
HALF_SQRT3 = math.sqrt(3.0) / 2.0
MESH = pl.DeviceIdType.MESH
F32 = jnp.float32
BF16 = jnp.bfloat16


def dft_tables():
    place = np.arange(BLK)
    groups = (3 * place, 3 * place + 1, -(3 * place + 1))
    mats = []
    for freq in groups:
        angle = 2.0 * np.pi * (np.outer(place, freq) % EXTENT) / EXTENT
        c, s = np.cos(angle), -np.sin(angle)
        mats.append(np.block([[c, s], [-s, c]]))
    fwd = np.stack(mats).astype(np.float32)
    both = np.stack([fwd, fwd.transpose(0, 2, 1)])
    high = both.astype(ml_dtypes.bfloat16)
    low = (both - high.astype(np.float32)).astype(ml_dtypes.bfloat16)
    return np.stack([high, low])


def split(x):
    high = x.astype(BF16)
    return high, (x - high.astype(F32)).astype(BF16)


def dot(a, b):
    return jnp.dot(a, b, preferred_element_type=F32)


def mul_right(x, high, low):
    xh, xl = split(x)
    return dot(xh, high) + (dot(xh, low) + dot(xl, high))


def mul_left(high, low, x):
    xh, xl = split(x)
    return dot(high, xh) + (dot(low, xh) + dot(high, xl))


def fwd_mat(tab, g):
    return tab[0, 0, g], tab[1, 0, g]


def t_mat(tab, g):
    return tab[0, 1, g], tab[1, 1, g]


def lanes(re, im):
    return jnp.concatenate([re, im], axis=1)


def rows(re, im):
    return jnp.concatenate([re, im], axis=0)


def response_rows(kernels, tab, mid):
    scale = 1.0 / (EXTENT * EXTENT)
    re = jnp.concatenate([kernels[0, k] for k in range(3)], axis=1) * scale
    im = jnp.concatenate([kernels[1, k] for k in range(3)], axis=1) * -scale
    taps = rows(re, im)
    for g in range(3):
        out = mul_left(*t_mat(tab, g), taps)
        mid[0, pl.ds(g * BLK, BLK), :] = out[:BLK]
        mid[1, pl.ds(g * BLK, BLK), :] = out[BLK:]


def response_cols(k, tab, mid, resp):
    cols = pl.ds(k * BLK, BLK)
    x = lanes(mid[0, :, cols], mid[1, :, cols])
    for g in range(3):
        out = mul_right(x, *fwd_mat(tab, g))
        resp[0, :, pl.ds(k * EXTENT + g * BLK, BLK)] = out[:, :BLK]
        resp[1, :, pl.ds(k * EXTENT + g * BLK, BLK)] = out[:, BLK:]


def spectrum_cols(ext, places, tab, mid):
    x0, x1, x2 = (
        jnp.concatenate([ext[pl.ds(s, n), pl.ds(j * BLK, BLK)] for s, n in places], axis=0) for j in range(3)
    )
    z0 = x0 + x1 + x2
    z1 = lanes(x0 - 0.5 * (x1 + x2), HALF_SQRT3 * (x2 - x1))
    h0, l0 = fwd_mat(tab, 0)
    outs = (mul_right(z0, h0[:BLK], l0[:BLK]), mul_right(z1, *fwd_mat(tab, 1)))
    for g, out in enumerate(outs):
        at = 0
        for s, n in places:
            mid[0, pl.ds(s, n), pl.ds(g * BLK, BLK)] = out[at : at + n, :BLK]
            mid[1, pl.ds(s, n), pl.ds(g * BLK, BLK)] = out[at : at + n, BLK:]
            at += n


def spectrum_rows(tab, mid, spec):
    two = pl.ds(0, CORE)
    a_re, b_re, c_re = (mid[0, pl.ds(j * BLK, BLK), two] for j in range(3))
    a_im, b_im, c_im = (mid[1, pl.ds(j * BLK, BLK), two] for j in range(3))
    s_re, s_im = b_re + c_re, b_im + c_im
    e_re, e_im = a_re - 0.5 * s_re, a_im - 0.5 * s_im
    f_re, f_im = HALF_SQRT3 * (b_re - c_re), HALF_SQRT3 * (b_im - c_im)
    z_re, z_im = a_re + s_re, a_im + s_im
    z_re = lanes(z_re, z_re[:, BLK:])
    z_im = lanes(z_im, -z_im[:, BLK:])
    out = mul_left(*t_mat(tab, 0), rows(z_re, z_im))
    spec[0, pl.ds(0, BLK), :] = out[:BLK]
    spec[1, pl.ds(0, BLK), :] = out[BLK:]
    out1 = mul_left(*t_mat(tab, 1), rows(e_re + f_im, e_im - f_re))
    out2 = mul_left(*t_mat(tab, 2), rows(e_re - f_im, e_im + f_re))
    spec[0, pl.ds(BLK, BLK), :] = lanes(out1[:BLK], out2[:BLK, BLK:])
    spec[1, pl.ds(BLK, BLK), :] = lanes(out1[BLK:], -out2[BLK:, BLK:])
    spec[0, pl.ds(2 * BLK, BLK), :] = lanes(out2[:BLK], out1[:BLK, BLK:])
    spec[1, pl.ds(2 * BLK, BLK), :] = lanes(out2[BLK:], -out1[BLK:, BLK:])


PAIRS = [[(b // 3, b % 3) for b in range(s, min(s + 2, 9))] for s in range(0, 9, 2)]


def field_rows(pair, resp, spec, tab, mid):
    width = len(pair) * BLK
    start = (pair[0][0] * 3 + pair[0][1]) * BLK
    cols = pl.ds(start, width)
    t = []
    for g in range(3):
        block = pl.ds(g * BLK, BLK)
        q_re, q_im = resp[0, block, cols], resp[1, block, cols]
        e_re = jnp.concatenate([spec[0, block, pl.ds(f * BLK, BLK)] for _, f in pair], axis=1)
        e_im = jnp.concatenate([spec[1, block, pl.ds(f * BLK, BLK)] for _, f in pair], axis=1)
        x = rows(e_re * q_re + e_im * q_im, e_im * q_re - e_re * q_im)
        t.append(mul_left(*fwd_mat(tab, g), x))
    s, d = t[1] + t[2], HALF_SQRT3 * (t[1] - t[2])
    first, e = t[0] + s, t[0] - 0.5 * s
    upper, lower = pl.ds(0, BLK), pl.ds(BLK, BLK)
    mid[0, upper, cols] = first[:BLK]
    mid[1, upper, cols] = first[BLK:]
    mid[0, lower, cols] = e[:BLK] - d[BLK:]
    mid[1, lower, cols] = e[BLK:] + d[:BLK]


def field_cols(h, tab, mid, field):
    t = []
    for g in range(3):
        x = jnp.concatenate(
            [
                lanes(*(mid[c, pl.ds(h * BLK, BLK), pl.ds(k * EXTENT + g * BLK, BLK)] for c in range(2)))
                for k in range(3)
            ],
            axis=0,
        )
        t.append(mul_right(x, *t_mat(tab, g)))
    s, d = t[1] + t[2], HALF_SQRT3 * (t[1] - t[2])
    first, e = t[0] + s, t[0] - 0.5 * s
    field[h, 0] = lanes(first[:, :BLK], e[:, :BLK] - d[:, BLK:])
    field[h, 1] = lanes(first[:, BLK:], e[:, BLK:] + d[:, :BLK])


def source_cols(h, slope, weight, tab, field, mid):
    scaled = jnp.concatenate([weight[k] * slope for k in range(3)], axis=0)
    s_re, s_im = scaled * field[h, 0], scaled * field[h, 1]
    a_re, a_im, b_re, b_im = s_re[:, :BLK], s_im[:, :BLK], s_re[:, BLK:], s_im[:, BLK:]
    e_re, e_im = a_re - 0.5 * b_re, a_im - 0.5 * b_im
    f_re, f_im = HALF_SQRT3 * b_re, HALF_SQRT3 * b_im
    z = (
        lanes(a_re + b_re, a_im + b_im),
        lanes(e_re + f_im, e_im - f_re),
        lanes(e_re - f_im, e_im + f_re),
    )
    for g in range(3):
        out = mul_right(z[g], *fwd_mat(tab, g))
        for k in range(3):
            cols = pl.ds(k * EXTENT + g * BLK, BLK)
            mid[0, pl.ds(h * BLK, BLK), cols] = out[k * BLK : (k + 1) * BLK, :BLK]
            mid[1, pl.ds(h * BLK, BLK), cols] = out[k * BLK : (k + 1) * BLK, BLK:]


def source_rows(pair, resp, tab, mid, acc):
    width = len(pair) * BLK
    start = (pair[0][0] * 3 + pair[0][1]) * BLK
    cols = pl.ds(start, width)
    upper, lower = pl.ds(0, BLK), pl.ds(BLK, BLK)
    a_re, a_im, b_re, b_im = mid[0, upper, cols], mid[1, upper, cols], mid[0, lower, cols], mid[1, lower, cols]
    e_re, e_im = a_re - 0.5 * b_re, a_im - 0.5 * b_im
    f_re, f_im = HALF_SQRT3 * b_re, HALF_SQRT3 * b_im
    z = (
        rows(a_re + b_re, a_im + b_im),
        rows(e_re + f_im, e_im - f_re),
        rows(e_re - f_im, e_im + f_re),
    )
    for g in range(3):
        out = mul_left(*t_mat(tab, g), z[g])
        block = pl.ds(g * BLK, BLK)
        o_re, o_im = out[:BLK], out[BLK:]
        q_re, q_im = resp[0, block, cols], resp[1, block, cols]
        p_re, p_im = o_re * q_re - o_im * q_im, o_re * q_im + o_im * q_re
        for n, (k, f) in enumerate(pair):
            into = pl.ds(f * BLK, BLK)
            part = slice(n * BLK, (n + 1) * BLK)
            if k == 0:
                acc[0, block, into] = p_re[:, part]
                acc[1, block, into] = p_im[:, part]
            else:
                acc[0, block, into] += p_re[:, part]
                acc[1, block, into] += p_im[:, part]


def gradient_rows(acc, tab, mid):
    p0, p1, p2 = (pl.ds(g * BLK, BLK) for g in range(3))
    t0 = mul_left(*fwd_mat(tab, 0), rows(acc[0, p0, :], acc[1, p0, :]))
    t0_re, t0_im = t0[:BLK], t0[BLK:]
    t0_re = lanes(t0_re[:, :BLK], t0_re[:, BLK:CORE] + t0_re[:, CORE:])
    t0_im = lanes(t0_im[:, :BLK], t0_im[:, BLK:CORE] - t0_im[:, CORE:])
    x_re = lanes(acc[0, p1, p0], acc[0, p1, p1] + acc[0, p2, p2])
    x_im = lanes(acc[1, p1, p0], acc[1, p1, p1] - acc[1, p2, p2])
    t1 = mul_left(*fwd_mat(tab, 1), rows(x_re, x_im))
    x_re = lanes(acc[0, p2, p0], acc[0, p2, p1] + acc[0, p1, p2])
    x_im = lanes(acc[1, p2, p0], acc[1, p2, p1] - acc[1, p1, p2])
    t2 = mul_left(*fwd_mat(tab, 2), rows(x_re, x_im))
    s, d = t1 + t2, HALF_SQRT3 * (t1 - t2)
    e_re, e_im = t0_re - 0.5 * s[:BLK], t0_im - 0.5 * s[BLK:]
    two = pl.ds(0, CORE)
    mid[0, p0, two], mid[1, p0, two] = t0_re + s[:BLK], t0_im + s[BLK:]
    mid[0, p1, two], mid[1, p1, two] = e_re - d[BLK:], e_im + d[:BLK]
    mid[0, p2, two], mid[1, p2, two] = e_re + d[BLK:], e_im - d[:BLK]


def gradient_cols(places, tab, mid):
    h0, l0 = t_mat(tab, 0)
    part = lambda c, g: jnp.concatenate([mid[c, pl.ds(s, n), pl.ds(g * BLK, BLK)] for s, n in places], axis=0)
    r0 = mul_right(lanes(part(0, 0), part(1, 0)), h0[:, :BLK], l0[:, :BLK])
    r1 = mul_right(lanes(part(0, 1), part(1, 1)), *t_mat(tab, 1))
    e, d = r0 - 0.5 * r1[:, :BLK], HALF_SQRT3 * r1[:, BLK:]
    return r0 + r1[:, :BLK], e - d, e + d


QUARTER = CORE // 4
EIGHTH = CORE // 8
PART = HALO // 4


def low_lanes(n):
    return lax.broadcasted_iota(jnp.int32, (n, BLK), 1) < HALO


def pack_low(x):
    n = x.shape[0] // 2
    return jnp.where(low_lanes(n), x[:n], pltpu.roll(x[n:], HALO, 1))


def pack_high(x):
    n = x.shape[0] // 2
    return jnp.where(low_lanes(n), pltpu.roll(x[:n], HALO, 1), x[n:])


def unpack_low(x):
    return rows(x, pltpu.roll(x, HALO, 1))


def unpack_high(x):
    return rows(pltpu.roll(x, HALO, 1), x)


def core_blocks(x):
    c0, c1, c2 = (pltpu.roll(x[:, j * BLK : (j + 1) * BLK], HALO, 1) for j in range(3))
    low = low_lanes(x.shape[0])
    return c0, c2, lanes(jnp.where(low, c0, c1), jnp.where(low, c1, c2))


def body_kernel(
    mask_hbm, kernels_hbm, target_hbm, tab_hbm, weight_hbm, link_hbm, out,
    mask, kernels, target, tab, mid, wide, resp, spec, field, acc, ext, resist,
    side_out, side_in, vert_out, vert_in, corner_out, corner_in, margin,
    clear_in, clear_sum, clear_far, power, power_in, power_mine, power_far, power_all,
    halo_parts, halo_in, core_parts, core_in, fold_out, fold_in, bend_out, bend_in, edge_out, edge_in, whole,
    mine, other, gathered,
    weight, link, load_sem, store_sem, side_send, side_recv, vert_send, vert_recv, corner_send, corner_recv, share_send, share_recv,
    clear_send, clear_recv, cfar_send, cfar_recv,
    psc_send, psc_recv, pfar_send, pfar_recv, pall_send, pall_recv,
    hsc_send, hsc_recv, gsc_send, gsc_recv, fold_send, fold_recv, bend_send, bend_recv,
    edge_send, edge_recv, gfar_send, gfar_recv, all_send, all_recv,
):
    tile = lax.axis_index("tile")
    kern = lax.axis_index("kern")
    tiles = lax.axis_size("tile")
    x = kern // 2
    half = kern % 2
    column = (tile + GRID_W // 2) % GRID_W
    right_ok = jnp.where((column < GRID_W - 1) & (tile + 1 < tiles), 1.0, 0.0)
    down_ok = jnp.where(tile + GRID_W < tiles, 1.0, 0.0)

    def valid(tile_by):
        return (tile + tile_by >= 0) & (tile + tile_by < tiles)

    def at(tile_by, kern_index):
        return {"tile": (tile + tile_by + tiles) % tiles, "kern": kern_index}

    far = at(0, 2 * x + 1 - half)
    x_at = [(x + d) % 4 for d in range(4)]
    peers = [at(0, 2 * x_at[d] + half) for d in range(4)]
    sign = 2 * (x % 2) - 1
    crossed = 2 * (x + 1 - 2 * (x % 2)) + half
    near_tiles = [1, -1] + [s * GRID_W + e for s in (1, -1) for e in (-1, 0, 1)]
    partners = [(valid(by), at(by, kern)) for by in near_tiles]
    partners += [(valid(by), at(by, crossed)) for by in (sign * GRID_W + e for e in (-1, 0, 1))]

    barrier = pltpu.get_barrier_semaphore()
    expected = 4
    for there, one in partners:
        expected = expected + there.astype(jnp.int32)

        @pl.when(there)
        def _():
            pl.semaphore_signal(barrier, inc=1, device_id=one, device_id_type=MESH)

    for one in [far] + peers[1:]:
        pl.semaphore_signal(barrier, inc=1, device_id=one, device_id_type=MESH)

    loads = [
        pltpu.make_async_copy(src, dst, load_sem.at[n])
        for n, (src, dst) in enumerate((
            (mask_hbm, mask), (kernels_hbm, kernels), (tab_hbm, tab), (target_hbm, target),
            (link_hbm, link), (weight_hbm, weight),
        ))
    ]
    for copy in (loads[0], loads[4], loads[5], loads[1], loads[2], loads[3]):
        copy.start()
    started = []

    def remote(src, dst, send, recv, device, there=None):
        copy = pltpu.make_async_remote_copy(
            src_ref=src, dst_ref=dst, send_sem=send, recv_sem=recv, device_id=device, device_id_type=MESH
        )
        if there is None:
            copy.start()
        else:
            pl.when(there)(copy.start)
        started.append((there, copy))
        return copy

    def clear_unless(there, *refs):
        @pl.when(jnp.logical_not(there))
        def _():
            for ref in refs:
                ref[...] = jnp.zeros(ref.shape, F32)

    from_left_tile, from_right_tile = valid(-1), valid(1)
    from_vert = [valid(-GRID_W), valid(GRID_W)]
    from_corner = [valid(-GRID_W - 1), valid(-GRID_W + 1), valid(GRID_W - 1), valid(GRID_W + 1)]
    clear_unless(from_left_tile, side_in.at[0], edge_in.at[0])
    clear_unless(from_right_tile, side_in.at[1], edge_in.at[1])
    for n in range(2):
        clear_unless(from_vert[n], vert_in.at[n])
    for n in range(4):
        clear_unless(from_corner[n], corner_in.at[n])

    loads[0].wait()
    a0, a1 = mask[0, :, pl.ds(0, BLK)], mask[0, :, pl.ds(BLK, BLK)]
    r0, r1 = pltpu.roll(a0, HALO, 1), pltpu.roll(a1, HALO, 1)
    lane_all = low_lanes(CORE)
    outer = jnp.where(lane_all, r1, r0)
    inner = jnp.where(lane_all, r0, r1)
    middle = pl.ds(HALO, CORE)
    ext[middle, pl.ds(BLK, BLK)] = inner
    ext[middle, pl.ds(0, BLK)] = outer
    loads[4].wait()
    right_link = link[0, 0].astype(F32) * right_ok
    down_link = link[0, 1].astype(F32) * down_ok
    flag = lax.broadcasted_iota(jnp.int32, (8, BLK), 0) < 1
    for n, first in enumerate((CORE - HALO, 0)):
        block = pl.ds(pl.multiple_of(HALO + first + PART * x, PART), PART)
        outer_part = ext[block, pl.ds(0, BLK)]
        vert_out[n, pl.ds(0, PART), :] = outer_part
        vert_out[n, pl.ds(PART, PART), :] = ext[block, pl.ds(BLK, BLK)]
        vert_out[n, pl.ds(2 * PART, 8), :] = jnp.where(flag, down_link, right_link)
        corner_out[n, 0] = pack_high(outer_part)
        corner_out[n, 1] = pack_low(outer_part) * right_link
    side_out[0] = pack_low(outer) * right_link
    side_out[1] = pack_high(outer)

    pl.semaphore_wait(barrier, expected)
    w = GRID_W
    verts = [
        remote(vert_out.at[0], vert_in.at[0], vert_send.at[0], vert_recv.at[0], at(w, kern), valid(w)),
        remote(vert_out.at[1], vert_in.at[1], vert_send.at[1], vert_recv.at[1], at(-w, kern), valid(-w)),
    ]
    for n, (by, src) in enumerate((
        (w + 1, corner_out.at[0, 1]), (w - 1, corner_out.at[0, 0]),
        (1 - w, corner_out.at[1, 1]), (-1 - w, corner_out.at[1, 0]),
    )):
        verts.append(remote(src, corner_in.at[n], corner_send.at[n], corner_recv.at[n], at(by, kern), valid(by)))
    sides = [
        remote(side_out.at[0], side_in.at[0], side_send.at[0], side_recv.at[0], at(1, kern), valid(1)),
        remote(side_out.at[1], side_in.at[1], side_send.at[1], side_recv.at[1], at(-1, kern), valid(-1)),
    ]

    loads[1].wait()
    loads[5].wait()
    taps = [[jnp.sum(kernels[c, k], keepdims=True) for k in range(3)] for c in range(2)]
    clear_part = sum(weight[k] * (taps[0][k] * taps[0][k] + taps[1][k] * taps[1][k]) for k in range(3))
    clear_in[x] = jnp.broadcast_to(clear_part, (8, BLK))
    clears = [
        remote(clear_in.at[x], clear_in.at[x], clear_send.at[d - 1], clear_recv.at[d - 1], peers[d])
        for d in range(1, 4)
    ]
    loads[2].wait()
    response_rows(kernels, tab, mid)
    response_cols(0, tab, mid, resp)

    for there, copy in zip((from_left_tile, from_right_tile), sides):
        pl.when(there)(copy.wait_recv)
    from_left, from_right = unpack_low(side_in[0]), unpack_high(side_in[1]) * right_link
    outer = ext[middle, pl.ds(0, BLK)]
    ext[middle, pl.ds(0, BLK)] = jnp.where(lane_all, from_left, outer)
    ext[middle, pl.ds(CORE, BLK)] = jnp.where(lane_all, outer, from_right)

    for there, copy in zip(from_vert + from_corner, verts):
        pl.when(there)(copy.wait_recv)
    down_above, right_above = (vert_in[0, pl.ds(2 * PART + r, 1), pl.ds(0, 1)] for r in (0, 1))
    right_below = vert_in[1, pl.ds(2 * PART + 1, 1), pl.ds(0, 1)]
    lane_part = low_lanes(PART)
    for n, (factor, beside) in enumerate(((down_above, right_above), (down_link, right_below))):
        edge = vert_in[n, pl.ds(0, PART), :]
        first, last = unpack_low(corner_in[2 * n]), unpack_high(corner_in[2 * n + 1])
        margin[x, n, :, pl.ds(0, BLK)] = jnp.where(lane_part, first, edge) * factor
        margin[x, n, :, pl.ds(BLK, BLK)] = vert_in[n, pl.ds(PART, PART), :] * factor
        margin[x, n, :, pl.ds(CORE, BLK)] = jnp.where(lane_part, edge, last * beside) * factor
    shares = [
        remote(margin.at[x], margin.at[x], share_send.at[d - 1], share_recv.at[d - 1], peers[d])
        for d in range(1, 4)
    ]
    for copy in clears:
        copy.wait_recv()
    clear_sum[...] = clear_in[0] + clear_in[1] + clear_in[2] + clear_in[3]
    clear_copy = remote(clear_sum, clear_far, cfar_send, cfar_recv, far)
    response_cols(1, tab, mid, resp)
    response_cols(2, tab, mid, resp)
    spectrum_cols(ext, [(HALO, CORE)], tab, mid)
    for copy in shares:
        copy.wait_recv()
    for q in range(4):
        ext[pl.ds(PART * q, PART), :] = margin[q, 0]
        ext[pl.ds(HALO + CORE + PART * q, PART), :] = margin[q, 1]
    spectrum_cols(ext, [(0, HALO), (HALO + CORE, HALO)], tab, mid)
    spectrum_rows(tab, mid, spec)
    for pair in PAIRS:
        field_rows(pair, resp, spec, tab, wide)

    scatter = []
    for h in range(2):
        field_cols(h, tab, wide, field)
        for q in range(4):
            p = 0.0
            for k in range(3):
                block = pl.ds(k * BLK + q * EIGHTH, EIGHTH)
                f_re, f_im = field[h, 0, block, :], field[h, 1, block, :]
                p = p + weight[k] * (f_re * f_re + f_im * f_im)
            power[h, q] = p
        scatter.append([
            remote(power.at[h, x_at[d]], power_in.at[h, d - 1], psc_send.at[h, d - 1], psc_recv.at[h, d - 1], peers[d])
            for d in range(1, 4)
        ])
    loads[3].wait()
    clear_copy.wait_recv()
    swaps = []
    for h in range(2):
        for copy in scatter[h]:
            copy.wait_recv()
        power_mine[h] = power[h, x] + power_in[h, 0] + power_in[h, 1] + power_in[h, 2]
        swaps.append(remote(power_mine.at[h], power_far.at[h], pfar_send.at[h], pfar_recv.at[h], far))
    gathers = []
    for h in range(2):
        swaps[h].wait_recv()
        power_all[h, x] = power_mine[h] + power_far[h]
        gathers.append([
            remote(power_all.at[h, x], power_all.at[h, x], pall_send.at[h, d - 1], pall_recv.at[h, d - 1], peers[d])
            for d in range(1, 4)
        ])
    clear = (clear_sum[...] + clear_far[...])[0:1, 0:1]
    for h in range(2):
        for copy in gathers[h]:
            copy.wait_recv()
        total = jnp.concatenate([power_all[h, q] for q in range(4)], axis=0)
        printed = 1.0 / (1.0 + jnp.exp(-STEEP * (total / clear - THRESH)))
        block = pl.ds(h * BLK, BLK)
        resist[0, block, :] = printed
        wanted = target[0, block, :].astype(F32)
        slope = (4.0 * STEEP) * (printed - wanted) * printed * (1.0 - printed) / clear
        source_cols(h, slope, weight, tab, field, wide)
    store = pltpu.make_async_copy(resist, out.at[0], store_sem.at[0])
    store.start()
    for pair in PAIRS:
        source_rows(pair, resp, tab, wide, acc)
    gradient_rows(acc, tab, mid)

    blocks = gradient_cols([(0, HALO), (HALO + CORE, HALO)], tab, mid)
    for c in range(3):
        for q, start in enumerate((64, 96, 32, 0)):
            halo_parts[q, :, pl.ds(c * BLK, BLK)] = blocks[c][start : start + 32]
    halo_scatter = [
        remote(halo_parts.at[x_at[d]], halo_in.at[d - 1], hsc_send.at[d - 1], hsc_recv.at[d - 1], peers[d])
        for d in range(1, 4)
    ]
    blocks = gradient_cols([(HALO, CORE)], tab, mid)
    for c in range(3):
        for q in range(4):
            core_parts[q, :, pl.ds(c * BLK, BLK)] = blocks[c][q * QUARTER : (q + 1) * QUARTER]
    core_scatter = [
        remote(core_parts.at[x_at[d]], core_in.at[d - 1], gsc_send.at[d - 1], gsc_recv.at[d - 1], peers[d])
        for d in range(1, 4)
    ]

    low_x = x < 2
    for copy in halo_scatter:
        copy.wait_recv()
    is_low = jnp.where(low_x, 1.0, 0.0)
    down_factor = is_low * down_link + (1.0 - is_low) * down_above
    right_factor = is_low * right_below + (1.0 - is_low) * right_above
    total = (halo_parts[x] + halo_in[0] + halo_in[1] + halo_in[2]) * down_factor
    first, last, fold_out[...] = core_blocks(total)
    bend_out[0] = pack_high(first)
    bend_out[1] = pack_low(last) * right_factor
    slot = jnp.where((x == 1) | (x == 2), 1, 0)
    step = jnp.where(low_x, GRID_W, -GRID_W)
    owner = jnp.where(low_x, 0, 6) + half
    remote(fold_out, fold_in.at[slot], fold_send, fold_recv.at[slot], at(step, owner), valid(step))
    for n, by in enumerate((step - 1, step + 1)):
        remote(
            bend_out.at[n], bend_in.at[slot, n], bend_send.at[n], bend_recv.at[slot, n], at(by, owner), valid(by)
        )

    for copy in core_scatter:
        copy.wait_recv()
    first, last, whole[...] = core_blocks(core_parts[x] + core_in[0] + core_in[1] + core_in[2])
    edge_out[0] = pack_low(last) * right_link
    edge_out[1] = pack_high(first)
    edges = [
        remote(edge_out.at[0], edge_in.at[0], edge_send.at[0], edge_recv.at[0], at(1, kern), valid(1)),
        remote(edge_out.at[1], edge_in.at[1], edge_send.at[1], edge_recv.at[1], at(-1, kern), valid(-1)),
    ]

    takes = (x == 0) | (x == 3)
    back = jnp.where(x == 0, -GRID_W, GRID_W)
    lane_fold = low_lanes(32)
    for s in range(2):
        arrivals = (
            (valid(back), fold_out, fold_in.at[s], fold_send, fold_recv.at[s]),
            (valid(back + 1), bend_out.at[0], bend_in.at[s, 0], bend_send.at[0], bend_recv.at[s, 0]),
            (valid(back - 1), bend_out.at[1], bend_in.at[s, 1], bend_send.at[1], bend_recv.at[s, 1]),
        )
        for there, src, dst, send, recv in arrivals:
            copy = pltpu.make_async_remote_copy(
                src_ref=src, dst_ref=dst, send_sem=send, recv_sem=recv, device_id=far, device_id_type=MESH
            )
            clear_unless(takes & there, dst)
            pl.when(takes & there)(copy.wait_recv)
        block = pl.ds(32 * s, 32)
        from_left = jnp.where(lane_fold, unpack_low(bend_in[s, 1]), 0.0)
        from_right = jnp.where(lane_fold, 0.0, unpack_high(bend_in[s, 0])) * right_link
        whole[block, :] += fold_in[s] + lanes(from_left, from_right)

    for there, copy in zip((from_left_tile, from_right_tile), edges):
        pl.when(there)(copy.wait_recv)
    lane_edge = low_lanes(QUARTER)
    from_left = jnp.where(lane_edge, unpack_low(edge_in[0]), 0.0)
    from_right = jnp.where(lane_edge, 0.0, unpack_high(edge_in[1])) * right_link
    partial = whole[...] + lanes(from_left, from_right)
    swaps = []
    for h in range(2):
        mine[h] = partial[h * 32 : (h + 1) * 32]
        swaps.append(remote(mine.at[h], other.at[h], gfar_send.at[h], gfar_recv.at[h], far))
    finals = []
    for h in range(2):
        swaps[h].wait_recv()
        gathered[x, h] = mine[h] + other[h]
        finals.append([
            remote(gathered.at[x, h], gathered.at[x, h], all_send.at[h, d - 1], all_recv.at[h, d - 1], peers[d])
            for d in range(1, 4)
        ])
    for h in range(2):
        for copy in finals[h]:
            copy.wait_recv()
    stores = []
    for q in range(4):
        for h in range(2):
            stores.append(
                pltpu.make_async_copy(
                    gathered.at[q, h], out.at[1, 0, pl.ds(64 * q + 32 * h, 32)], store_sem.at[1 + 2 * q + h]
                )
            )
            stores[-1].start()
    for there, copy in started:
        if there is None:
            copy.wait_send()
        else:
            pl.when(there)(copy.wait_send)
    store.wait()
    for copy in stores:
        copy.wait()


def body(mask, kernels, weight, link, target):
    anywhere = pl.BlockSpec(memory_space=pl.ANY)
    dma = pltpu.SemaphoreType.DMA
    f32 = lambda *shape: pltpu.VMEM(shape, F32)
    buffers = [
        f32(1, CORE, CORE), f32(2, 3, BLK, BLK), pltpu.VMEM((1, CORE, CORE), jnp.int32),
        pltpu.VMEM((2, 2, 3, CORE, CORE), BF16),
        f32(2, EXTENT, EXTENT), f32(2, CORE, 3 * EXTENT), f32(2, EXTENT, 3 * EXTENT), f32(2, EXTENT, EXTENT),
        f32(2, 2, EXTENT, CORE), f32(2, EXTENT, EXTENT), f32(EXTENT, EXTENT), f32(1, CORE, CORE),
        f32(2, BLK, BLK), f32(2, BLK, BLK), f32(2, 2 * PART + 8, BLK), f32(2, 2 * PART + 8, BLK),
        f32(2, 2, PART // 2, BLK), f32(4, PART // 2, BLK), f32(4, 2, PART, EXTENT),
        f32(4, 8, BLK), f32(8, BLK), f32(8, BLK),
        f32(2, 4, EIGHTH, CORE), f32(2, 3, EIGHTH, CORE), f32(2, EIGHTH, CORE), f32(2, EIGHTH, CORE),
        f32(2, 4, EIGHTH, CORE),
        f32(4, 32, EXTENT), f32(3, 32, EXTENT), f32(4, QUARTER, EXTENT), f32(3, QUARTER, EXTENT),
        f32(32, CORE), f32(2, 32, CORE), f32(2, 16, BLK), f32(2, 2, 16, BLK),
        f32(2, 32, BLK), f32(2, 32, BLK), f32(QUARTER, CORE),
        f32(2, 32, CORE), f32(2, 32, CORE), f32(4, 2, 32, CORE),
    ]
    sems = [pltpu.SMEM((3,), F32), pltpu.SMEM((1, 2), jnp.int32), dma((6,)), dma((9,))] + [dma((2,))] * 4 + [dma((4,))] * 2 + [dma((3,))] * 2
    sems += [dma((3,))] * 2 + [dma] * 2
    sems += [dma((2, 3))] * 2 + [dma((2,))] * 2 + [dma((2, 3))] * 2
    sems += [dma((3,))] * 4 + [dma, dma((2,)), dma((2,)), dma((2, 2))]
    sems += [dma((2,))] * 4 + [dma((2, 3))] * 2
    both = pl.pallas_call(
        body_kernel,
        out_shape=jax.ShapeDtypeStruct((2, 1, CORE, CORE), F32),
        in_specs=[anywhere] * 6,
        out_specs=anywhere,
        scratch_shapes=buffers + sems,
        compiler_params=pltpu.CompilerParams(
            collective_id=0, has_side_effects=True, vmem_limit_bytes=60 * 2**20
        ),
    )(mask, kernels, target, jnp.asarray(dft_tables()), weight, link)
    return both[0], both[1]


def solution(mesh):
    in_specs = (
        P("tile", None, None),
        P(None, "kern", None, None),
        P("kern"),
        P("tile", None),
        P("tile", None, None),
    )
    out_specs = (P("tile", None, None), P("tile", None, None))
    return jax.shard_map(body, mesh=mesh, in_specs=in_specs, out_specs=out_specs, check_vma=False)
```

```python
import functools
import math

import jax
import jax.numpy as jnp
import ml_dtypes
import numpy as np
from jax import lax
from jax.experimental import pallas as pl
from jax.experimental.pallas import tpu as pltpu
from jax.sharding import PartitionSpec as P

GRID_W = 8
STEEP = 20.0
THRESH = 0.33
BLK = 128
EXTENT = 3 * BLK
CORE = 2 * BLK
HALO = BLK // 2
HALF_SQRT3 = math.sqrt(3.0) / 2.0
MESH = pl.DeviceIdType.MESH
F32 = jnp.float32
BF16 = jnp.bfloat16


def dft_tables():
    place = np.arange(BLK)
    groups = (3 * place, 3 * place + 1, -(3 * place + 1))
    mats = []
    for freq in groups:
        angle = 2.0 * np.pi * (np.outer(place, freq) % EXTENT) / EXTENT
        c, s = np.cos(angle), -np.sin(angle)
        mats.append(np.block([[c, s], [-s, c]]))
    fwd = np.stack(mats).astype(np.float32)
    both = np.stack([fwd, fwd.transpose(0, 2, 1)])
    high = both.astype(ml_dtypes.bfloat16)
    low = (both - high.astype(np.float32)).astype(ml_dtypes.bfloat16)
    return np.stack([high, low])


def split(x):
    high = x.astype(BF16)
    return high, (x - high.astype(F32)).astype(BF16)


def dot(a, b):
    return jnp.dot(a, b, preferred_element_type=F32)


def mul_right(x, high, low):
    xh, xl = split(x)
    return dot(xh, high) + (dot(xh, low) + dot(xl, high))


def mul_left(high, low, x):
    xh, xl = split(x)
    n = x.shape[1]
    both = dot(high, jnp.concatenate([xh, xl], axis=1))
    return both[:, :n] + (both[:, n:] + dot(low, xh))


def fwd_mat(tab, g):
    return tab[0, 0, g], tab[1, 0, g]


def t_mat(tab, g):
    return tab[0, 1, g], tab[1, 1, g]


def lanes(re, im):
    return jnp.concatenate([re, im], axis=1)


def rows(re, im):
    return jnp.concatenate([re, im], axis=0)


def response_rows(kernels, tab, mid):
    scale = 1.0 / (EXTENT * EXTENT)
    re = jnp.concatenate([kernels[0, k] for k in range(3)], axis=1) * scale
    im = jnp.concatenate([kernels[1, k] for k in range(3)], axis=1) * -scale
    taps = rows(re, im)
    for g in range(3):
        out = mul_left(*t_mat(tab, g), taps)
        mid[0, pl.ds(g * BLK, BLK), :] = out[:BLK]
        mid[1, pl.ds(g * BLK, BLK), :] = out[BLK:]


def response_cols(k, tab, mid, resp):
    cols = pl.ds(k * BLK, BLK)
    x = lanes(mid[0, :, cols], mid[1, :, cols])
    for g in range(3):
        out = mul_right(x, *fwd_mat(tab, g))
        resp[0, :, pl.ds(k * EXTENT + g * BLK, BLK)] = out[:, :BLK]
        resp[1, :, pl.ds(k * EXTENT + g * BLK, BLK)] = out[:, BLK:]


def spectrum_cols(ext, places, tab, mid):
    x0, x1, x2 = (
        jnp.concatenate([ext[pl.ds(s, n), pl.ds(j * BLK, BLK)] for s, n in places], axis=0) for j in range(3)
    )
    z0 = x0 + x1 + x2
    z1 = lanes(x0 - 0.5 * (x1 + x2), HALF_SQRT3 * (x2 - x1))
    h0, l0 = fwd_mat(tab, 0)
    outs = (mul_right(z0, h0[:BLK], l0[:BLK]), mul_right(z1, *fwd_mat(tab, 1)))
    for g, out in enumerate(outs):
        at = 0
        for s, n in places:
            mid[0, pl.ds(s, n), pl.ds(g * BLK, BLK)] = out[at : at + n, :BLK]
            mid[1, pl.ds(s, n), pl.ds(g * BLK, BLK)] = out[at : at + n, BLK:]
            at += n


def spectrum_rows(tab, mid, spec):
    two = pl.ds(0, CORE)
    a_re, b_re, c_re = (mid[0, pl.ds(j * BLK, BLK), two] for j in range(3))
    a_im, b_im, c_im = (mid[1, pl.ds(j * BLK, BLK), two] for j in range(3))
    s_re, s_im = b_re + c_re, b_im + c_im
    e_re, e_im = a_re - 0.5 * s_re, a_im - 0.5 * s_im
    f_re, f_im = HALF_SQRT3 * (b_re - c_re), HALF_SQRT3 * (b_im - c_im)
    z_re, z_im = a_re + s_re, a_im + s_im
    z_re = lanes(z_re, z_re[:, BLK:])
    z_im = lanes(z_im, -z_im[:, BLK:])
    out = mul_left(*t_mat(tab, 0), rows(z_re, z_im))
    spec[0, pl.ds(0, BLK), :] = out[:BLK]
    spec[1, pl.ds(0, BLK), :] = out[BLK:]
    out1 = mul_left(*t_mat(tab, 1), rows(e_re + f_im, e_im - f_re))
    out2 = mul_left(*t_mat(tab, 2), rows(e_re - f_im, e_im + f_re))
    spec[0, pl.ds(BLK, BLK), :] = lanes(out1[:BLK], out2[:BLK, BLK:])
    spec[1, pl.ds(BLK, BLK), :] = lanes(out1[BLK:], -out2[BLK:, BLK:])
    spec[0, pl.ds(2 * BLK, BLK), :] = lanes(out2[:BLK], out1[:BLK, BLK:])
    spec[1, pl.ds(2 * BLK, BLK), :] = lanes(out2[BLK:], -out1[BLK:, BLK:])


PAIRS = [[(b // 3, b % 3) for b in range(s, min(s + 2, 9))] for s in range(0, 9, 2)]


def field_rows(pair, resp, spec, tab, mid):
    width = len(pair) * BLK
    start = (pair[0][0] * 3 + pair[0][1]) * BLK
    cols = pl.ds(start, width)
    t = []
    for g in range(3):
        block = pl.ds(g * BLK, BLK)
        q_re, q_im = resp[0, block, cols], resp[1, block, cols]
        e_re = jnp.concatenate([spec[0, block, pl.ds(f * BLK, BLK)] for _, f in pair], axis=1)
        e_im = jnp.concatenate([spec[1, block, pl.ds(f * BLK, BLK)] for _, f in pair], axis=1)
        x = rows(e_re * q_re + e_im * q_im, e_im * q_re - e_re * q_im)
        t.append(mul_left(*fwd_mat(tab, g), x))
    s, d = t[1] + t[2], HALF_SQRT3 * (t[1] - t[2])
    first, e = t[0] + s, t[0] - 0.5 * s
    upper, lower = pl.ds(0, BLK), pl.ds(BLK, BLK)
    mid[0, upper, cols] = first[:BLK]
    mid[1, upper, cols] = first[BLK:]
    mid[0, lower, cols] = e[:BLK] - d[BLK:]
    mid[1, lower, cols] = e[BLK:] + d[:BLK]


def field_cols(h, tab, mid, field):
    t = []
    for g in range(3):
        x = jnp.concatenate(
            [
                lanes(*(mid[c, pl.ds(h * BLK, BLK), pl.ds(k * EXTENT + g * BLK, BLK)] for c in range(2)))
                for k in range(3)
            ],
            axis=0,
        )
        t.append(mul_right(x, *t_mat(tab, g)))
    s, d = t[1] + t[2], HALF_SQRT3 * (t[1] - t[2])
    first, e = t[0] + s, t[0] - 0.5 * s
    field[h, 0] = lanes(first[:, :BLK], e[:, :BLK] - d[:, BLK:])
    field[h, 1] = lanes(first[:, BLK:], e[:, BLK:] + d[:, :BLK])


def source_cols(h, slope, weight, tab, field, mid):
    scaled = jnp.concatenate([weight[k] * slope for k in range(3)], axis=0)
    s_re, s_im = scaled * field[h, 0], scaled * field[h, 1]
    a_re, a_im, b_re, b_im = s_re[:, :BLK], s_im[:, :BLK], s_re[:, BLK:], s_im[:, BLK:]
    e_re, e_im = a_re - 0.5 * b_re, a_im - 0.5 * b_im
    f_re, f_im = HALF_SQRT3 * b_re, HALF_SQRT3 * b_im
    z = (
        lanes(a_re + b_re, a_im + b_im),
        lanes(e_re + f_im, e_im - f_re),
        lanes(e_re - f_im, e_im + f_re),
    )
    for g in range(3):
        out = mul_right(z[g], *fwd_mat(tab, g))
        for k in range(3):
            cols = pl.ds(k * EXTENT + g * BLK, BLK)
            mid[0, pl.ds(h * BLK, BLK), cols] = out[k * BLK : (k + 1) * BLK, :BLK]
            mid[1, pl.ds(h * BLK, BLK), cols] = out[k * BLK : (k + 1) * BLK, BLK:]


def source_rows(pair, resp, tab, mid, acc):
    width = len(pair) * BLK
    start = (pair[0][0] * 3 + pair[0][1]) * BLK
    cols = pl.ds(start, width)
    upper, lower = pl.ds(0, BLK), pl.ds(BLK, BLK)
    a_re, a_im, b_re, b_im = mid[0, upper, cols], mid[1, upper, cols], mid[0, lower, cols], mid[1, lower, cols]
    e_re, e_im = a_re - 0.5 * b_re, a_im - 0.5 * b_im
    f_re, f_im = HALF_SQRT3 * b_re, HALF_SQRT3 * b_im
    z = (
        rows(a_re + b_re, a_im + b_im),
        rows(e_re + f_im, e_im - f_re),
        rows(e_re - f_im, e_im + f_re),
    )
    for g in range(3):
        out = mul_left(*t_mat(tab, g), z[g])
        block = pl.ds(g * BLK, BLK)
        o_re, o_im = out[:BLK], out[BLK:]
        q_re, q_im = resp[0, block, cols], resp[1, block, cols]
        p_re, p_im = o_re * q_re - o_im * q_im, o_re * q_im + o_im * q_re
        for n, (k, f) in enumerate(pair):
            into = pl.ds(f * BLK, BLK)
            part = slice(n * BLK, (n + 1) * BLK)
            if k == 0:
                acc[0, block, into] = p_re[:, part]
                acc[1, block, into] = p_im[:, part]
            else:
                acc[0, block, into] += p_re[:, part]
                acc[1, block, into] += p_im[:, part]


def gradient_rows(acc, tab, mid):
    p0, p1, p2 = (pl.ds(g * BLK, BLK) for g in range(3))
    t0 = mul_left(*fwd_mat(tab, 0), rows(acc[0, p0, :], acc[1, p0, :]))
    t0_re, t0_im = t0[:BLK], t0[BLK:]
    t0_re = lanes(t0_re[:, :BLK], t0_re[:, BLK:CORE] + t0_re[:, CORE:])
    t0_im = lanes(t0_im[:, :BLK], t0_im[:, BLK:CORE] - t0_im[:, CORE:])
    x_re = lanes(acc[0, p1, p0], acc[0, p1, p1] + acc[0, p2, p2])
    x_im = lanes(acc[1, p1, p0], acc[1, p1, p1] - acc[1, p2, p2])
    t1 = mul_left(*fwd_mat(tab, 1), rows(x_re, x_im))
    x_re = lanes(acc[0, p2, p0], acc[0, p2, p1] + acc[0, p1, p2])
    x_im = lanes(acc[1, p2, p0], acc[1, p2, p1] - acc[1, p1, p2])
    t2 = mul_left(*fwd_mat(tab, 2), rows(x_re, x_im))
    s, d = t1 + t2, HALF_SQRT3 * (t1 - t2)
    e_re, e_im = t0_re - 0.5 * s[:BLK], t0_im - 0.5 * s[BLK:]
    two = pl.ds(0, CORE)
    mid[0, p0, two], mid[1, p0, two] = t0_re + s[:BLK], t0_im + s[BLK:]
    mid[0, p1, two], mid[1, p1, two] = e_re - d[BLK:], e_im + d[:BLK]
    mid[0, p2, two], mid[1, p2, two] = e_re + d[BLK:], e_im - d[:BLK]


def gradient_cols(places, tab, mid):
    h0, l0 = t_mat(tab, 0)
    part = lambda c, g: jnp.concatenate([mid[c, pl.ds(s, n), pl.ds(g * BLK, BLK)] for s, n in places], axis=0)
    r0 = mul_right(lanes(part(0, 0), part(1, 0)), h0[:, :BLK], l0[:, :BLK])
    r1 = mul_right(lanes(part(0, 1), part(1, 1)), *t_mat(tab, 1))
    e, d = r0 - 0.5 * r1[:, :BLK], HALF_SQRT3 * r1[:, BLK:]
    return r0 + r1[:, :BLK], e - d, e + d


QUARTER = CORE // 4
EIGHTH = CORE // 8
PART = HALO // 4
FARTHEST_FIRST = (2, 1, 3)


def low_lanes(n):
    return lax.broadcasted_iota(jnp.int32, (n, BLK), 1) < HALO


def pack_low(x):
    n = x.shape[0] // 2
    return jnp.where(low_lanes(n), x[:n], pltpu.roll(x[n:], HALO, 1))


def pack_high(x):
    n = x.shape[0] // 2
    return jnp.where(low_lanes(n), pltpu.roll(x[:n], HALO, 1), x[n:])


def unpack_low(x):
    return rows(x, pltpu.roll(x, HALO, 1))


def unpack_high(x):
    return rows(pltpu.roll(x, HALO, 1), x)


def core_blocks(x):
    c0, c1, c2 = (pltpu.roll(x[:, j * BLK : (j + 1) * BLK], HALO, 1) for j in range(3))
    low = low_lanes(x.shape[0])
    return c0, c2, lanes(jnp.where(low, c0, c1), jnp.where(low, c1, c2))


def body_kernel(
    mask_hbm, kernels_hbm, target_hbm, tab_hbm, weight_hbm, link_hbm, out,
    mask, kernels, target, tab, mid, wide, resp, spec, field, acc, ext, resist,
    side_out, side_in, vert_out, vert_in, corner_out, corner_in, margin,
    clear_in, clear_sum, clear_far, power, power_in, power_mine, power_far, power_all,
    halo_parts, halo_in, core_parts, core_in, fold_out, fold_in, bend_out, bend_in, edge_out, edge_in, whole,
    mine, other, gathered,
    weight, link, load_sem, store_sem, side_send, side_recv, vert_send, vert_recv, corner_send, corner_recv, share_send, share_recv,
    clear_send, clear_recv, cfar_send, cfar_recv,
    psc_send, psc_recv, pfar_send, pfar_recv, pall_send, pall_recv,
    hsc_send, hsc_recv, gsc_send, gsc_recv, fold_send, fold_recv, bend_send, bend_recv,
    edge_send, edge_recv, gfar_send, gfar_recv, all_send, all_recv,
):
    tile = lax.axis_index("tile")
    kern = lax.axis_index("kern")
    tiles = lax.axis_size("tile")
    x = kern // 2
    half = kern % 2
    column = (tile + GRID_W // 2) % GRID_W
    right_ok = jnp.where((column < GRID_W - 1) & (tile + 1 < tiles), 1.0, 0.0)
    down_ok = jnp.where(tile + GRID_W < tiles, 1.0, 0.0)

    def valid(tile_by):
        return (tile + tile_by >= 0) & (tile + tile_by < tiles)

    def at(tile_by, kern_index):
        return {"tile": (tile + tile_by + tiles) % tiles, "kern": kern_index}

    far = at(0, 2 * x + 1 - half)
    x_at = [(x + d) % 4 for d in range(4)]
    peers = [at(0, 2 * x_at[d] + half) for d in range(4)]
    sign = 2 * (x % 2) - 1
    crossed = 2 * (x + 1 - 2 * (x % 2)) + half
    near_tiles = [1, -1] + [s * GRID_W + e for s in (1, -1) for e in (-1, 0, 1)]
    partners = [(valid(by), at(by, kern)) for by in near_tiles]
    partners += [(valid(by), at(by, crossed)) for by in (sign * GRID_W + e for e in (-1, 0, 1))]

    barrier = pltpu.get_barrier_semaphore()
    expected = 4
    for there, one in partners:
        expected = expected + there.astype(jnp.int32)

        @pl.when(there)
        def _():
            pl.semaphore_signal(barrier, inc=1, device_id=one, device_id_type=MESH)

    for one in [far] + peers[1:]:
        pl.semaphore_signal(barrier, inc=1, device_id=one, device_id_type=MESH)

    loads = [
        pltpu.make_async_copy(src, dst, load_sem.at[n])
        for n, (src, dst) in enumerate((
            (mask_hbm, mask), (kernels_hbm, kernels), (tab_hbm, tab), (target_hbm, target),
            (link_hbm, link), (weight_hbm, weight),
        ))
    ]
    for copy in (loads[0], loads[4], loads[5], loads[1], loads[2], loads[3]):
        copy.start()
    started = []

    def remote(src, dst, send, recv, device, there=None):
        copy = pltpu.make_async_remote_copy(
            src_ref=src, dst_ref=dst, send_sem=send, recv_sem=recv, device_id=device, device_id_type=MESH
        )
        if there is None:
            copy.start()
        else:
            pl.when(there)(copy.start)
        started.append((there, copy))
        return copy

    def finish_sends():
        for there, copy in started:
            if there is None:
                copy.wait_send()
            else:
                pl.when(there)(copy.wait_send)
        started.clear()

    def clear_unless(there, *refs):
        @pl.when(jnp.logical_not(there))
        def _():
            for ref in refs:
                ref[...] = jnp.zeros(ref.shape, F32)

    from_left_tile, from_right_tile = valid(-1), valid(1)
    from_vert = [valid(-GRID_W), valid(GRID_W)]
    from_corner = [valid(-GRID_W - 1), valid(-GRID_W + 1), valid(GRID_W - 1), valid(GRID_W + 1)]
    clear_unless(from_left_tile, side_in.at[0], edge_in.at[0])
    clear_unless(from_right_tile, side_in.at[1], edge_in.at[1])
    for n in range(2):
        clear_unless(from_vert[n], vert_in.at[n])
    for n in range(4):
        clear_unless(from_corner[n], corner_in.at[n])

    loads[0].wait()
    a0, a1 = mask[0, :, pl.ds(0, BLK)], mask[0, :, pl.ds(BLK, BLK)]
    r0, r1 = pltpu.roll(a0, HALO, 1), pltpu.roll(a1, HALO, 1)
    lane_all = low_lanes(CORE)
    outer = jnp.where(lane_all, r1, r0)
    inner = jnp.where(lane_all, r0, r1)
    middle = pl.ds(HALO, CORE)
    ext[middle, pl.ds(BLK, BLK)] = inner
    ext[middle, pl.ds(0, BLK)] = outer
    loads[4].wait()
    right_link = link[0, 0].astype(F32) * right_ok
    down_link = link[0, 1].astype(F32) * down_ok
    flag = lax.broadcasted_iota(jnp.int32, (8, BLK), 0) < 1
    for n, first in enumerate((CORE - HALO, 0)):
        block = pl.ds(pl.multiple_of(HALO + first + PART * x, PART), PART)
        outer_part = ext[block, pl.ds(0, BLK)]
        vert_out[n, pl.ds(0, PART), :] = outer_part
        vert_out[n, pl.ds(PART, PART), :] = ext[block, pl.ds(BLK, BLK)]
        vert_out[n, pl.ds(2 * PART, 8), :] = jnp.where(flag, down_link, right_link)
        corner_out[n, 0] = pack_high(outer_part)
        corner_out[n, 1] = pack_low(outer_part) * right_link
    side_out[0] = pack_low(outer) * right_link
    side_out[1] = pack_high(outer)

    pl.semaphore_wait(barrier, expected)
    w = GRID_W
    verts = [
        remote(vert_out.at[0], vert_in.at[0], vert_send.at[0], vert_recv.at[0], at(w, kern), valid(w)),
        remote(vert_out.at[1], vert_in.at[1], vert_send.at[1], vert_recv.at[1], at(-w, kern), valid(-w)),
    ]
    for n, (by, src) in enumerate((
        (w + 1, corner_out.at[0, 1]), (w - 1, corner_out.at[0, 0]),
        (1 - w, corner_out.at[1, 1]), (-1 - w, corner_out.at[1, 0]),
    )):
        verts.append(remote(src, corner_in.at[n], corner_send.at[n], corner_recv.at[n], at(by, kern), valid(by)))
    sides = [
        remote(side_out.at[0], side_in.at[0], side_send.at[0], side_recv.at[0], at(1, kern), valid(1)),
        remote(side_out.at[1], side_in.at[1], side_send.at[1], side_recv.at[1], at(-1, kern), valid(-1)),
    ]

    loads[1].wait()
    loads[5].wait()
    taps = [[jnp.sum(kernels[c, k], keepdims=True) for k in range(3)] for c in range(2)]
    clear_part = sum(weight[k] * (taps[0][k] * taps[0][k] + taps[1][k] * taps[1][k]) for k in range(3))
    clear_in[x] = jnp.broadcast_to(clear_part, (8, BLK))
    clears = [
        remote(clear_in.at[x], clear_in.at[x], clear_send.at[d - 1], clear_recv.at[d - 1], peers[d])
        for d in FARTHEST_FIRST
    ]
    loads[2].wait()
    response_rows(kernels, tab, mid)
    response_cols(0, tab, mid, resp)

    for there, copy in zip((from_left_tile, from_right_tile), sides):
        pl.when(there)(copy.wait_recv)
    from_left, from_right = unpack_low(side_in[0]), unpack_high(side_in[1]) * right_link
    outer = ext[middle, pl.ds(0, BLK)]
    ext[middle, pl.ds(0, BLK)] = jnp.where(lane_all, from_left, outer)
    ext[middle, pl.ds(CORE, BLK)] = jnp.where(lane_all, outer, from_right)

    for there, copy in zip(from_vert + from_corner, verts):
        pl.when(there)(copy.wait_recv)
    down_above, right_above = (vert_in[0, pl.ds(2 * PART + r, 1), pl.ds(0, 1)] for r in (0, 1))
    right_below = vert_in[1, pl.ds(2 * PART + 1, 1), pl.ds(0, 1)]
    lane_part = low_lanes(PART)
    for n, (factor, beside) in enumerate(((down_above, right_above), (down_link, right_below))):
        edge = vert_in[n, pl.ds(0, PART), :]
        first, last = unpack_low(corner_in[2 * n]), unpack_high(corner_in[2 * n + 1])
        margin[x, n, :, pl.ds(0, BLK)] = jnp.where(lane_part, first, edge) * factor
        margin[x, n, :, pl.ds(BLK, BLK)] = vert_in[n, pl.ds(PART, PART), :] * factor
        margin[x, n, :, pl.ds(CORE, BLK)] = jnp.where(lane_part, edge, last * beside) * factor
    shares = [
        remote(margin.at[x], margin.at[x], share_send.at[d - 1], share_recv.at[d - 1], peers[d])
        for d in FARTHEST_FIRST
    ]
    for copy in clears:
        copy.wait_recv()
    clear_sum[...] = clear_in[0] + clear_in[1] + clear_in[2] + clear_in[3]
    clear_copy = remote(clear_sum, clear_far, cfar_send, cfar_recv, far)
    response_cols(1, tab, mid, resp)
    response_cols(2, tab, mid, resp)
    spectrum_cols(ext, [(HALO, CORE)], tab, mid)
    for copy in shares:
        copy.wait_recv()
    for q in range(4):
        ext[pl.ds(PART * q, PART), :] = margin[q, 0]
        ext[pl.ds(HALO + CORE + PART * q, PART), :] = margin[q, 1]
    spectrum_cols(ext, [(0, HALO), (HALO + CORE, HALO)], tab, mid)
    spectrum_rows(tab, mid, spec)
    for pair in PAIRS:
        field_rows(pair, resp, spec, tab, wide)

    scatter = []
    for h in range(2):
        field_cols(h, tab, wide, field)
        for q in range(4):
            p = 0.0
            for k in range(3):
                block = pl.ds(k * BLK + q * EIGHTH, EIGHTH)
                f_re, f_im = field[h, 0, block, :], field[h, 1, block, :]
                p = p + weight[k] * (f_re * f_re + f_im * f_im)
            power[h, q] = p
        scatter.append([
            remote(power.at[h, x_at[d]], power_in.at[h, d - 1], psc_send.at[h, d - 1], psc_recv.at[h, d - 1], peers[d])
            for d in FARTHEST_FIRST
        ])
    loads[3].wait()
    clear_copy.wait_recv()
    swaps = []
    for h in range(2):
        for copy in scatter[h]:
            copy.wait_recv()
        power_mine[h] = power[h, x] + power_in[h, 0] + power_in[h, 1] + power_in[h, 2]
        swaps.append(remote(power_mine.at[h], power_far.at[h], pfar_send.at[h], pfar_recv.at[h], far))
    finish_sends()
    gathers = []
    for h in range(2):
        swaps[h].wait_recv()
        power_all[h, x] = power_mine[h] + power_far[h]
        gathers.append([
            remote(power_all.at[h, x], power_all.at[h, x], pall_send.at[h, d - 1], pall_recv.at[h, d - 1], peers[d])
            for d in FARTHEST_FIRST
        ])
    clear = (clear_sum[...] + clear_far[...])[0:1, 0:1]
    for h in range(2):
        for copy in gathers[h]:
            copy.wait_recv()
        total = jnp.concatenate([power_all[h, q] for q in range(4)], axis=0)
        printed = 1.0 / (1.0 + jnp.exp(-STEEP * (total / clear - THRESH)))
        block = pl.ds(h * BLK, BLK)
        resist[0, block, :] = printed
        wanted = target[0, block, :].astype(F32)
        slope = (4.0 * STEEP) * (printed - wanted) * printed * (1.0 - printed) / clear
        source_cols(h, slope, weight, tab, field, wide)
    store = pltpu.make_async_copy(resist, out.at[0], store_sem.at[0])
    store.start()
    for pair in PAIRS:
        source_rows(pair, resp, tab, wide, acc)
    gradient_rows(acc, tab, mid)

    blocks = gradient_cols([(0, HALO), (HALO + CORE, HALO)], tab, mid)
    for c in range(3):
        for q, start in enumerate((64, 96, 32, 0)):
            halo_parts[q, :, pl.ds(c * BLK, BLK)] = blocks[c][start : start + 32]
    halo_scatter = [
        remote(halo_parts.at[x_at[d]], halo_in.at[d - 1], hsc_send.at[d - 1], hsc_recv.at[d - 1], peers[d])
        for d in FARTHEST_FIRST
    ]
    blocks = gradient_cols([(HALO, CORE)], tab, mid)
    for c in range(3):
        for q in range(4):
            core_parts[q, :, pl.ds(c * BLK, BLK)] = blocks[c][q * QUARTER : (q + 1) * QUARTER]
    core_scatter = [
        remote(core_parts.at[x_at[d]], core_in.at[d - 1], gsc_send.at[d - 1], gsc_recv.at[d - 1], peers[d])
        for d in FARTHEST_FIRST
    ]

    low_x = x < 2
    for copy in halo_scatter:
        copy.wait_recv()
    is_low = jnp.where(low_x, 1.0, 0.0)
    down_factor = is_low * down_link + (1.0 - is_low) * down_above
    right_factor = is_low * right_below + (1.0 - is_low) * right_above
    total = (halo_parts[x] + halo_in[0] + halo_in[1] + halo_in[2]) * down_factor
    first, last, fold_out[...] = core_blocks(total)
    bend_out[0] = pack_high(first)
    bend_out[1] = pack_low(last) * right_factor
    slot = jnp.where((x == 1) | (x == 2), 1, 0)
    step = jnp.where(low_x, GRID_W, -GRID_W)
    owner = jnp.where(low_x, 0, 6) + half
    remote(fold_out, fold_in.at[slot], fold_send, fold_recv.at[slot], at(step, owner), valid(step))
    for n, by in enumerate((step - 1, step + 1)):
        remote(
            bend_out.at[n], bend_in.at[slot, n], bend_send.at[n], bend_recv.at[slot, n], at(by, owner), valid(by)
        )

    for copy in core_scatter:
        copy.wait_recv()
    first, last, whole[...] = core_blocks(core_parts[x] + core_in[0] + core_in[1] + core_in[2])
    edge_out[0] = pack_low(last) * right_link
    edge_out[1] = pack_high(first)
    edges = [
        remote(edge_out.at[0], edge_in.at[0], edge_send.at[0], edge_recv.at[0], at(1, kern), valid(1)),
        remote(edge_out.at[1], edge_in.at[1], edge_send.at[1], edge_recv.at[1], at(-1, kern), valid(-1)),
    ]

    takes = (x == 0) | (x == 3)
    back = jnp.where(x == 0, -GRID_W, GRID_W)
    lane_fold = low_lanes(32)
    for s in range(2):
        arrivals = (
            (valid(back), fold_out, fold_in.at[s], fold_send, fold_recv.at[s]),
            (valid(back + 1), bend_out.at[0], bend_in.at[s, 0], bend_send.at[0], bend_recv.at[s, 0]),
            (valid(back - 1), bend_out.at[1], bend_in.at[s, 1], bend_send.at[1], bend_recv.at[s, 1]),
        )
        for there, src, dst, send, recv in arrivals:
            copy = pltpu.make_async_remote_copy(
                src_ref=src, dst_ref=dst, send_sem=send, recv_sem=recv, device_id=far, device_id_type=MESH
            )
            clear_unless(takes & there, dst)
            pl.when(takes & there)(copy.wait_recv)
        block = pl.ds(32 * s, 32)
        from_left = jnp.where(lane_fold, unpack_low(bend_in[s, 1]), 0.0)
        from_right = jnp.where(lane_fold, 0.0, unpack_high(bend_in[s, 0])) * right_link
        whole[block, :] += fold_in[s] + lanes(from_left, from_right)

    for there, copy in zip((from_left_tile, from_right_tile), edges):
        pl.when(there)(copy.wait_recv)
    lane_edge = low_lanes(QUARTER)
    from_left = jnp.where(lane_edge, unpack_low(edge_in[0]), 0.0)
    from_right = jnp.where(lane_edge, 0.0, unpack_high(edge_in[1])) * right_link
    partial = whole[...] + lanes(from_left, from_right)
    swaps = []
    for h in range(2):
        mine[h] = partial[h * 32 : (h + 1) * 32]
        swaps.append(remote(mine.at[h], other.at[h], gfar_send.at[h], gfar_recv.at[h], far))
    finish_sends()
    finals = []
    stores = [store]
    for h in range(2):
        swaps[h].wait_recv()
        gathered[h] = mine[h] + other[h]
        place = out.at[1, 0, pl.ds(pl.multiple_of(QUARTER * x + 32 * h, 32), 32)]
        finals += [
            remote(gathered.at[h], place, all_send.at[h, d - 1], all_recv.at[h, d - 1], peers[d])
            for d in FARTHEST_FIRST
        ]
        stores.append(pltpu.make_async_copy(gathered.at[h], place, store_sem.at[1 + h]))
        stores[-1].start()
    for copy in finals:
        copy.wait_recv()
    finish_sends()
    for copy in stores:
        copy.wait()


def store_kernel(both, resist_out, grad_out, held, load_sem, store_sem):
    pieces = [(n, pl.ds(q * BLK, BLK)) for n in range(2) for q in range(2)]
    loads = [
        pltpu.make_async_copy(both.at[n, 0, block], held.at[n, 0, block], load_sem.at[i])
        for i, (n, block) in enumerate(pieces)
    ]
    for copy in loads:
        copy.start()
    stores = []
    for i, (n, block) in enumerate(pieces):
        loads[i].wait()
        into = (resist_out, grad_out)[n]
        stores.append(pltpu.make_async_copy(held.at[n, 0, block], into.at[0, block], store_sem.at[i]))
        stores[-1].start()
    for copy in stores:
        copy.wait()


def body(mask, kernels, weight, link, target):
    anywhere = pl.BlockSpec(memory_space=pl.ANY)
    dma = pltpu.SemaphoreType.DMA
    f32 = lambda *shape: pltpu.VMEM(shape, F32)
    buffers = [
        f32(1, CORE, CORE), f32(2, 3, BLK, BLK), pltpu.VMEM((1, CORE, CORE), jnp.int32),
        pltpu.VMEM((2, 2, 3, CORE, CORE), BF16),
        f32(2, EXTENT, EXTENT), f32(2, CORE, 3 * EXTENT), f32(2, EXTENT, 3 * EXTENT), f32(2, EXTENT, EXTENT),
        f32(2, 2, EXTENT, CORE), f32(2, EXTENT, EXTENT), f32(EXTENT, EXTENT), f32(1, CORE, CORE),
        f32(2, BLK, BLK), f32(2, BLK, BLK), f32(2, 2 * PART + 8, BLK), f32(2, 2 * PART + 8, BLK),
        f32(2, 2, PART // 2, BLK), f32(4, PART // 2, BLK), f32(4, 2, PART, EXTENT),
        f32(4, 8, BLK), f32(8, BLK), f32(8, BLK),
        f32(2, 4, EIGHTH, CORE), f32(2, 3, EIGHTH, CORE), f32(2, EIGHTH, CORE), f32(2, EIGHTH, CORE),
        f32(2, 4, EIGHTH, CORE),
        f32(4, 32, EXTENT), f32(3, 32, EXTENT), f32(4, QUARTER, EXTENT), f32(3, QUARTER, EXTENT),
        f32(32, CORE), f32(2, 32, CORE), f32(2, 16, BLK), f32(2, 2, 16, BLK),
        f32(2, 32, BLK), f32(2, 32, BLK), f32(QUARTER, CORE),
        f32(2, 32, CORE), f32(2, 32, CORE), f32(2, 32, CORE),
    ]
    sems = [pltpu.SMEM((3,), F32), pltpu.SMEM((1, 2), jnp.int32), dma((6,)), dma((3,))] + [dma((2,))] * 4 + [dma((4,))] * 2 + [dma((3,))] * 2
    sems += [dma((3,))] * 2 + [dma] * 2
    sems += [dma((2, 3))] * 2 + [dma((2,))] * 2 + [dma((2, 3))] * 2
    sems += [dma((3,))] * 4 + [dma, dma((2,)), dma((2,)), dma((2, 2))]
    sems += [dma((2,))] * 4 + [dma((2, 3))] * 2
    both = pl.pallas_call(
        body_kernel,
        out_shape=jax.ShapeDtypeStruct((2, 1, CORE, CORE), F32),
        in_specs=[anywhere] * 6,
        out_specs=anywhere,
        scratch_shapes=buffers + sems,
        compiler_params=pltpu.CompilerParams(
            collective_id=0, has_side_effects=True, vmem_limit_bytes=60 * 2**20
        ),
    )(mask, kernels, target, jnp.asarray(dft_tables()), weight, link)
    out = jax.ShapeDtypeStruct((1, CORE, CORE), F32)
    return pl.pallas_call(
        store_kernel,
        out_shape=(out, out),
        in_specs=[anywhere],
        out_specs=(anywhere, anywhere),
        scratch_shapes=[f32(2, 1, CORE, CORE), dma((4,)), dma((4,))],
        compiler_params=pltpu.CompilerParams(vmem_limit_bytes=60 * 2**20),
    )(both)


def solution(mesh):
    in_specs = (
        P("tile", None, None),
        P(None, "kern", None, None),
        P("kern"),
        P("tile", None),
        P("tile", None, None),
    )
    out_specs = (P("tile", None, None), P("tile", None, None))
    return jax.shard_map(body, mesh=mesh, in_specs=in_specs, out_specs=out_specs, check_vma=False)
```

```python
import functools
import math

import jax
import jax.numpy as jnp
import ml_dtypes
import numpy as np
from jax import lax
from jax.experimental import pallas as pl
from jax.experimental.pallas import tpu as pltpu
from jax.sharding import PartitionSpec as P

GRID_W = 8
STEEP = 20.0
THRESH = 0.33
BLK = 128
EXTENT = 3 * BLK
CORE = 2 * BLK
HALO = BLK // 2
HALF_SQRT3 = math.sqrt(3.0) / 2.0
MESH = pl.DeviceIdType.MESH
F32 = jnp.float32
BF16 = jnp.bfloat16


def dft_tables():
    place = np.arange(BLK)
    groups = (3 * place, 3 * place + 1, -(3 * place + 1))
    mats = []
    for freq in groups:
        angle = 2.0 * np.pi * (np.outer(place, freq) % EXTENT) / EXTENT
        c, s = np.cos(angle), -np.sin(angle)
        mats.append(np.block([[c, s], [-s, c]]))
    fwd = np.stack(mats).astype(np.float32)
    both = np.stack([fwd, fwd.transpose(0, 2, 1)])
    high = both.astype(ml_dtypes.bfloat16)
    low = (both - high.astype(np.float32)).astype(ml_dtypes.bfloat16)
    return np.stack([high, low])


def split(x):
    high = x.astype(BF16)
    return high, (x - high.astype(F32)).astype(BF16)


def dot(a, b):
    return jnp.dot(a, b, preferred_element_type=F32)


def mul_right(x, high, low):
    xh, xl = split(x)
    return dot(xh, high) + (dot(xh, low) + dot(xl, high))


def mul_left(high, low, x):
    xh, xl = split(x)
    n = x.shape[1]
    both = dot(high, jnp.concatenate([xh, xl], axis=1))
    return both[:, :n] + (both[:, n:] + dot(low, xh))


def fwd_mat(tab, g):
    return tab[0, 0, g], tab[1, 0, g]


def t_mat(tab, g):
    return tab[0, 1, g], tab[1, 1, g]


def lanes(re, im):
    return jnp.concatenate([re, im], axis=1)


def rows(re, im):
    return jnp.concatenate([re, im], axis=0)


def response_rows(kernels, tab, mid):
    scale = 1.0 / (EXTENT * EXTENT)
    re = jnp.concatenate([kernels[0, k] for k in range(3)], axis=1) * scale
    im = jnp.concatenate([kernels[1, k] for k in range(3)], axis=1) * -scale
    taps = rows(re, im)
    for g in range(3):
        out = mul_left(*t_mat(tab, g), taps)
        mid[0, pl.ds(g * BLK, BLK), :] = out[:BLK]
        mid[1, pl.ds(g * BLK, BLK), :] = out[BLK:]


def response_cols(k, tab, mid, resp):
    cols = pl.ds(k * BLK, BLK)
    x = lanes(mid[0, :, cols], mid[1, :, cols])
    for g in range(3):
        out = mul_right(x, *fwd_mat(tab, g))
        resp[0, :, pl.ds(k * EXTENT + g * BLK, BLK)] = out[:, :BLK]
        resp[1, :, pl.ds(k * EXTENT + g * BLK, BLK)] = out[:, BLK:]


def spectrum_cols(ext, places, tab, mid):
    x0, x1, x2 = (
        jnp.concatenate([ext[pl.ds(s, n), pl.ds(j * BLK, BLK)] for s, n in places], axis=0) for j in range(3)
    )
    z0 = x0 + x1 + x2
    z1 = lanes(x0 - 0.5 * (x1 + x2), HALF_SQRT3 * (x2 - x1))
    h0, l0 = fwd_mat(tab, 0)
    outs = (mul_right(z0, h0[:BLK], l0[:BLK]), mul_right(z1, *fwd_mat(tab, 1)))
    for g, out in enumerate(outs):
        at = 0
        for s, n in places:
            mid[0, pl.ds(s, n), pl.ds(g * BLK, BLK)] = out[at : at + n, :BLK]
            mid[1, pl.ds(s, n), pl.ds(g * BLK, BLK)] = out[at : at + n, BLK:]
            at += n


def spectrum_rows(tab, mid, spec):
    two = pl.ds(0, CORE)
    a_re, b_re, c_re = (mid[0, pl.ds(j * BLK, BLK), two] for j in range(3))
    a_im, b_im, c_im = (mid[1, pl.ds(j * BLK, BLK), two] for j in range(3))
    s_re, s_im = b_re + c_re, b_im + c_im
    e_re, e_im = a_re - 0.5 * s_re, a_im - 0.5 * s_im
    f_re, f_im = HALF_SQRT3 * (b_re - c_re), HALF_SQRT3 * (b_im - c_im)
    z_re, z_im = a_re + s_re, a_im + s_im
    z_re = lanes(z_re, z_re[:, BLK:])
    z_im = lanes(z_im, -z_im[:, BLK:])
    out = mul_left(*t_mat(tab, 0), rows(z_re, z_im))
    spec[0, pl.ds(0, BLK), :] = out[:BLK]
    spec[1, pl.ds(0, BLK), :] = out[BLK:]
    out1 = mul_left(*t_mat(tab, 1), rows(e_re + f_im, e_im - f_re))
    out2 = mul_left(*t_mat(tab, 2), rows(e_re - f_im, e_im + f_re))
    spec[0, pl.ds(BLK, BLK), :] = lanes(out1[:BLK], out2[:BLK, BLK:])
    spec[1, pl.ds(BLK, BLK), :] = lanes(out1[BLK:], -out2[BLK:, BLK:])
    spec[0, pl.ds(2 * BLK, BLK), :] = lanes(out2[:BLK], out1[:BLK, BLK:])
    spec[1, pl.ds(2 * BLK, BLK), :] = lanes(out2[BLK:], -out1[BLK:, BLK:])


PAIRS = [[(b // 3, b % 3) for b in range(s, min(s + 2, 9))] for s in range(0, 9, 2)]


def field_rows(pair, resp, spec, tab, mid):
    width = len(pair) * BLK
    start = (pair[0][0] * 3 + pair[0][1]) * BLK
    cols = pl.ds(start, width)
    t = []
    for g in range(3):
        block = pl.ds(g * BLK, BLK)
        q_re, q_im = resp[0, block, cols], resp[1, block, cols]
        e_re = jnp.concatenate([spec[0, block, pl.ds(f * BLK, BLK)] for _, f in pair], axis=1)
        e_im = jnp.concatenate([spec[1, block, pl.ds(f * BLK, BLK)] for _, f in pair], axis=1)
        x = rows(e_re * q_re + e_im * q_im, e_im * q_re - e_re * q_im)
        t.append(mul_left(*fwd_mat(tab, g), x))
    s, d = t[1] + t[2], HALF_SQRT3 * (t[1] - t[2])
    first, e = t[0] + s, t[0] - 0.5 * s
    upper, lower = pl.ds(0, BLK), pl.ds(BLK, BLK)
    mid[0, upper, cols] = first[:BLK]
    mid[1, upper, cols] = first[BLK:]
    mid[0, lower, cols] = e[:BLK] - d[BLK:]
    mid[1, lower, cols] = e[BLK:] + d[:BLK]


def field_cols(h, tab, mid, field):
    t = []
    for g in range(3):
        x = jnp.concatenate(
            [
                lanes(*(mid[c, pl.ds(h * BLK, BLK), pl.ds(k * EXTENT + g * BLK, BLK)] for c in range(2)))
                for k in range(3)
            ],
            axis=0,
        )
        t.append(mul_right(x, *t_mat(tab, g)))
    s, d = t[1] + t[2], HALF_SQRT3 * (t[1] - t[2])
    first, e = t[0] + s, t[0] - 0.5 * s
    field[h, 0] = lanes(first[:, :BLK], e[:, :BLK] - d[:, BLK:])
    field[h, 1] = lanes(first[:, BLK:], e[:, BLK:] + d[:, :BLK])


def source_cols(h, slope, weight, tab, field, mid):
    scaled = jnp.concatenate([weight[k] * slope for k in range(3)], axis=0)
    s_re, s_im = scaled * field[h, 0], scaled * field[h, 1]
    a_re, a_im, b_re, b_im = s_re[:, :BLK], s_im[:, :BLK], s_re[:, BLK:], s_im[:, BLK:]
    e_re, e_im = a_re - 0.5 * b_re, a_im - 0.5 * b_im
    f_re, f_im = HALF_SQRT3 * b_re, HALF_SQRT3 * b_im
    z = (
        lanes(a_re + b_re, a_im + b_im),
        lanes(e_re + f_im, e_im - f_re),
        lanes(e_re - f_im, e_im + f_re),
    )
    for g in range(3):
        out = mul_right(z[g], *fwd_mat(tab, g))
        for k in range(3):
            cols = pl.ds(k * EXTENT + g * BLK, BLK)
            mid[0, pl.ds(h * BLK, BLK), cols] = out[k * BLK : (k + 1) * BLK, :BLK]
            mid[1, pl.ds(h * BLK, BLK), cols] = out[k * BLK : (k + 1) * BLK, BLK:]


def source_rows(pair, resp, tab, mid, acc):
    width = len(pair) * BLK
    start = (pair[0][0] * 3 + pair[0][1]) * BLK
    cols = pl.ds(start, width)
    upper, lower = pl.ds(0, BLK), pl.ds(BLK, BLK)
    a_re, a_im, b_re, b_im = mid[0, upper, cols], mid[1, upper, cols], mid[0, lower, cols], mid[1, lower, cols]
    e_re, e_im = a_re - 0.5 * b_re, a_im - 0.5 * b_im
    f_re, f_im = HALF_SQRT3 * b_re, HALF_SQRT3 * b_im
    z = (
        rows(a_re + b_re, a_im + b_im),
        rows(e_re + f_im, e_im - f_re),
        rows(e_re - f_im, e_im + f_re),
    )
    for g in range(3):
        out = mul_left(*t_mat(tab, g), z[g])
        block = pl.ds(g * BLK, BLK)
        o_re, o_im = out[:BLK], out[BLK:]
        q_re, q_im = resp[0, block, cols], resp[1, block, cols]
        p_re, p_im = o_re * q_re - o_im * q_im, o_re * q_im + o_im * q_re
        for n, (k, f) in enumerate(pair):
            into = pl.ds(f * BLK, BLK)
            part = slice(n * BLK, (n + 1) * BLK)
            if k == 0:
                acc[0, block, into] = p_re[:, part]
                acc[1, block, into] = p_im[:, part]
            else:
                acc[0, block, into] += p_re[:, part]
                acc[1, block, into] += p_im[:, part]


def gradient_rows(acc, tab, mid):
    p0, p1, p2 = (pl.ds(g * BLK, BLK) for g in range(3))
    t0 = mul_left(*fwd_mat(tab, 0), rows(acc[0, p0, :], acc[1, p0, :]))
    t0_re, t0_im = t0[:BLK], t0[BLK:]
    t0_re = lanes(t0_re[:, :BLK], t0_re[:, BLK:CORE] + t0_re[:, CORE:])
    t0_im = lanes(t0_im[:, :BLK], t0_im[:, BLK:CORE] - t0_im[:, CORE:])
    x_re = lanes(acc[0, p1, p0], acc[0, p1, p1] + acc[0, p2, p2])
    x_im = lanes(acc[1, p1, p0], acc[1, p1, p1] - acc[1, p2, p2])
    t1 = mul_left(*fwd_mat(tab, 1), rows(x_re, x_im))
    x_re = lanes(acc[0, p2, p0], acc[0, p2, p1] + acc[0, p1, p2])
    x_im = lanes(acc[1, p2, p0], acc[1, p2, p1] - acc[1, p1, p2])
    t2 = mul_left(*fwd_mat(tab, 2), rows(x_re, x_im))
    s, d = t1 + t2, HALF_SQRT3 * (t1 - t2)
    e_re, e_im = t0_re - 0.5 * s[:BLK], t0_im - 0.5 * s[BLK:]
    two = pl.ds(0, CORE)
    mid[0, p0, two], mid[1, p0, two] = t0_re + s[:BLK], t0_im + s[BLK:]
    mid[0, p1, two], mid[1, p1, two] = e_re - d[BLK:], e_im + d[:BLK]
    mid[0, p2, two], mid[1, p2, two] = e_re + d[BLK:], e_im - d[:BLK]


def gradient_cols(places, tab, mid):
    h0, l0 = t_mat(tab, 0)
    part = lambda c, g: jnp.concatenate([mid[c, pl.ds(s, n), pl.ds(g * BLK, BLK)] for s, n in places], axis=0)
    r0 = mul_right(lanes(part(0, 0), part(1, 0)), h0[:, :BLK], l0[:, :BLK])
    r1 = mul_right(lanes(part(0, 1), part(1, 1)), *t_mat(tab, 1))
    e, d = r0 - 0.5 * r1[:, :BLK], HALF_SQRT3 * r1[:, BLK:]
    return r0 + r1[:, :BLK], e - d, e + d


QUARTER = CORE // 4
EIGHTH = CORE // 8
PART = HALO // 4
FARTHEST_FIRST = (2, 3, 1)


def low_lanes(n):
    return lax.broadcasted_iota(jnp.int32, (n, BLK), 1) < HALO


def pack_low(x):
    n = x.shape[0] // 2
    return jnp.where(low_lanes(n), x[:n], pltpu.roll(x[n:], HALO, 1))


def pack_high(x):
    n = x.shape[0] // 2
    return jnp.where(low_lanes(n), pltpu.roll(x[:n], HALO, 1), x[n:])


def unpack_low(x):
    return rows(x, pltpu.roll(x, HALO, 1))


def unpack_high(x):
    return rows(pltpu.roll(x, HALO, 1), x)


def core_blocks(x):
    c0, c1, c2 = (pltpu.roll(x[:, j * BLK : (j + 1) * BLK], HALO, 1) for j in range(3))
    low = low_lanes(x.shape[0])
    return c0, c2, lanes(jnp.where(low, c0, c1), jnp.where(low, c1, c2))


def body_kernel(
    mask_hbm, kernels_hbm, target_hbm, tab_hbm, weight_hbm, link_hbm, out,
    mask, kernels, target, tab, mid, wide, resp, spec, field, acc, ext, resist,
    side_out, side_in, vert_out, vert_in, corner_out, corner_in, margin,
    clear_in, clear_sum, clear_far, power, power_in, power_mine, power_far, power_all,
    halo_parts, halo_in, core_parts, core_in, fold_out, fold_in, bend_out, bend_in, edge_out, edge_in, whole,
    mine, other, gathered,
    weight, link, load_sem, store_sem, side_send, side_recv, vert_send, vert_recv, corner_send, corner_recv, share_send, share_recv,
    clear_send, clear_recv, cfar_send, cfar_recv,
    psc_send, psc_recv, pfar_send, pfar_recv, pall_send, pall_recv,
    hsc_send, hsc_recv, gsc_send, gsc_recv, gmid_send, gmid_recv, fold_send, fold_recv, bend_send, bend_recv,
    edge_send, edge_recv, gfar_send, gfar_recv, all_send, all_recv,
):
    tile = lax.axis_index("tile")
    kern = lax.axis_index("kern")
    tiles = lax.axis_size("tile")
    x = kern // 2
    half = kern % 2
    column = (tile + GRID_W // 2) % GRID_W
    right_ok = jnp.where((column < GRID_W - 1) & (tile + 1 < tiles), 1.0, 0.0)
    down_ok = jnp.where(tile + GRID_W < tiles, 1.0, 0.0)

    def valid(tile_by):
        return (tile + tile_by >= 0) & (tile + tile_by < tiles)

    def at(tile_by, kern_index):
        return {"tile": (tile + tile_by + tiles) % tiles, "kern": kern_index}

    far = at(0, 2 * x + 1 - half)
    x_at = [(x + d) % 4 for d in range(4)]
    peers = [at(0, 2 * x_at[d] + half) for d in range(4)]
    sign = 2 * (x % 2) - 1
    crossed = 2 * (x + 1 - 2 * (x % 2)) + half
    near_tiles = [1, -1] + [s * GRID_W + e for s in (1, -1) for e in (-1, 0, 1)]
    partners = [(valid(by), at(by, kern)) for by in near_tiles]
    partners += [(valid(by), at(by, crossed)) for by in (sign * GRID_W + e for e in (-1, 0, 1))]

    barrier = pltpu.get_barrier_semaphore()
    expected = 4
    for there, one in partners:
        expected = expected + there.astype(jnp.int32)

        @pl.when(there)
        def _():
            pl.semaphore_signal(barrier, inc=1, device_id=one, device_id_type=MESH)

    for one in [far] + peers[1:]:
        pl.semaphore_signal(barrier, inc=1, device_id=one, device_id_type=MESH)

    loads = [
        pltpu.make_async_copy(src, dst, load_sem.at[n])
        for n, (src, dst) in enumerate((
            (mask_hbm, mask), (kernels_hbm, kernels), (tab_hbm, tab), (target_hbm, target),
            (link_hbm, link), (weight_hbm, weight),
        ))
    ]
    for copy in (loads[0], loads[4], loads[5], loads[1], loads[2], loads[3]):
        copy.start()
    started = []

    def remote(src, dst, send, recv, device, there=None):
        copy = pltpu.make_async_remote_copy(
            src_ref=src, dst_ref=dst, send_sem=send, recv_sem=recv, device_id=device, device_id_type=MESH
        )
        if there is None:
            copy.start()
        else:
            pl.when(there)(copy.start)
        started.append((there, copy))
        return copy

    def finish_sends():
        for there, copy in started:
            if there is None:
                copy.wait_send()
            else:
                pl.when(there)(copy.wait_send)
        started.clear()

    def clear_unless(there, *refs):
        @pl.when(jnp.logical_not(there))
        def _():
            for ref in refs:
                ref[...] = jnp.zeros(ref.shape, F32)

    from_left_tile, from_right_tile = valid(-1), valid(1)
    from_vert = [valid(-GRID_W), valid(GRID_W)]
    from_corner = [valid(-GRID_W - 1), valid(-GRID_W + 1), valid(GRID_W - 1), valid(GRID_W + 1)]
    clear_unless(from_left_tile, side_in.at[0], edge_in.at[0])
    clear_unless(from_right_tile, side_in.at[1], edge_in.at[1])
    for n in range(2):
        clear_unless(from_vert[n], vert_in.at[n])
    for n in range(4):
        clear_unless(from_corner[n], corner_in.at[n])

    loads[0].wait()
    a0, a1 = mask[0, :, pl.ds(0, BLK)], mask[0, :, pl.ds(BLK, BLK)]
    r0, r1 = pltpu.roll(a0, HALO, 1), pltpu.roll(a1, HALO, 1)
    lane_all = low_lanes(CORE)
    outer = jnp.where(lane_all, r1, r0)
    inner = jnp.where(lane_all, r0, r1)
    middle = pl.ds(HALO, CORE)
    ext[middle, pl.ds(BLK, BLK)] = inner
    ext[middle, pl.ds(0, BLK)] = outer
    loads[4].wait()
    right_link = link[0, 0].astype(F32) * right_ok
    down_link = link[0, 1].astype(F32) * down_ok
    flag = lax.broadcasted_iota(jnp.int32, (8, BLK), 0) < 1
    for n, first in enumerate((CORE - HALO, 0)):
        block = pl.ds(pl.multiple_of(HALO + first + PART * x, PART), PART)
        outer_part = ext[block, pl.ds(0, BLK)]
        vert_out[n, pl.ds(0, PART), :] = outer_part
        vert_out[n, pl.ds(PART, PART), :] = ext[block, pl.ds(BLK, BLK)]
        vert_out[n, pl.ds(2 * PART, 8), :] = jnp.where(flag, down_link, right_link)
        corner_out[n, 0] = pack_high(outer_part)
        corner_out[n, 1] = pack_low(outer_part) * right_link
    side_out[0] = pack_low(outer) * right_link
    side_out[1] = pack_high(outer)

    pl.semaphore_wait(barrier, expected)
    w = GRID_W
    sides = [
        remote(side_out.at[0], side_in.at[0], side_send.at[0], side_recv.at[0], at(1, kern), valid(1)),
        remote(side_out.at[1], side_in.at[1], side_send.at[1], side_recv.at[1], at(-1, kern), valid(-1)),
    ]
    verts = [
        remote(vert_out.at[0], vert_in.at[0], vert_send.at[0], vert_recv.at[0], at(w, kern), valid(w)),
        remote(vert_out.at[1], vert_in.at[1], vert_send.at[1], vert_recv.at[1], at(-w, kern), valid(-w)),
    ]
    for n, (by, src) in enumerate((
        (w + 1, corner_out.at[0, 1]), (w - 1, corner_out.at[0, 0]),
        (1 - w, corner_out.at[1, 1]), (-1 - w, corner_out.at[1, 0]),
    )):
        verts.append(remote(src, corner_in.at[n], corner_send.at[n], corner_recv.at[n], at(by, kern), valid(by)))

    loads[1].wait()
    loads[5].wait()
    taps = [[jnp.sum(kernels[c, k], keepdims=True) for k in range(3)] for c in range(2)]
    clear_part = sum(weight[k] * (taps[0][k] * taps[0][k] + taps[1][k] * taps[1][k]) for k in range(3))
    clear_in[x] = jnp.broadcast_to(clear_part, (8, BLK))
    clears = [
        remote(clear_in.at[x], clear_in.at[x], clear_send.at[d - 1], clear_recv.at[d - 1], peers[d])
        for d in FARTHEST_FIRST
    ]
    loads[2].wait()
    response_rows(kernels, tab, mid)
    response_cols(0, tab, mid, resp)

    for there, copy in zip((from_left_tile, from_right_tile), sides):
        pl.when(there)(copy.wait_recv)
    from_left, from_right = unpack_low(side_in[0]), unpack_high(side_in[1]) * right_link
    outer = ext[middle, pl.ds(0, BLK)]
    ext[middle, pl.ds(0, BLK)] = jnp.where(lane_all, from_left, outer)
    ext[middle, pl.ds(CORE, BLK)] = jnp.where(lane_all, outer, from_right)

    for there, copy in zip(from_vert + from_corner, verts):
        pl.when(there)(copy.wait_recv)
    down_above, right_above = (vert_in[0, pl.ds(2 * PART + r, 1), pl.ds(0, 1)] for r in (0, 1))
    right_below = vert_in[1, pl.ds(2 * PART + 1, 1), pl.ds(0, 1)]
    lane_part = low_lanes(PART)
    for n, (factor, beside) in enumerate(((down_above, right_above), (down_link, right_below))):
        edge = vert_in[n, pl.ds(0, PART), :]
        first, last = unpack_low(corner_in[2 * n]), unpack_high(corner_in[2 * n + 1])
        margin[x, n, :, pl.ds(0, BLK)] = jnp.where(lane_part, first, edge) * factor
        margin[x, n, :, pl.ds(BLK, BLK)] = vert_in[n, pl.ds(PART, PART), :] * factor
        margin[x, n, :, pl.ds(CORE, BLK)] = jnp.where(lane_part, edge, last * beside) * factor
    shares = [
        remote(margin.at[x], margin.at[x], share_send.at[d - 1], share_recv.at[d - 1], peers[d])
        for d in FARTHEST_FIRST
    ]
    for copy in clears:
        copy.wait_recv()
    clear_sum[...] = clear_in[0] + clear_in[1] + clear_in[2] + clear_in[3]
    clear_copy = remote(clear_sum, clear_far, cfar_send, cfar_recv, far)
    response_cols(1, tab, mid, resp)
    response_cols(2, tab, mid, resp)
    spectrum_cols(ext, [(HALO, CORE)], tab, mid)
    for copy in shares:
        copy.wait_recv()
    for q in range(4):
        ext[pl.ds(PART * q, PART), :] = margin[q, 0]
        ext[pl.ds(HALO + CORE + PART * q, PART), :] = margin[q, 1]
    spectrum_cols(ext, [(0, HALO), (HALO + CORE, HALO)], tab, mid)
    spectrum_rows(tab, mid, spec)
    for pair in PAIRS:
        field_rows(pair, resp, spec, tab, wide)

    scatter = []
    for h in range(2):
        field_cols(h, tab, wide, field)
        for q in range(4):
            p = 0.0
            for k in range(3):
                block = pl.ds(k * BLK + q * EIGHTH, EIGHTH)
                f_re, f_im = field[h, 0, block, :], field[h, 1, block, :]
                p = p + weight[k] * (f_re * f_re + f_im * f_im)
            power[h, q] = p
        scatter.append([
            remote(power.at[h, x_at[d]], power_in.at[h, d - 1], psc_send.at[h, d - 1], psc_recv.at[h, d - 1], peers[d])
            for d in FARTHEST_FIRST
        ])
    loads[3].wait()
    clear_copy.wait_recv()
    swaps = []
    for h in range(2):
        for copy in scatter[h]:
            copy.wait_recv()
        power_mine[h] = power[h, x] + power_in[h, 0] + power_in[h, 1] + power_in[h, 2]
        swaps.append(remote(power_mine.at[h], power_far.at[h], pfar_send.at[h], pfar_recv.at[h], far))
    finish_sends()
    gathers = []
    for h in range(2):
        swaps[h].wait_recv()
        power_all[h, x] = power_mine[h] + power_far[h]
        gathers.append([
            remote(power_all.at[h, x], power_all.at[h, x], pall_send.at[h, d - 1], pall_recv.at[h, d - 1], peers[d])
            for d in FARTHEST_FIRST
        ])
    clear = (clear_sum[...] + clear_far[...])[0:1, 0:1]
    for h in range(2):
        for copy in gathers[h]:
            copy.wait_recv()
        total = jnp.concatenate([power_all[h, q] for q in range(4)], axis=0)
        printed = 1.0 / (1.0 + jnp.exp(-STEEP * (total / clear - THRESH)))
        block = pl.ds(h * BLK, BLK)
        resist[0, block, :] = printed
        wanted = target[0, block, :].astype(F32)
        slope = (4.0 * STEEP) * (printed - wanted) * printed * (1.0 - printed) / clear
        source_cols(h, slope, weight, tab, field, wide)
    store = pltpu.make_async_copy(resist, out.at[0], store_sem.at[0])
    store.start()
    for pair in PAIRS:
        source_rows(pair, resp, tab, wide, acc)
    gradient_rows(acc, tab, mid)

    blocks = gradient_cols([(0, HALO), (HALO + CORE, HALO)], tab, mid)
    for c in range(3):
        for q, start in enumerate((64, 96, 32, 0)):
            halo_parts[q, :, pl.ds(c * BLK, BLK)] = blocks[c][start : start + 32]
    halo_scatter = [
        remote(halo_parts.at[x_at[d]], halo_in.at[d - 1], hsc_send.at[d - 1], hsc_recv.at[d - 1], peers[d])
        for d in FARTHEST_FIRST
    ]
    blocks = gradient_cols([(HALO, CORE)], tab, mid)
    for n, c in enumerate((0, 2, 1)):
        for q in range(4):
            core_parts[q, n] = blocks[c][q * QUARTER : (q + 1) * QUARTER]
    outer_blocks = pl.ds(0, 2)
    core_scatter = [
        remote(
            core_parts.at[x_at[d], outer_blocks], core_in.at[d - 1, outer_blocks],
            gsc_send.at[d - 1], gsc_recv.at[d - 1], peers[d],
        )
        for d in FARTHEST_FIRST
    ]
    middle_scatter = [
        remote(core_parts.at[x_at[d], 2], core_in.at[d - 1, 2], gmid_send.at[d - 1], gmid_recv.at[d - 1], peers[d])
        for d in FARTHEST_FIRST
    ]

    low_x = x < 2
    for copy in halo_scatter:
        copy.wait_recv()
    is_low = jnp.where(low_x, 1.0, 0.0)
    down_factor = is_low * down_link + (1.0 - is_low) * down_above
    right_factor = is_low * right_below + (1.0 - is_low) * right_above
    total = (halo_parts[x] + halo_in[0] + halo_in[1] + halo_in[2]) * down_factor
    first, last, fold_out[...] = core_blocks(total)
    bend_out[0] = pack_high(first)
    bend_out[1] = pack_low(last) * right_factor
    slot = jnp.where((x == 1) | (x == 2), 1, 0)
    step = jnp.where(low_x, GRID_W, -GRID_W)
    owner = jnp.where(low_x, 0, 6) + half
    remote(fold_out, fold_in.at[slot], fold_send, fold_recv.at[slot], at(step, owner), valid(step))
    for n, by in enumerate((step - 1, step + 1)):
        remote(
            bend_out.at[n], bend_in.at[slot, n], bend_send.at[n], bend_recv.at[slot, n], at(by, owner), valid(by)
        )

    for copy in core_scatter:
        copy.wait_recv()
    first, last = (
        pltpu.roll(core_parts[x, n] + core_in[0, n] + core_in[1, n] + core_in[2, n], HALO, 1) for n in (0, 1)
    )
    edge_out[0] = pack_low(last) * right_link
    edge_out[1] = pack_high(first)
    edges = [
        remote(edge_out.at[0], edge_in.at[0], edge_send.at[0], edge_recv.at[0], at(1, kern), valid(1)),
        remote(edge_out.at[1], edge_in.at[1], edge_send.at[1], edge_recv.at[1], at(-1, kern), valid(-1)),
    ]

    for copy in middle_scatter:
        copy.wait_recv()
    between = pltpu.roll(core_parts[x, 2] + core_in[0, 2] + core_in[1, 2] + core_in[2, 2], HALO, 1)
    lane_edge = low_lanes(QUARTER)
    whole[...] = lanes(jnp.where(lane_edge, first, between), jnp.where(lane_edge, between, last))
    takes = (x == 0) | (x == 3)
    back = jnp.where(x == 0, -GRID_W, GRID_W)
    lane_fold = low_lanes(32)
    for s in range(2):
        arrivals = (
            (valid(back), fold_out, fold_in.at[s], fold_send, fold_recv.at[s]),
            (valid(back + 1), bend_out.at[0], bend_in.at[s, 0], bend_send.at[0], bend_recv.at[s, 0]),
            (valid(back - 1), bend_out.at[1], bend_in.at[s, 1], bend_send.at[1], bend_recv.at[s, 1]),
        )
        for there, src, dst, send, recv in arrivals:
            copy = pltpu.make_async_remote_copy(
                src_ref=src, dst_ref=dst, send_sem=send, recv_sem=recv, device_id=far, device_id_type=MESH
            )
            clear_unless(takes & there, dst)
            pl.when(takes & there)(copy.wait_recv)
        block = pl.ds(32 * s, 32)
        from_left = jnp.where(lane_fold, unpack_low(bend_in[s, 1]), 0.0)
        from_right = jnp.where(lane_fold, 0.0, unpack_high(bend_in[s, 0])) * right_link
        whole[block, :] += fold_in[s] + lanes(from_left, from_right)

    for there, copy in zip((from_left_tile, from_right_tile), edges):
        pl.when(there)(copy.wait_recv)
    from_left = jnp.where(lane_edge, unpack_low(edge_in[0]), 0.0)
    from_right = jnp.where(lane_edge, 0.0, unpack_high(edge_in[1])) * right_link
    partial = whole[...] + lanes(from_left, from_right)
    swaps = []
    for h in range(2):
        mine[h] = partial[h * 32 : (h + 1) * 32]
        swaps.append(remote(mine.at[h], other.at[h], gfar_send.at[h], gfar_recv.at[h], far))
    finish_sends()
    finals = []
    stores = [store]
    for h in range(2):
        swaps[h].wait_recv()
        gathered[h] = mine[h] + other[h]
        place = out.at[1, 0, pl.ds(pl.multiple_of(QUARTER * x + 32 * h, 32), 32)]
        finals += [
            remote(gathered.at[h], place, all_send.at[h, d - 1], all_recv.at[h, d - 1], peers[d])
            for d in FARTHEST_FIRST
        ]
        stores.append(pltpu.make_async_copy(gathered.at[h], place, store_sem.at[1 + h]))
        stores[-1].start()
    for copy in finals:
        copy.wait_recv()
    finish_sends()
    for copy in stores:
        copy.wait()


def store_kernel(both, resist_out, grad_out, held, load_sem, store_sem):
    pieces = [(n, pl.ds(q * BLK, BLK)) for n in range(2) for q in range(2)]
    loads = [
        pltpu.make_async_copy(both.at[n, 0, block], held.at[n, 0, block], load_sem.at[i])
        for i, (n, block) in enumerate(pieces)
    ]
    for copy in loads:
        copy.start()
    stores = []
    for i, (n, block) in enumerate(pieces):
        loads[i].wait()
        into = (resist_out, grad_out)[n]
        stores.append(pltpu.make_async_copy(held.at[n, 0, block], into.at[0, block], store_sem.at[i]))
        stores[-1].start()
    for copy in stores:
        copy.wait()


def body(mask, kernels, weight, link, target):
    anywhere = pl.BlockSpec(memory_space=pl.ANY)
    dma = pltpu.SemaphoreType.DMA
    f32 = lambda *shape: pltpu.VMEM(shape, F32)
    buffers = [
        f32(1, CORE, CORE), f32(2, 3, BLK, BLK), pltpu.VMEM((1, CORE, CORE), jnp.int32),
        pltpu.VMEM((2, 2, 3, CORE, CORE), BF16),
        f32(2, EXTENT, EXTENT), f32(2, CORE, 3 * EXTENT), f32(2, EXTENT, 3 * EXTENT), f32(2, EXTENT, EXTENT),
        f32(2, 2, EXTENT, CORE), f32(2, EXTENT, EXTENT), f32(EXTENT, EXTENT), f32(1, CORE, CORE),
        f32(2, BLK, BLK), f32(2, BLK, BLK), f32(2, 2 * PART + 8, BLK), f32(2, 2 * PART + 8, BLK),
        f32(2, 2, PART // 2, BLK), f32(4, PART // 2, BLK), f32(4, 2, PART, EXTENT),
        f32(4, 8, BLK), f32(8, BLK), f32(8, BLK),
        f32(2, 4, EIGHTH, CORE), f32(2, 3, EIGHTH, CORE), f32(2, EIGHTH, CORE), f32(2, EIGHTH, CORE),
        f32(2, 4, EIGHTH, CORE),
        f32(4, 32, EXTENT), f32(3, 32, EXTENT), f32(4, 3, QUARTER, BLK), f32(3, 3, QUARTER, BLK),
        f32(32, CORE), f32(2, 32, CORE), f32(2, 16, BLK), f32(2, 2, 16, BLK),
        f32(2, 32, BLK), f32(2, 32, BLK), f32(QUARTER, CORE),
        f32(2, 32, CORE), f32(2, 32, CORE), f32(2, 32, CORE),
    ]
    sems = [pltpu.SMEM((3,), F32), pltpu.SMEM((1, 2), jnp.int32), dma((6,)), dma((3,))] + [dma((2,))] * 4 + [dma((4,))] * 2 + [dma((3,))] * 2
    sems += [dma((3,))] * 2 + [dma] * 2
    sems += [dma((2, 3))] * 2 + [dma((2,))] * 2 + [dma((2, 3))] * 2
    sems += [dma((3,))] * 6 + [dma, dma((2,)), dma((2,)), dma((2, 2))]
    sems += [dma((2,))] * 4 + [dma((2, 3))] * 2
    both = pl.pallas_call(
        body_kernel,
        out_shape=jax.ShapeDtypeStruct((2, 1, CORE, CORE), F32),
        in_specs=[anywhere] * 6,
        out_specs=anywhere,
        scratch_shapes=buffers + sems,
        compiler_params=pltpu.CompilerParams(
            collective_id=0, has_side_effects=True, vmem_limit_bytes=60 * 2**20
        ),
    )(mask, kernels, target, jnp.asarray(dft_tables()), weight, link)
    out = jax.ShapeDtypeStruct((1, CORE, CORE), F32)
    return pl.pallas_call(
        store_kernel,
        out_shape=(out, out),
        in_specs=[anywhere],
        out_specs=(anywhere, anywhere),
        scratch_shapes=[f32(2, 1, CORE, CORE), dma((4,)), dma((4,))],
        compiler_params=pltpu.CompilerParams(vmem_limit_bytes=60 * 2**20),
    )(both)


def solution(mesh):
    in_specs = (
        P("tile", None, None),
        P(None, "kern", None, None),
        P("kern"),
        P("tile", None),
        P("tile", None, None),
    )
    out_specs = (P("tile", None, None), P("tile", None, None))
    return jax.shard_map(body, mesh=mesh, in_specs=in_specs, out_specs=out_specs, check_vma=False)
```

```python
import functools
import math

import jax
import jax.numpy as jnp
import ml_dtypes
import numpy as np
from jax import lax
from jax.experimental import pallas as pl
from jax.experimental.pallas import tpu as pltpu
from jax.sharding import PartitionSpec as P

GRID_W = 8
STEEP = 20.0
THRESH = 0.33
BLK = 128
EXTENT = 3 * BLK
CORE = 2 * BLK
HALO = BLK // 2
HALF_SQRT3 = math.sqrt(3.0) / 2.0
MESH = pl.DeviceIdType.MESH
F32 = jnp.float32
BF16 = jnp.bfloat16


def dft_tables():
    place = np.arange(BLK)
    groups = (3 * place, 3 * place + 1, -(3 * place + 1))
    mats = []
    for freq in groups:
        angle = 2.0 * np.pi * (np.outer(place, freq) % EXTENT) / EXTENT
        c, s = np.cos(angle), -np.sin(angle)
        mats.append(np.block([[c, s], [-s, c]]))
    fwd = np.stack(mats).astype(np.float32)
    both = np.stack([fwd, fwd.transpose(0, 2, 1)])
    high = both.astype(ml_dtypes.bfloat16)
    low = (both - high.astype(np.float32)).astype(ml_dtypes.bfloat16)
    return np.stack([high, low])


def split(x):
    high = x.astype(BF16)
    return high, (x - high.astype(F32)).astype(BF16)


def dot(a, b):
    return jnp.dot(a, b, preferred_element_type=F32)


def mul_right(x, high, low):
    xh, xl = split(x)
    n = high.shape[1]
    both = dot(xh, jnp.concatenate([high, low], axis=1))
    return both[:, :n] + (both[:, n:] + dot(xl, high))


def mul_left(high, low, x):
    xh, xl = split(x)
    n = x.shape[1]
    both = dot(high, jnp.concatenate([xh, xl], axis=1))
    return both[:, :n] + (both[:, n:] + dot(low, xh))


def fwd_mat(tab, g):
    return tab[0, 0, g], tab[1, 0, g]


def t_mat(tab, g):
    return tab[0, 1, g], tab[1, 1, g]


def lanes(re, im):
    return jnp.concatenate([re, im], axis=1)


def rows(re, im):
    return jnp.concatenate([re, im], axis=0)


def response_rows(kernels, tab, mid):
    scale = 1.0 / (EXTENT * EXTENT)
    re = jnp.concatenate([kernels[0, k] for k in range(3)], axis=1) * scale
    im = jnp.concatenate([kernels[1, k] for k in range(3)], axis=1) * -scale
    taps = rows(re, im)
    for g in range(3):
        out = mul_left(*t_mat(tab, g), taps)
        mid[0, pl.ds(g * BLK, BLK), :] = out[:BLK]
        mid[1, pl.ds(g * BLK, BLK), :] = out[BLK:]


def response_cols(k, tab, mid, resp):
    cols = pl.ds(k * BLK, BLK)
    x = lanes(mid[0, :, cols], mid[1, :, cols])
    for g in range(3):
        out = mul_right(x, *fwd_mat(tab, g))
        resp[0, :, pl.ds(k * EXTENT + g * BLK, BLK)] = out[:, :BLK]
        resp[1, :, pl.ds(k * EXTENT + g * BLK, BLK)] = out[:, BLK:]


def spectrum_cols(ext, places, tab, mid):
    x0, x1, x2 = (
        jnp.concatenate([ext[pl.ds(s, n), pl.ds(j * BLK, BLK)] for s, n in places], axis=0) for j in range(3)
    )
    z0 = x0 + x1 + x2
    z1 = lanes(x0 - 0.5 * (x1 + x2), HALF_SQRT3 * (x2 - x1))
    h0, l0 = fwd_mat(tab, 0)
    outs = (mul_right(z0, h0[:BLK], l0[:BLK]), mul_right(z1, *fwd_mat(tab, 1)))
    for g, out in enumerate(outs):
        at = 0
        for s, n in places:
            mid[0, pl.ds(s, n), pl.ds(g * BLK, BLK)] = out[at : at + n, :BLK]
            mid[1, pl.ds(s, n), pl.ds(g * BLK, BLK)] = out[at : at + n, BLK:]
            at += n


def spectrum_rows(tab, mid, spec):
    two = pl.ds(0, CORE)
    a_re, b_re, c_re = (mid[0, pl.ds(j * BLK, BLK), two] for j in range(3))
    a_im, b_im, c_im = (mid[1, pl.ds(j * BLK, BLK), two] for j in range(3))
    s_re, s_im = b_re + c_re, b_im + c_im
    e_re, e_im = a_re - 0.5 * s_re, a_im - 0.5 * s_im
    f_re, f_im = HALF_SQRT3 * (b_re - c_re), HALF_SQRT3 * (b_im - c_im)
    z_re, z_im = a_re + s_re, a_im + s_im
    z_re = lanes(z_re, z_re[:, BLK:])
    z_im = lanes(z_im, -z_im[:, BLK:])
    out = mul_left(*t_mat(tab, 0), rows(z_re, z_im))
    spec[0, pl.ds(0, BLK), :] = out[:BLK]
    spec[1, pl.ds(0, BLK), :] = out[BLK:]
    out1 = mul_left(*t_mat(tab, 1), rows(e_re + f_im, e_im - f_re))
    out2 = mul_left(*t_mat(tab, 2), rows(e_re - f_im, e_im + f_re))
    spec[0, pl.ds(BLK, BLK), :] = lanes(out1[:BLK], out2[:BLK, BLK:])
    spec[1, pl.ds(BLK, BLK), :] = lanes(out1[BLK:], -out2[BLK:, BLK:])
    spec[0, pl.ds(2 * BLK, BLK), :] = lanes(out2[:BLK], out1[:BLK, BLK:])
    spec[1, pl.ds(2 * BLK, BLK), :] = lanes(out2[BLK:], -out1[BLK:, BLK:])


PAIRS = [[(b // 3, b % 3) for b in range(s, min(s + 4, 9))] for s in range(0, 9, 4)]


def field_rows(pair, resp, spec, tab, mid):
    width = len(pair) * BLK
    start = (pair[0][0] * 3 + pair[0][1]) * BLK
    cols = pl.ds(start, width)
    t = []
    for g in range(3):
        block = pl.ds(g * BLK, BLK)
        q_re, q_im = resp[0, block, cols], resp[1, block, cols]
        e_re = jnp.concatenate([spec[0, block, pl.ds(f * BLK, BLK)] for _, f in pair], axis=1)
        e_im = jnp.concatenate([spec[1, block, pl.ds(f * BLK, BLK)] for _, f in pair], axis=1)
        x = rows(e_re * q_re + e_im * q_im, e_im * q_re - e_re * q_im)
        t.append(mul_left(*fwd_mat(tab, g), x))
    s, d = t[1] + t[2], HALF_SQRT3 * (t[1] - t[2])
    first, e = t[0] + s, t[0] - 0.5 * s
    upper, lower = pl.ds(0, BLK), pl.ds(BLK, BLK)
    mid[0, upper, cols] = first[:BLK]
    mid[1, upper, cols] = first[BLK:]
    mid[0, lower, cols] = e[:BLK] - d[BLK:]
    mid[1, lower, cols] = e[BLK:] + d[:BLK]


def field_cols(h, tab, mid, field):
    t = []
    for g in range(3):
        x = jnp.concatenate(
            [
                lanes(*(mid[c, pl.ds(h * BLK, BLK), pl.ds(k * EXTENT + g * BLK, BLK)] for c in range(2)))
                for k in range(3)
            ],
            axis=0,
        )
        t.append(mul_right(x, *t_mat(tab, g)))
    s, d = t[1] + t[2], HALF_SQRT3 * (t[1] - t[2])
    first, e = t[0] + s, t[0] - 0.5 * s
    field[h, 0] = lanes(first[:, :BLK], e[:, :BLK] - d[:, BLK:])
    field[h, 1] = lanes(first[:, BLK:], e[:, BLK:] + d[:, :BLK])


def source_cols(h, slope, weight, tab, field, mid):
    scaled = jnp.concatenate([weight[k] * slope for k in range(3)], axis=0)
    s_re, s_im = scaled * field[h, 0], scaled * field[h, 1]
    a_re, a_im, b_re, b_im = s_re[:, :BLK], s_im[:, :BLK], s_re[:, BLK:], s_im[:, BLK:]
    e_re, e_im = a_re - 0.5 * b_re, a_im - 0.5 * b_im
    f_re, f_im = HALF_SQRT3 * b_re, HALF_SQRT3 * b_im
    z = (
        lanes(a_re + b_re, a_im + b_im),
        lanes(e_re + f_im, e_im - f_re),
        lanes(e_re - f_im, e_im + f_re),
    )
    for g in range(3):
        out = mul_right(z[g], *fwd_mat(tab, g))
        for k in range(3):
            cols = pl.ds(k * EXTENT + g * BLK, BLK)
            mid[0, pl.ds(h * BLK, BLK), cols] = out[k * BLK : (k + 1) * BLK, :BLK]
            mid[1, pl.ds(h * BLK, BLK), cols] = out[k * BLK : (k + 1) * BLK, BLK:]


def source_rows(pair, resp, tab, mid, acc):
    width = len(pair) * BLK
    start = (pair[0][0] * 3 + pair[0][1]) * BLK
    cols = pl.ds(start, width)
    upper, lower = pl.ds(0, BLK), pl.ds(BLK, BLK)
    a_re, a_im, b_re, b_im = mid[0, upper, cols], mid[1, upper, cols], mid[0, lower, cols], mid[1, lower, cols]
    e_re, e_im = a_re - 0.5 * b_re, a_im - 0.5 * b_im
    f_re, f_im = HALF_SQRT3 * b_re, HALF_SQRT3 * b_im
    z = (
        rows(a_re + b_re, a_im + b_im),
        rows(e_re + f_im, e_im - f_re),
        rows(e_re - f_im, e_im + f_re),
    )
    for g in range(3):
        out = mul_left(*t_mat(tab, g), z[g])
        block = pl.ds(g * BLK, BLK)
        o_re, o_im = out[:BLK], out[BLK:]
        q_re, q_im = resp[0, block, cols], resp[1, block, cols]
        p_re, p_im = o_re * q_re - o_im * q_im, o_re * q_im + o_im * q_re
        for n, (k, f) in enumerate(pair):
            into = pl.ds(f * BLK, BLK)
            part = slice(n * BLK, (n + 1) * BLK)
            if k == 0:
                acc[0, block, into] = p_re[:, part]
                acc[1, block, into] = p_im[:, part]
            else:
                acc[0, block, into] += p_re[:, part]
                acc[1, block, into] += p_im[:, part]


def gradient_rows(acc, tab, mid):
    p0, p1, p2 = (pl.ds(g * BLK, BLK) for g in range(3))
    t0 = mul_left(*fwd_mat(tab, 0), rows(acc[0, p0, :], acc[1, p0, :]))
    t0_re, t0_im = t0[:BLK], t0[BLK:]
    t0_re = lanes(t0_re[:, :BLK], t0_re[:, BLK:CORE] + t0_re[:, CORE:])
    t0_im = lanes(t0_im[:, :BLK], t0_im[:, BLK:CORE] - t0_im[:, CORE:])
    x_re = lanes(acc[0, p1, p0], acc[0, p1, p1] + acc[0, p2, p2])
    x_im = lanes(acc[1, p1, p0], acc[1, p1, p1] - acc[1, p2, p2])
    t1 = mul_left(*fwd_mat(tab, 1), rows(x_re, x_im))
    x_re = lanes(acc[0, p2, p0], acc[0, p2, p1] + acc[0, p1, p2])
    x_im = lanes(acc[1, p2, p0], acc[1, p2, p1] - acc[1, p1, p2])
    t2 = mul_left(*fwd_mat(tab, 2), rows(x_re, x_im))
    s, d = t1 + t2, HALF_SQRT3 * (t1 - t2)
    e_re, e_im = t0_re - 0.5 * s[:BLK], t0_im - 0.5 * s[BLK:]
    two = pl.ds(0, CORE)
    mid[0, p0, two], mid[1, p0, two] = t0_re + s[:BLK], t0_im + s[BLK:]
    mid[0, p1, two], mid[1, p1, two] = e_re - d[BLK:], e_im + d[:BLK]
    mid[0, p2, two], mid[1, p2, two] = e_re + d[BLK:], e_im - d[:BLK]


def gradient_cols(places, tab, mid):
    h0, l0 = t_mat(tab, 0)
    part = lambda c, g: jnp.concatenate([mid[c, pl.ds(s, n), pl.ds(g * BLK, BLK)] for s, n in places], axis=0)
    r0 = mul_right(lanes(part(0, 0), part(1, 0)), h0[:, :BLK], l0[:, :BLK])
    r1 = mul_right(lanes(part(0, 1), part(1, 1)), *t_mat(tab, 1))
    e, d = r0 - 0.5 * r1[:, :BLK], HALF_SQRT3 * r1[:, BLK:]
    return r0 + r1[:, :BLK], e - d, e + d


QUARTER = CORE // 4
EIGHTH = CORE // 8
PART = HALO // 4
FARTHEST_FIRST = (2, 3, 1)


def low_lanes(n):
    return lax.broadcasted_iota(jnp.int32, (n, BLK), 1) < HALO


def pack_low(x):
    n = x.shape[0] // 2
    return jnp.where(low_lanes(n), x[:n], pltpu.roll(x[n:], HALO, 1))


def pack_high(x):
    n = x.shape[0] // 2
    return jnp.where(low_lanes(n), pltpu.roll(x[:n], HALO, 1), x[n:])


def unpack_low(x):
    return rows(x, pltpu.roll(x, HALO, 1))


def unpack_high(x):
    return rows(pltpu.roll(x, HALO, 1), x)


def core_blocks(x):
    c0, c1, c2 = (pltpu.roll(x[:, j * BLK : (j + 1) * BLK], HALO, 1) for j in range(3))
    low = low_lanes(x.shape[0])
    return c0, c2, lanes(jnp.where(low, c0, c1), jnp.where(low, c1, c2))


def body_kernel(
    mask_hbm, kernels_hbm, target_hbm, tab_hbm, weight_hbm, link_hbm, out,
    mask, kernels, target, tab, mid, wide, resp, spec, field, acc, ext, resist,
    side_out, side_in, vert_out, vert_in, corner_out, corner_in, margin,
    clear_in, clear_sum, clear_far, power, power_in, power_mine, power_far, power_all,
    halo_parts, halo_in, core_parts, core_in, fold_out, fold_in, bend_out, bend_in, edge_out, edge_in, whole,
    mine, other, gathered,
    weight, link, load_sem, store_sem, side_send, side_recv, vert_send, vert_recv, corner_send, corner_recv, share_send, share_recv,
    clear_send, clear_recv, cfar_send, cfar_recv,
    psc_send, psc_recv, pfar_send, pfar_recv, pall_send, pall_recv,
    hsc_send, hsc_recv, gsc_send, gsc_recv, gmid_send, gmid_recv, fold_send, fold_recv, bend_send, bend_recv,
    edge_send, edge_recv, gfar_send, gfar_recv, all_send, all_recv,
):
    tile = lax.axis_index("tile")
    kern = lax.axis_index("kern")
    tiles = lax.axis_size("tile")
    x = kern // 2
    half = kern % 2
    column = (tile + GRID_W // 2) % GRID_W
    right_ok = jnp.where((column < GRID_W - 1) & (tile + 1 < tiles), 1.0, 0.0)
    down_ok = jnp.where(tile + GRID_W < tiles, 1.0, 0.0)

    def valid(tile_by):
        return (tile + tile_by >= 0) & (tile + tile_by < tiles)

    def at(tile_by, kern_index):
        return {"tile": (tile + tile_by + tiles) % tiles, "kern": kern_index}

    far = at(0, 2 * x + 1 - half)
    x_at = [(x + d) % 4 for d in range(4)]
    peers = [at(0, 2 * x_at[d] + half) for d in range(4)]
    sign = 2 * (x % 2) - 1
    crossed = 2 * (x + 1 - 2 * (x % 2)) + half
    near_tiles = [1, -1] + [s * GRID_W + e for s in (1, -1) for e in (-1, 0, 1)]
    partners = [(valid(by), at(by, kern)) for by in near_tiles]
    partners += [(valid(by), at(by, crossed)) for by in (sign * GRID_W + e for e in (-1, 0, 1))]

    barrier = pltpu.get_barrier_semaphore()
    expected = 4
    for there, one in partners:
        expected = expected + there.astype(jnp.int32)

        @pl.when(there)
        def _():
            pl.semaphore_signal(barrier, inc=1, device_id=one, device_id_type=MESH)

    for one in [far] + peers[1:]:
        pl.semaphore_signal(barrier, inc=1, device_id=one, device_id_type=MESH)

    loads = [
        pltpu.make_async_copy(src, dst, load_sem.at[n])
        for n, (src, dst) in enumerate((
            (mask_hbm, mask), (kernels_hbm, kernels), (tab_hbm, tab), (target_hbm, target),
            (link_hbm, link), (weight_hbm, weight),
        ))
    ]
    for copy in (loads[0], loads[4], loads[5], loads[1], loads[2], loads[3]):
        copy.start()
    started = []

    def remote(src, dst, send, recv, device, there=None):
        copy = pltpu.make_async_remote_copy(
            src_ref=src, dst_ref=dst, send_sem=send, recv_sem=recv, device_id=device, device_id_type=MESH
        )
        if there is None:
            copy.start()
        else:
            pl.when(there)(copy.start)
        started.append((there, copy))
        return copy

    def finish_sends():
        for there, copy in started:
            if there is None:
                copy.wait_send()
            else:
                pl.when(there)(copy.wait_send)
        started.clear()

    def clear_unless(there, *refs):
        @pl.when(jnp.logical_not(there))
        def _():
            for ref in refs:
                ref[...] = jnp.zeros(ref.shape, F32)

    from_left_tile, from_right_tile = valid(-1), valid(1)
    from_vert = [valid(-GRID_W), valid(GRID_W)]
    from_corner = [valid(-GRID_W - 1), valid(-GRID_W + 1), valid(GRID_W - 1), valid(GRID_W + 1)]
    clear_unless(from_left_tile, side_in.at[0], edge_in.at[0])
    clear_unless(from_right_tile, side_in.at[1], edge_in.at[1])
    for n in range(2):
        clear_unless(from_vert[n], vert_in.at[n])
    for n in range(4):
        clear_unless(from_corner[n], corner_in.at[n])

    loads[0].wait()
    a0, a1 = mask[0, :, pl.ds(0, BLK)], mask[0, :, pl.ds(BLK, BLK)]
    r0, r1 = pltpu.roll(a0, HALO, 1), pltpu.roll(a1, HALO, 1)
    lane_all = low_lanes(CORE)
    outer = jnp.where(lane_all, r1, r0)
    inner = jnp.where(lane_all, r0, r1)
    middle = pl.ds(HALO, CORE)
    ext[middle, pl.ds(BLK, BLK)] = inner
    ext[middle, pl.ds(0, BLK)] = outer
    loads[4].wait()
    right_link = link[0, 0].astype(F32) * right_ok
    down_link = link[0, 1].astype(F32) * down_ok
    flag = lax.broadcasted_iota(jnp.int32, (8, BLK), 0) < 1
    for n, first in enumerate((CORE - HALO, 0)):
        block = pl.ds(pl.multiple_of(HALO + first + PART * x, PART), PART)
        outer_part = ext[block, pl.ds(0, BLK)]
        vert_out[n, pl.ds(0, PART), :] = outer_part
        vert_out[n, pl.ds(PART, PART), :] = ext[block, pl.ds(BLK, BLK)]
        vert_out[n, pl.ds(2 * PART, 8), :] = jnp.where(flag, down_link, right_link)
        corner_out[n, 0] = pack_high(outer_part)
        corner_out[n, 1] = pack_low(outer_part) * right_link
    side_out[0] = pack_low(outer) * right_link
    side_out[1] = pack_high(outer)

    pl.semaphore_wait(barrier, expected)
    w = GRID_W
    sides = [
        remote(side_out.at[0], side_in.at[0], side_send.at[0], side_recv.at[0], at(1, kern), valid(1)),
        remote(side_out.at[1], side_in.at[1], side_send.at[1], side_recv.at[1], at(-1, kern), valid(-1)),
    ]
    verts = [
        remote(vert_out.at[0], vert_in.at[0], vert_send.at[0], vert_recv.at[0], at(w, kern), valid(w)),
        remote(vert_out.at[1], vert_in.at[1], vert_send.at[1], vert_recv.at[1], at(-w, kern), valid(-w)),
    ]
    for n, (by, src) in enumerate((
        (w + 1, corner_out.at[0, 1]), (w - 1, corner_out.at[0, 0]),
        (1 - w, corner_out.at[1, 1]), (-1 - w, corner_out.at[1, 0]),
    )):
        verts.append(remote(src, corner_in.at[n], corner_send.at[n], corner_recv.at[n], at(by, kern), valid(by)))

    loads[1].wait()
    loads[5].wait()
    taps = [[jnp.sum(kernels[c, k], keepdims=True) for k in range(3)] for c in range(2)]
    clear_part = sum(weight[k] * (taps[0][k] * taps[0][k] + taps[1][k] * taps[1][k]) for k in range(3))
    clear_in[x] = jnp.broadcast_to(clear_part, (8, BLK))
    clears = [
        remote(clear_in.at[x], clear_in.at[x], clear_send.at[d - 1], clear_recv.at[d - 1], peers[d])
        for d in FARTHEST_FIRST
    ]
    loads[2].wait()
    response_rows(kernels, tab, mid)
    response_cols(0, tab, mid, resp)

    for there, copy in zip((from_left_tile, from_right_tile), sides):
        pl.when(there)(copy.wait_recv)
    from_left, from_right = unpack_low(side_in[0]), unpack_high(side_in[1]) * right_link
    outer = ext[middle, pl.ds(0, BLK)]
    ext[middle, pl.ds(0, BLK)] = jnp.where(lane_all, from_left, outer)
    ext[middle, pl.ds(CORE, BLK)] = jnp.where(lane_all, outer, from_right)

    for there, copy in zip(from_vert + from_corner, verts):
        pl.when(there)(copy.wait_recv)
    down_above, right_above = (vert_in[0, pl.ds(2 * PART + r, 1), pl.ds(0, 1)] for r in (0, 1))
    right_below = vert_in[1, pl.ds(2 * PART + 1, 1), pl.ds(0, 1)]
    lane_part = low_lanes(PART)
    for n, (factor, beside) in enumerate(((down_above, right_above), (down_link, right_below))):
        edge = vert_in[n, pl.ds(0, PART), :]
        first, last = unpack_low(corner_in[2 * n]), unpack_high(corner_in[2 * n + 1])
        margin[x, n, :, pl.ds(0, BLK)] = jnp.where(lane_part, first, edge) * factor
        margin[x, n, :, pl.ds(BLK, BLK)] = vert_in[n, pl.ds(PART, PART), :] * factor
        margin[x, n, :, pl.ds(CORE, BLK)] = jnp.where(lane_part, edge, last * beside) * factor
    shares = [
        remote(margin.at[x], margin.at[x], share_send.at[d - 1], share_recv.at[d - 1], peers[d])
        for d in FARTHEST_FIRST
    ]
    for copy in clears:
        copy.wait_recv()
    clear_sum[...] = clear_in[0] + clear_in[1] + clear_in[2] + clear_in[3]
    clear_copy = remote(clear_sum, clear_far, cfar_send, cfar_recv, far)
    response_cols(1, tab, mid, resp)
    response_cols(2, tab, mid, resp)
    spectrum_cols(ext, [(HALO, CORE)], tab, mid)
    for copy in shares:
        copy.wait_recv()
    for q in range(4):
        ext[pl.ds(PART * q, PART), :] = margin[q, 0]
        ext[pl.ds(HALO + CORE + PART * q, PART), :] = margin[q, 1]
    spectrum_cols(ext, [(0, HALO), (HALO + CORE, HALO)], tab, mid)
    spectrum_rows(tab, mid, spec)
    for pair in PAIRS:
        field_rows(pair, resp, spec, tab, wide)

    scatter = []
    for h in range(2):
        field_cols(h, tab, wide, field)
        for q in range(4):
            p = 0.0
            for k in range(3):
                block = pl.ds(k * BLK + q * EIGHTH, EIGHTH)
                f_re, f_im = field[h, 0, block, :], field[h, 1, block, :]
                p = p + weight[k] * (f_re * f_re + f_im * f_im)
            power[h, q] = p
        scatter.append([
            remote(power.at[h, x_at[d]], power_in.at[h, d - 1], psc_send.at[h, d - 1], psc_recv.at[h, d - 1], peers[d])
            for d in FARTHEST_FIRST
        ])
    loads[3].wait()
    clear_copy.wait_recv()
    swaps = []
    for h in range(2):
        for copy in scatter[h]:
            copy.wait_recv()
        power_mine[h] = power[h, x] + power_in[h, 0] + power_in[h, 1] + power_in[h, 2]
        swaps.append(remote(power_mine.at[h], power_far.at[h], pfar_send.at[h], pfar_recv.at[h], far))
    finish_sends()
    gathers = []
    for h in range(2):
        swaps[h].wait_recv()
        power_all[h, x] = power_mine[h] + power_far[h]
        gathers.append([
            remote(power_all.at[h, x], power_all.at[h, x], pall_send.at[h, d - 1], pall_recv.at[h, d - 1], peers[d])
            for d in FARTHEST_FIRST
        ])
    clear = (clear_sum[...] + clear_far[...])[0:1, 0:1]
    for h in range(2):
        for copy in gathers[h]:
            copy.wait_recv()
        total = jnp.concatenate([power_all[h, q] for q in range(4)], axis=0)
        printed = 1.0 / (1.0 + jnp.exp(-STEEP * (total / clear - THRESH)))
        block = pl.ds(h * BLK, BLK)
        resist[0, block, :] = printed
        wanted = target[0, block, :].astype(F32)
        slope = (4.0 * STEEP) * (printed - wanted) * printed * (1.0 - printed) / clear
        source_cols(h, slope, weight, tab, field, wide)
    store = pltpu.make_async_copy(resist, out.at[0], store_sem.at[0])
    store.start()
    for pair in PAIRS:
        source_rows(pair, resp, tab, wide, acc)
    gradient_rows(acc, tab, mid)

    blocks = gradient_cols([(0, HALO), (HALO + CORE, HALO)], tab, mid)
    for c in range(3):
        for q, start in enumerate((64, 96, 32, 0)):
            halo_parts[q, :, pl.ds(c * BLK, BLK)] = blocks[c][start : start + 32]
    halo_scatter = [
        remote(halo_parts.at[x_at[d]], halo_in.at[d - 1], hsc_send.at[d - 1], hsc_recv.at[d - 1], peers[d])
        for d in FARTHEST_FIRST
    ]
    blocks = gradient_cols([(HALO, CORE)], tab, mid)
    for n, c in enumerate((0, 2, 1)):
        for q in range(4):
            core_parts[q, n] = blocks[c][q * QUARTER : (q + 1) * QUARTER]
    outer_blocks = pl.ds(0, 2)
    core_scatter = [
        remote(
            core_parts.at[x_at[d], outer_blocks], core_in.at[d - 1, outer_blocks],
            gsc_send.at[d - 1], gsc_recv.at[d - 1], peers[d],
        )
        for d in FARTHEST_FIRST
    ]
    middle_scatter = [
        remote(core_parts.at[x_at[d], 2], core_in.at[d - 1, 2], gmid_send.at[d - 1], gmid_recv.at[d - 1], peers[d])
        for d in FARTHEST_FIRST
    ]

    low_x = x < 2
    for copy in halo_scatter:
        copy.wait_recv()
    is_low = jnp.where(low_x, 1.0, 0.0)
    down_factor = is_low * down_link + (1.0 - is_low) * down_above
    right_factor = is_low * right_below + (1.0 - is_low) * right_above
    total = (halo_parts[x] + halo_in[0] + halo_in[1] + halo_in[2]) * down_factor
    first, last, fold_out[...] = core_blocks(total)
    bend_out[0] = pack_high(first)
    bend_out[1] = pack_low(last) * right_factor
    slot = jnp.where((x == 1) | (x == 2), 1, 0)
    step = jnp.where(low_x, GRID_W, -GRID_W)
    owner = jnp.where(low_x, 0, 6) + half
    remote(fold_out, fold_in.at[slot], fold_send, fold_recv.at[slot], at(step, owner), valid(step))
    for n, by in enumerate((step - 1, step + 1)):
        remote(
            bend_out.at[n], bend_in.at[slot, n], bend_send.at[n], bend_recv.at[slot, n], at(by, owner), valid(by)
        )

    for copy in core_scatter:
        copy.wait_recv()
    first, last = (
        pltpu.roll(core_parts[x, n] + core_in[0, n] + core_in[1, n] + core_in[2, n], HALO, 1) for n in (0, 1)
    )
    edge_out[0] = pack_low(last) * right_link
    edge_out[1] = pack_high(first)
    edges = [
        remote(edge_out.at[0], edge_in.at[0], edge_send.at[0], edge_recv.at[0], at(1, kern), valid(1)),
        remote(edge_out.at[1], edge_in.at[1], edge_send.at[1], edge_recv.at[1], at(-1, kern), valid(-1)),
    ]

    for copy in middle_scatter:
        copy.wait_recv()
    between = pltpu.roll(core_parts[x, 2] + core_in[0, 2] + core_in[1, 2] + core_in[2, 2], HALO, 1)
    lane_edge = low_lanes(QUARTER)
    whole[...] = lanes(jnp.where(lane_edge, first, between), jnp.where(lane_edge, between, last))
    takes = (x == 0) | (x == 3)
    back = jnp.where(x == 0, -GRID_W, GRID_W)
    lane_fold = low_lanes(32)
    for s in range(2):
        arrivals = (
            (valid(back), fold_out, fold_in.at[s], fold_send, fold_recv.at[s]),
            (valid(back + 1), bend_out.at[0], bend_in.at[s, 0], bend_send.at[0], bend_recv.at[s, 0]),
            (valid(back - 1), bend_out.at[1], bend_in.at[s, 1], bend_send.at[1], bend_recv.at[s, 1]),
        )
        for there, src, dst, send, recv in arrivals:
            copy = pltpu.make_async_remote_copy(
                src_ref=src, dst_ref=dst, send_sem=send, recv_sem=recv, device_id=far, device_id_type=MESH
            )
            clear_unless(takes & there, dst)
            pl.when(takes & there)(copy.wait_recv)
        block = pl.ds(32 * s, 32)
        from_left = jnp.where(lane_fold, unpack_low(bend_in[s, 1]), 0.0)
        from_right = jnp.where(lane_fold, 0.0, unpack_high(bend_in[s, 0])) * right_link
        whole[block, :] += fold_in[s] + lanes(from_left, from_right)

    for there, copy in zip((from_left_tile, from_right_tile), edges):
        pl.when(there)(copy.wait_recv)
    from_left = jnp.where(lane_edge, unpack_low(edge_in[0]), 0.0)
    from_right = jnp.where(lane_edge, 0.0, unpack_high(edge_in[1])) * right_link
    partial = whole[...] + lanes(from_left, from_right)
    swaps = []
    for h in range(2):
        mine[h] = partial[h * 32 : (h + 1) * 32]
        swaps.append(remote(mine.at[h], other.at[h], gfar_send.at[h], gfar_recv.at[h], far))
    finish_sends()
    finals = []
    stores = [store]
    for h in range(2):
        swaps[h].wait_recv()
        gathered[h] = mine[h] + other[h]
        place = out.at[1, 0, pl.ds(pl.multiple_of(QUARTER * x + 32 * h, 32), 32)]
        finals += [
            remote(gathered.at[h], place, all_send.at[h, d - 1], all_recv.at[h, d - 1], peers[d])
            for d in FARTHEST_FIRST
        ]
        stores.append(pltpu.make_async_copy(gathered.at[h], place, store_sem.at[1 + h]))
        stores[-1].start()
    for copy in finals:
        copy.wait_recv()
    finish_sends()
    for copy in stores:
        copy.wait()


def store_kernel(both, resist_out, grad_out, held, load_sem, store_sem):
    pieces = [(n, pl.ds(q * BLK, BLK)) for n in range(2) for q in range(2)]
    loads = [
        pltpu.make_async_copy(both.at[n, 0, block], held.at[n, 0, block], load_sem.at[i])
        for i, (n, block) in enumerate(pieces)
    ]
    for copy in loads:
        copy.start()
    stores = []
    for i, (n, block) in enumerate(pieces):
        loads[i].wait()
        into = (resist_out, grad_out)[n]
        stores.append(pltpu.make_async_copy(held.at[n, 0, block], into.at[0, block], store_sem.at[i]))
        stores[-1].start()
    for copy in stores:
        copy.wait()


def body(mask, kernels, weight, link, target):
    anywhere = pl.BlockSpec(memory_space=pl.ANY)
    dma = pltpu.SemaphoreType.DMA
    f32 = lambda *shape: pltpu.VMEM(shape, F32)
    buffers = [
        f32(1, CORE, CORE), f32(2, 3, BLK, BLK), pltpu.VMEM((1, CORE, CORE), jnp.int32),
        pltpu.VMEM((2, 2, 3, CORE, CORE), BF16),
        f32(2, EXTENT, EXTENT), f32(2, CORE, 3 * EXTENT), f32(2, EXTENT, 3 * EXTENT), f32(2, EXTENT, EXTENT),
        f32(2, 2, EXTENT, CORE), f32(2, EXTENT, EXTENT), f32(EXTENT, EXTENT), f32(1, CORE, CORE),
        f32(2, BLK, BLK), f32(2, BLK, BLK), f32(2, 2 * PART + 8, BLK), f32(2, 2 * PART + 8, BLK),
        f32(2, 2, PART // 2, BLK), f32(4, PART // 2, BLK), f32(4, 2, PART, EXTENT),
        f32(4, 8, BLK), f32(8, BLK), f32(8, BLK),
        f32(2, 4, EIGHTH, CORE), f32(2, 3, EIGHTH, CORE), f32(2, EIGHTH, CORE), f32(2, EIGHTH, CORE),
        f32(2, 4, EIGHTH, CORE),
        f32(4, 32, EXTENT), f32(3, 32, EXTENT), f32(4, 3, QUARTER, BLK), f32(3, 3, QUARTER, BLK),
        f32(32, CORE), f32(2, 32, CORE), f32(2, 16, BLK), f32(2, 2, 16, BLK),
        f32(2, 32, BLK), f32(2, 32, BLK), f32(QUARTER, CORE),
        f32(2, 32, CORE), f32(2, 32, CORE), f32(2, 32, CORE),
    ]
    sems = [pltpu.SMEM((3,), F32), pltpu.SMEM((1, 2), jnp.int32), dma((6,)), dma((3,))] + [dma((2,))] * 4 + [dma((4,))] * 2 + [dma((3,))] * 2
    sems += [dma((3,))] * 2 + [dma] * 2
    sems += [dma((2, 3))] * 2 + [dma((2,))] * 2 + [dma((2, 3))] * 2
    sems += [dma((3,))] * 6 + [dma, dma((2,)), dma((2,)), dma((2, 2))]
    sems += [dma((2,))] * 4 + [dma((2, 3))] * 2
    both = pl.pallas_call(
        body_kernel,
        out_shape=jax.ShapeDtypeStruct((2, 1, CORE, CORE), F32),
        in_specs=[anywhere] * 6,
        out_specs=anywhere,
        scratch_shapes=buffers + sems,
        compiler_params=pltpu.CompilerParams(
            collective_id=0, has_side_effects=True, vmem_limit_bytes=60 * 2**20
        ),
    )(mask, kernels, target, jnp.asarray(dft_tables()), weight, link)
    out = jax.ShapeDtypeStruct((1, CORE, CORE), F32)
    return pl.pallas_call(
        store_kernel,
        out_shape=(out, out),
        in_specs=[anywhere],
        out_specs=(anywhere, anywhere),
        scratch_shapes=[f32(2, 1, CORE, CORE), dma((4,)), dma((4,))],
        compiler_params=pltpu.CompilerParams(vmem_limit_bytes=60 * 2**20),
    )(both)


def solution(mesh):
    in_specs = (
        P("tile", None, None),
        P(None, "kern", None, None),
        P("kern"),
        P("tile", None),
        P("tile", None, None),
    )
    out_specs = (P("tile", None, None), P("tile", None, None))
    return jax.shard_map(body, mesh=mesh, in_specs=in_specs, out_specs=out_specs, check_vma=False)
```
